32 devices in a mesh: dp: 4 (over y, x), tp: 8 (over z, core).
Axes of the slice: x: 2, y: 2, z: 4, core: 2. Of those that a mesh axis runs over, the one named last changes fastest.
Arguments:
- inputs: bfloat16 [16, 1024, 1024], P('dp', 'tp'), may hold values from -6 to 6
- memory: bfloat16 [16, 512, 1024], P('dp', 'tp'), may hold values from -6 to 6
- segments: int32 [16, 1024], P('dp', 'tp'), may hold values from 0 to 2, as said below
- memory_segments: int32 [16, 512], P('dp', 'tp'), may hold values from 0 to 2, as said below
- gain_self: float32 [1024], replicated, may hold values from 0.5 to 1.5
- gain_cross: float32 [1024], replicated, may hold values from 0.5 to 1.5
- gain_ffn: float32 [1024], replicated, may hold values from 0.5 to 1.5
- relative_bias: float32 [32, 16], replicated, may hold values from -4 to 4
- self_query: bfloat16 [1024, 1024], replicated, may hold values from -0.1875 to 0.1875
- self_key: bfloat16 [1024, 512], replicated, may hold values from -0.1875 to 0.1875
- self_value: bfloat16 [1024, 512], replicated, may hold values from -0.1875 to 0.1875
- self_out: bfloat16 [1024, 1024], replicated, may hold values from -1.5 to 1.5
- cross_query: bfloat16 [1024, 1024], replicated, may hold values from -0.1875 to 0.1875
- cross_key: bfloat16 [1024, 512], replicated, may hold values from -0.1875 to 0.1875
- cross_value: bfloat16 [1024, 512], replicated, may hold values from -0.1875 to 0.1875
- cross_out: bfloat16 [1024, 1024], replicated, may hold values from -1.5 to 1.5
- ffn_gate: bfloat16 [1024, 2816], P(None, 'tp'), may hold values from -0.1875 to 0.1875
- ffn_up: bfloat16 [1024, 2816], P(None, 'tp'), may hold values from -0.1875 to 0.1875
- ffn_down: bfloat16 [2816, 1024], P('tp'), may hold values from -0.15625 to 0.15625
- cotangent: bfloat16 [16, 1024, 1024], P('dp', 'tp'), may hold values from -6 to 6
Outputs:
- output: bfloat16 [16, 1024, 1024], P('dp', 'tp')
- input_grad: float32 [16, 1024, 1024], P('dp', 'tp')
- memory_grad: float32 [16, 512, 1024], P('dp', 'tp')
- gain_self_grad: float32 [1024], P(('dp', 'tp'))
- gain_cross_grad: float32 [1024], P(('dp', 'tp'))
- gain_ffn_grad: float32 [1024], P(('dp', 'tp'))
- relative_grad: float32 [512], P(('dp', 'tp'))
- self_query_grad: float32 [1024, 1024], P(('dp', 'tp'))
- self_key_grad: float32 [1024, 512], P(('dp', 'tp'))
- self_value_grad: float32 [1024, 512], P(('dp', 'tp'))
- self_out_grad: float32 [1024, 1024], P(('dp', 'tp'))
- cross_query_grad: float32 [1024, 1024], P(('dp', 'tp'))
- cross_key_grad: float32 [1024, 512], P(('dp', 'tp'))
- cross_value_grad: float32 [1024, 512], P(('dp', 'tp'))
- cross_out_grad: float32 [1024, 1024], P(('dp', 'tp'))
- ffn_gate_grad: float32 [1024, 2816], P('dp', 'tp')
- ffn_up_grad: float32 [1024, 2816], P('dp', 'tp')
- ffn_down_grad: float32 [2816, 1024], P('tp', 'dp')
The draws below stay inside these ranges and needn't reach their ends.
Inputs may be any that keep to these rules, and one draw needn't show every extreme that they name: `segments`: along each row the ids never fall, and each of 0, 1 and 2 appears. `memory_segments`: along each row the ids never fall, and each of 0, 1 and 2 appears.
All inputs are finite; a program needn't handle non-finite values.
Results may differ from the reference program's by a relative error of at most 0.025.
Values may be sent and summed in bfloat16 or wider, within the bound.
A program may use at most 320 MiB of HBM per device.

```python
import math
from functools import partial
import jax
import jax.numpy as jnp
from jax import lax

D = 1024
FF = 2816
HEADS = 16
HEAD_DIM = 64
GROUPS = 8
BUCKETS = 32
MAX_DIST = 128
SEQ_DEV = 128
ENC = 512
ROW_LEN = 1024
ROWS = 16
N_TP = 8


def three_documents(key, length, device_span):
    first_key, last_key = jax.random.split(key)
    first_end = jax.random.randint(first_key, (ROWS, 1), 1, device_span)
    last_start = jax.random.randint(last_key, (ROWS, 1), length - device_span + 1, length)
    position_row = jnp.arange(length, dtype=jnp.int32)[None, :]
    return (position_row >= first_end).astype(jnp.int32) + (position_row >= last_start).astype(jnp.int32)


def draw_segments(key, part):
    key = jax.random.fold_in(key, 11)
    return three_documents(key, ROW_LEN, SEQ_DEV)


def draw_memory_segments(key, part):
    key = jax.random.fold_in(key, 23)
    return three_documents(key, ENC, ENC // N_TP)


def block_scale(rng, shape, cuts, low, high):
    loudness, own = 1.0, jax.random.fold_in(rng, 6)
    for dim, blocks in cuts:
        heights = jnp.exp(jax.random.uniform(jax.random.fold_in(own, dim), (blocks,), jnp.float32, low / len(cuts), high / len(cuts)))
        loudness = loudness * jnp.repeat(heights, shape[dim] // blocks).reshape([-1 if axis == dim else 1 for axis in range(len(shape))])
    return loudness


def gaussian(key, dims, spread, limit, pieces=(), kind=jnp.bfloat16):
    array = spread * jax.random.normal(key, dims, jnp.float32)
    if pieces:
        array = array * block_scale(key, dims, pieces, -0.22, 0.18)
    return jnp.clip(array, -limit, limit).astype(kind)


def setup_inputs(seed: int = 0) -> dict:
    streams_of = jax.random.split(jax.random.key(seed), 21)
    return {
        "inputs": gaussian(streams_of[0], (ROWS, ROW_LEN, D), 1.0, 6.0, ((0, 4), (1, 8))),
        "memory": gaussian(streams_of[1], (ROWS, ENC, D), 1.0, 6.0, ((0, 4), (1, 8))),
        "segments": draw_segments(jax.random.fold_in(streams_of[20], 71), 0),
        "memory_segments": draw_memory_segments(jax.random.fold_in(streams_of[20], 71), 0),
        "gain_self": jnp.clip(1.0 + 0.1 * jax.random.normal(streams_of[4], (D,), jnp.float32), 0.5, 1.5),
        "gain_cross": jnp.clip(1.0 + 0.1 * jax.random.normal(streams_of[5], (D,), jnp.float32), 0.5, 1.5),
        "gain_ffn": jnp.clip(1.0 + 0.1 * jax.random.normal(streams_of[6], (D,), jnp.float32), 0.5, 1.5),
        "relative_bias": gaussian(streams_of[7], (BUCKETS, HEADS), 1.0, 4.0, (), jnp.float32),
        "self_query": gaussian(streams_of[8], (D, HEADS * HEAD_DIM), D ** -0.5, 0.1875),
        "self_key": gaussian(streams_of[9], (D, GROUPS * HEAD_DIM), D ** -0.5, 0.1875),
        "self_value": gaussian(streams_of[10], (D, GROUPS * HEAD_DIM), D ** -0.5, 0.1875),
        "self_out": gaussian(streams_of[11], (HEADS * HEAD_DIM, D), 16 ** -0.5, 1.5),
        "cross_query": gaussian(streams_of[12], (D, HEADS * HEAD_DIM), D ** -0.5, 0.1875),
        "cross_key": gaussian(streams_of[13], (D, GROUPS * HEAD_DIM), D ** -0.5, 0.1875),
        "cross_value": gaussian(streams_of[14], (D, GROUPS * HEAD_DIM), D ** -0.5, 0.1875),
        "cross_out": gaussian(streams_of[15], (HEADS * HEAD_DIM, D), 16 ** -0.5, 1.5),
        "ffn_gate": gaussian(streams_of[16], (D, FF), D ** -0.5, 0.1875, ((1, 8),)),
        "ffn_up": gaussian(streams_of[17], (D, FF), D ** -0.5, 0.1875, ((1, 8),)),
        "ffn_down": gaussian(streams_of[18], (FF, D), (FF // 2) ** -0.5, 0.15625, ((0, 8),)),
        "cotangent": gaussian(streams_of[19], (ROWS, ROW_LEN, D), 1.0, 6.0, ((0, 4), (1, 8))),
    }


@jax.custom_vjp
def low(v):
    return lax.optimization_barrier(v.astype(jnp.bfloat16)).astype(jnp.float32)

@jax.custom_vjp
def low_back(v):
    return v

def low_keep(v):
    return (low(v), None)

def low_pass(kept, grad):
    return (grad,)

def back_keep(v):
    return (v, None)

def back_low(kept, grad):
    return (low(grad),)
low.defvjp(low_keep, low_pass)
low_back.defvjp(back_keep, back_low)
norm_epsilon = 1e-06
highest = lax.Precision.HIGHEST

def root_norm(operand, gain_vector):
    return operand * lax.rsqrt(lax.optimization_barrier(jnp.mean(operand * operand, axis=-1, keepdims=True)) + norm_epsilon) * gain_vector

def bucket_of(distance):
    exact = BUCKETS // 2
    bucket_count = jnp.zeros_like(distance)
    for step_index in range(1, exact):
        threshold = math.ceil(exact * (MAX_DIST / exact) ** (step_index / exact))
        bucket_count = bucket_count + (distance >= threshold).astype(jnp.int32)
    return jnp.where(distance < exact, distance, exact + bucket_count)

def dense(left, right):
    return jnp.dot(left, right, precision=highest)

def attend(queries, key_rows, value_rows, allowed, bias):
    length = queries.shape[0]
    span = key_rows.shape[0]
    grouped = queries.reshape(length, GROUPS, HEADS // GROUPS, HEAD_DIM)
    keyed = key_rows.reshape(span, GROUPS, HEAD_DIM)
    valued = value_rows.reshape(span, GROUPS, HEAD_DIM)
    scores = jnp.einsum('qgjd,kgd->gjqk', grouped, keyed, precision=highest) * HEAD_DIM ** (-0.5) + bias
    scores = low_back(scores)
    scores = jnp.where(allowed, scores, -1e+30)
    weights = jax.nn.softmax(scores, axis=-1)
    context = jnp.einsum('gjqk,kgd->qgjd', low(weights), valued, precision=highest)
    return context.reshape(length, HEADS * HEAD_DIM)

def one_row(params, row):
    gain_self, gain_cross, gain_ffn, relative_bias, self_query, self_key, self_value, self_out, cross_query, cross_key, cross_value, cross_out, ffn_gate, ffn_up, ffn_down = params
    stream, memory_row, segment_row, memory_segment_row = row
    length = stream.shape[0]
    position = jnp.arange(length, dtype=jnp.int32)
    distance = jnp.maximum(position[:, None] - position[None, :], 0)
    bias = jnp.take(relative_bias, bucket_of(distance), axis=0)
    bias = jnp.transpose(bias, (2, 0, 1)).reshape(GROUPS, HEADS // GROUPS, length, length)
    allowed_self = (segment_row[:, None] == segment_row[None, :]) & (position[:, None] >= position[None, :])
    held_self = low(root_norm(stream, gain_self))
    queries = low_back(low(dense(held_self, self_query)))
    key_rows = low_back(low(dense(held_self, self_key)))
    value_rows = low_back(low(dense(held_self, self_value)))
    self_context = low_back(low(attend(queries, key_rows, value_rows, allowed_self, bias)))
    stream_one = stream + low_back(dense(self_context, self_out))
    held_cross = low(root_norm(stream_one, gain_cross))
    cross_queries = low_back(low(dense(held_cross, cross_query)))
    memory_keys = low_back(low(dense(memory_row, cross_key)))
    memory_values = low_back(low(dense(memory_row, cross_value)))
    allowed_cross = segment_row[:, None] == memory_segment_row[None, :]
    cross_context = low_back(low(attend(cross_queries, memory_keys, memory_values, allowed_cross, 0.0)))
    stream_two = stream_one + low_back(dense(cross_context, cross_out))
    held_ffn = low(root_norm(stream_two, gain_ffn))
    gate = low_back(dense(held_ffn, ffn_gate))
    up_part = low_back(dense(held_ffn, ffn_up))
    hidden = low(jax.nn.gelu(gate, approximate=True) * up_part)
    return stream_two + low_back(dense(hidden, ffn_down))

def reference(inputs, memory, segments, memory_segments, gain_self, gain_cross, gain_ffn, relative_bias, self_query, self_key, self_value, self_out, cross_query, cross_key, cross_value, cross_out, ffn_gate, ffn_up, ffn_down, cotangent):
    params = tuple((weight.astype(jnp.float32) for weight in (gain_self, gain_cross, gain_ffn, relative_bias, self_query, self_key, self_value, self_out, cross_query, cross_key, cross_value, cross_out, ffn_gate, ffn_up, ffn_down)))

    def forward(stream, memory_rows, weights):
        row_step = jax.checkpoint(partial(one_row, weights))
        return lax.map(row_step, (stream, memory_rows, segments, memory_segments))
    result, pullback = jax.vjp(forward, inputs.astype(jnp.float32), memory.astype(jnp.float32), params)
    input_grad, memory_grad, weight_grads = pullback(cotangent.astype(jnp.float32))
    gain_self_grad, gain_cross_grad, gain_ffn_grad, relative_grad, self_query_grad, self_key_grad, self_value_grad, self_out_grad, cross_query_grad, cross_key_grad, cross_value_grad, cross_out_grad, ffn_gate_grad, ffn_up_grad, ffn_down_grad = weight_grads
    return (result.astype(jnp.bfloat16), input_grad, memory_grad, gain_self_grad, gain_cross_grad, gain_ffn_grad, relative_grad.reshape(-1), self_query_grad, self_key_grad, self_value_grad, self_out_grad, cross_query_grad, cross_key_grad, cross_value_grad, cross_out_grad, ffn_gate_grad, ffn_up_grad, ffn_down_grad)
```

```python
import functools
import math

import jax
import jax.numpy as jnp
from jax import lax
from jax.experimental import pallas as pl
from jax.experimental.pallas import tpu as pltpu
from jax.sharding import PartitionSpec as P

HEADS = 16
HEAD_DIM = 64
GROUPS = 8
BUCKETS = 32
MAX_DIST = 128
BLOCK = 128
PAIRS = GROUPS // 2
FAR = -1e30
SCALE = HEAD_DIM ** (-0.5)
MIB = 1 << 20

norm_epsilon = 1e-06
f32 = jnp.float32
bf16 = jnp.bfloat16


def nn(left, right):
    return lax.dot_general(left, right, (((1,), (0,)), ((), ())), preferred_element_type=f32)


def nt(left, right):
    return lax.dot_general(left, right, (((1,), (1,)), ((), ())), preferred_element_type=f32)


def tn(left, right):
    return lax.dot_general(left, right, (((0,), (0,)), ((), ())), preferred_element_type=f32)


def bits_of(count):
    return count.bit_length() - 1


def xor_static(value, flips, count):
    result = value
    for bit in range(bits_of(count)):
        if flips >> bit & 1:
            result = result + (1 << bit) * (1 - 2 * ((value // (1 << bit)) % 2))
    return result


def half_order(count, first_low):
    nb = bits_of(count)
    bits = list(range(nb)) if first_low else list(range(nb))[::-1]
    order = []
    for index in range(count):
        s = 0
        for place, bit in enumerate(bits):
            if index >> (nb - 1 - place) & 1:
                s |= 1 << bit
        order.append(s)
    return order, bits


def norm_scale(v):
    return lax.rsqrt(jnp.mean(v * v, axis=-1, keepdims=True) + norm_epsilon)


def norm_back(v, gain, dy):
    s = norm_scale(v)
    gained = dy * gain
    grad = s * gained - v * (s * s * s * jnp.mean(gained * v, axis=-1, keepdims=True))
    return grad, jnp.sum(dy * v * s, axis=0)


def bucket_of(distance):
    exact = BUCKETS // 2
    bucket_count = jnp.zeros_like(distance)
    for step_index in range(1, exact):
        threshold = math.ceil(exact * (MAX_DIST / exact) ** (step_index / exact))
        bucket_count = bucket_count + (distance >= threshold).astype(jnp.int32)
    return jnp.where(distance < exact, distance, exact + bucket_count)


def whole_vmem():
    return pl.BlockSpec(memory_space=pltpu.VMEM)


def whole_smem():
    return pl.BlockSpec(memory_space=pltpu.SMEM)


def any_space():
    return pl.BlockSpec(memory_space=pl.ANY)


def params(limit_mib, **more):
    return pltpu.CompilerParams(vmem_limit_bytes=limit_mib * MIB, **more)


class Places:
    def __init__(self, rows):
        self.tp = lax.axis_size("tp")
        self.dp = lax.axis_size("dp")
        self.rows = rows
        self.share = self.tp // rows
        self.z_count = self.tp // 2

    def row(self):
        return lax.axis_index("tp") // self.share

    def part(self):
        return lax.axis_index("tp") % self.share

    def row_perm(self, k):
        share = self.share
        return [(t, ((t // share) ^ k) * share + t % share) for t in range(self.tp)]

    def part_perm(self, shift):
        share = self.share
        return [
            (t // share * share + (t % share + shift) % share, t) for t in range(self.tp)
        ]

    def core_perm(self):
        return [(t, t ^ 1) for t in range(self.tp)]

    def z_perm(self, shift):
        z_count = self.z_count
        return [(t, (t // 2 + shift) % z_count * 2 + t % 2) for t in range(self.tp)]

    def dp_perm(self, flips):
        return [(d, d ^ flips) for d in range(self.dp)]


def exchange_rows(at, array):
    row = at.row()
    received = []
    for k in range(1, at.rows):
        chunk = lax.dynamic_index_in_dim(array, xor_static(row, k, at.rows), 0, keepdims=False)
        received.append(lax.ppermute(chunk, "tp", at.row_perm(k)))
    return received


def place_kernel(at, *refs):
    own, pieces, out, sems = refs[0], refs[1 : at.rows], refs[at.rows], refs[at.rows + 1]
    row = at.row()
    copies = [pltpu.make_async_copy(own.at[row], out.at[row], sems.at[0])]
    for k in range(1, at.rows):
        copies.append(
            pltpu.make_async_copy(
                pieces[k - 1], out.at[xor_static(row, k, at.rows)], sems.at[k]
            )
        )
    for copy in copies:
        copy.start()
    for copy in copies:
        copy.wait()


def place_rows(at, own, pieces):
    return pl.pallas_call(
        functools.partial(place_kernel, at),
        out_shape=jax.ShapeDtypeStruct(own.shape, own.dtype),
        in_specs=[any_space()] * at.rows,
        out_specs=any_space(),
        scratch_shapes=[pltpu.SemaphoreType.DMA((at.rows,))],
        name="place_rows",
    )(own, *pieces)


def place_wide_kernel(at, *refs):
    own, pieces, out = refs[0], refs[1 : at.rows], refs[at.rows]
    row = at.row()
    out[row] = own[row].astype(f32)
    for k in range(1, at.rows):
        out[xor_static(row, k, at.rows)] = pieces[k - 1][...].astype(f32)


def place_wide(at, own, pieces):
    return pl.pallas_call(
        functools.partial(place_wide_kernel, at),
        out_shape=jax.ShapeDtypeStruct(own.shape, f32),
        in_specs=[whole_vmem()] * at.rows,
        out_specs=whole_vmem(),
        compiler_params=params(24),
        name="place_wide",
    )(own, *pieces)


def exchange_segments(at, packed):
    row = at.row()
    pieces = [lax.dynamic_index_in_dim(packed, row, 0, keepdims=False)]
    pieces += exchange_rows(at, packed)
    blocks = jnp.stack(pieces)
    for bit in range(bits_of(at.rows)):
        grouped = blocks.reshape(-1, 2, 1 << bit, blocks.shape[-1])
        flipped = grouped[:, ::-1]
        blocks = jnp.where((row // (1 << bit)) % 2 == 1, flipped, grouped).reshape(blocks.shape)
    return [blocks] + [
        lax.ppermute(blocks, "tp", at.part_perm(s)) for s in range(1, at.share)
    ]


def near_kinds(share):
    kinds = [(s, 0) for s in range(share)]
    return kinds + [(s, 1) for s in range(share) if s > 0 or share == 1]


def kind_distance(at, kind):
    s, back = kind
    part = at.part()
    return part - (part + s) % at.share + at.share * back


def tile_distance(at, kind):
    key = lax.broadcasted_iota(jnp.int32, (BLOCK, BLOCK), 0)
    query = lax.broadcasted_iota(jnp.int32, (BLOCK, BLOCK), 1)
    return BLOCK * kind_distance(at, kind) + query - key


def bias_tiles_kernel(at, table, out):
    group = pl.program_id(0)
    for number, kind in enumerate(near_kinds(at.share)):
        distance = tile_distance(at, kind)
        bucket = bucket_of(jnp.maximum(distance, 0))
        for j in range(2):
            head = group * 2 + j
            last = table[(BUCKETS - 1) * HEADS + head]
            value = jnp.zeros((BLOCK, BLOCK), f32)
            for b in range(BUCKETS - 1):
                value = jnp.where(bucket == b, table[b * HEADS + head] - last, value)
            out[0, number, :, j * BLOCK : (j + 1) * BLOCK] = jnp.where(distance < 0, FAR, value)


def bias_tiles(at, table):
    kinds = len(near_kinds(at.share))
    return pl.pallas_call(
        functools.partial(bias_tiles_kernel, at),
        grid=(GROUPS,),
        out_shape=jax.ShapeDtypeStruct((GROUPS, kinds, BLOCK, 2 * BLOCK), f32),
        in_specs=[whole_smem()],
        out_specs=pl.BlockSpec((1, kinds, BLOCK, 2 * BLOCK), lambda g: (g, 0, 0, 0)),
        name="bias_tiles",
    )(table)


def query_features(seg_block, last_parts, group):
    shape = (HEAD_DIM, 2 * BLOCK)
    row = lax.broadcasted_iota(jnp.int32, shape, 0)
    seg = jnp.concatenate([seg_block, seg_block], axis=1)
    feature = jnp.where((row < 3) & (seg != row), FAR, 0.0)
    if last_parts is not None:
        lane = lax.broadcasted_iota(jnp.int32, shape, 1)
        for part in range(3):
            first = last_parts[part * HEADS + group * 2]
            second = last_parts[part * HEADS + group * 2 + 1]
            feature = jnp.where(row == 3 + part, jnp.where(lane < BLOCK, first, second), feature)
    return feature.astype(bf16)


def turned(block):
    return block.astype(f32).T.astype(block.dtype)


def stacked_heads(pair):
    t = turned(pair)
    return jnp.concatenate([t[:HEAD_DIM], t[HEAD_DIM:]], axis=1)


def unstacked_heads(wide):
    return jnp.concatenate([wide[:, :BLOCK], wide[:, BLOCK:]], axis=0).T


def with_other(half, other, odd):
    return jnp.concatenate([other, half] if odd else [half, other], axis=0)


def fold_rows(tile):
    return tile.reshape(tile.shape[0] // 8, 8, tile.shape[1])


class Keys:
    def __init__(self, share, blocks, causal):
        self.share, self.blocks, self.causal = share, blocks, causal
        self.count = share * blocks

    def blocks_for(self, i):
        return (i + 1 if self.causal else self.blocks) * self.share

    def near(self, i, index, kinds):
        if not self.causal:
            return None
        j, s = divmod(index, self.share)
        kind = (s, i - j)
        return kinds.index(kind) if kind in kinds else None


def load_keys(keys, k_refs, feat_refs, odd, kaug):
    lane = lax.broadcasted_iota(jnp.int32, (BLOCK, 2 * HEAD_DIM), 1)
    own = (lane >= HEAD_DIM) if odd else (lane < HEAD_DIM)
    for index in range(keys.count):
        j, s = divmod(index, keys.share)
        rows = pl.ds(j * BLOCK, BLOCK)
        kaug[pl.ds(index * BLOCK, BLOCK), :] = jnp.where(
            own, k_refs[s][rows, :].astype(f32), feat_refs[s][rows, :].astype(f32)
        ).astype(bf16)


def turn_keys(keys, refs, target):
    for index in range(keys.count):
        j, s = divmod(index, keys.share)
        target[:, pl.ds(index * BLOCK, BLOCK)] = turned(refs[s][pl.ds(j * BLOCK, BLOCK), :])


def forward_kernel(keys, kinds, *refs):
    refs = list(refs)
    take = lambda n: [refs.pop(0) for _ in range(n)]
    q_ref, seg_ref = take(2)
    k_refs, v_refs, feat_refs = take(keys.share), take(keys.share), take(keys.share)
    tiles, last_parts = take(2) if keys.causal else (None, None)
    ctx_ref, log_ref, kaug, vt, sbuf, pbuf = refs
    pair = pl.program_id(0)
    turn_keys(keys, v_refs, vt)
    for gi in range(2):
        load_keys(keys, k_refs, feat_refs, gi, kaug)
        for i in range(q_ref.shape[0] // BLOCK):
            tokens = pl.ds(i * BLOCK, BLOCK)
            lanes = pl.ds(gi * BLOCK, BLOCK)
            features = query_features(seg_ref[:, tokens], last_parts, pair * 2 + gi)
            right = with_other(stacked_heads(q_ref[tokens, lanes]), features, gi)
            count = keys.blocks_for(i)
            top = jnp.full((8, 2 * BLOCK), -jnp.inf, f32)
            for index in range(count):
                rows = pl.ds(index * BLOCK, BLOCK)
                scores = nn(kaug[rows, :], right)
                near = keys.near(i, index, kinds)
                if near is not None:
                    scores = scores + tiles[gi, near]
                sbuf[rows, :] = scores
                top = jnp.maximum(top, jnp.max(fold_rows(scores), axis=0))
            top = jnp.max(top, axis=0, keepdims=True)
            total = jnp.zeros((8, 2 * BLOCK), f32)
            for index in range(count):
                rows = pl.ds(index * BLOCK, BLOCK)
                exponent = jnp.exp(sbuf[rows, :] - top)
                total = total + jnp.sum(fold_rows(exponent), axis=0)
                pbuf[rows, :] = exponent.astype(bf16)
            total = jnp.sum(total, axis=0, keepdims=True)
            length = count * BLOCK
            context = nn(vt[pl.ds(gi * HEAD_DIM, HEAD_DIM), :length], pbuf[:length, :])
            ctx_ref[tokens, lanes] = unstacked_heads(context * (1.0 / total)).astype(bf16)
            log_ref[gi, pl.ds(i, 1), :] = top + jnp.log(total)


def backward_kernel(keys, kinds, *refs):
    refs = list(refs)
    take = lambda n: [refs.pop(0) for _ in range(n)]
    q_ref, seg_ref = take(2)
    k_refs, v_refs, feat_refs = take(keys.share), take(keys.share), take(keys.share)
    tiles, last_parts = take(2) if keys.causal else (None, None)
    log_ref, dctx_ref = take(2)
    (dq_ref,) = take(1)
    dkv_refs = take(keys.share)
    dtiles, dfar = take(2) if keys.causal else (None, None)
    kaug, kt, vn, sbuf, pbuf, gbuf, dk_acc, dv_acc = refs
    pair = pl.program_id(0)
    turn_keys(keys, k_refs, kt)
    for index in range(keys.count):
        j, s = divmod(index, keys.share)
        vn[pl.ds(index * BLOCK, BLOCK), :] = v_refs[s][pl.ds(j * BLOCK, BLOCK), :]
    for gi in range(2):
        load_keys(keys, k_refs, feat_refs, gi, kaug)
        group_rows = pl.ds(gi * HEAD_DIM, HEAD_DIM)
        seen = set()
        far = jnp.zeros((8, 2 * BLOCK), f32)
        n_blocks = q_ref.shape[0] // BLOCK
        for i in reversed(range(n_blocks)):
            tokens = pl.ds(i * BLOCK, BLOCK)
            lanes = pl.ds(gi * BLOCK, BLOCK)
            features = query_features(seg_ref[:, tokens], last_parts, pair * 2 + gi)
            queries = stacked_heads(q_ref[tokens, lanes])
            right = with_other(queries, features, gi)
            grads = stacked_heads(dctx_ref[tokens, lanes])
            grads_right = with_other(grads, jnp.zeros_like(grads), gi)
            logsum = log_ref[gi, pl.ds(i, 1), :]
            count = keys.blocks_for(i)
            middle = jnp.zeros((8, 2 * BLOCK), f32)
            for index in range(count):
                rows = pl.ds(index * BLOCK, BLOCK)
                scores = nn(kaug[rows, :], right)
                near = keys.near(i, index, kinds)
                if near is not None:
                    scores = scores + tiles[gi, near]
                probs = jnp.exp(scores - logsum)
                grad_probs = nn(vn[rows, :], grads_right)
                middle = middle + jnp.sum(fold_rows(probs * grad_probs), axis=0)
                sbuf[rows, :] = probs
                gbuf[rows, :] = grad_probs
                pbuf[rows, :] = probs.astype(bf16)
            middle = jnp.sum(middle, axis=0, keepdims=True)
            length = count * BLOCK
            grad_v = nt(grads, pbuf[:length, :])
            for index in range(count):
                rows = pl.ds(index * BLOCK, BLOCK)
                grad_scores = (sbuf[rows, :] * (gbuf[rows, :] - middle)).astype(bf16)
                pbuf[rows, :] = grad_scores
                if keys.causal:
                    wide = grad_scores.astype(f32)
                    near = keys.near(i, index, kinds)
                    if near is None:
                        far = far + jnp.sum(fold_rows(wide), axis=0)
                    elif near in seen:
                        dtiles[gi, near] = dtiles[gi, near] + wide
                    else:
                        dtiles[gi, near] = wide
                        seen.add(near)
            grad_k = nt(queries, pbuf[:length, :])
            grad_q = nn(kt[group_rows, :length], pbuf[:length, :])
            dq_ref[tokens, lanes] = unstacked_heads(grad_q * SCALE).astype(bf16)
            if i == n_blocks - 1:
                dk_acc[group_rows, :length] = grad_k
                dv_acc[group_rows, :length] = grad_v
            else:
                dk_acc[group_rows, :length] += grad_k
                dv_acc[group_rows, :length] += grad_v
        if keys.causal:
            dfar[gi] = far
    for index in range(keys.count):
        j, s = divmod(index, keys.share)
        columns = pl.ds(index * BLOCK, BLOCK)
        rows = pl.ds(j * BLOCK, BLOCK)
        dkv_refs[s][0, rows, :] = dk_acc[:, columns].T.astype(bf16)
        dkv_refs[s][1, rows, :] = dv_acc[:, columns].T.astype(bf16)


def attention_operands(at, queries, key_values, features, seg_row, tiles, last_parts):
    causal = tiles is not None
    tokens = queries.shape[0]
    span = key_values[0].shape[0]
    keys = Keys(at.share, span // BLOCK, causal)
    operands = [queries, seg_row, *key_values, *key_values, *features]
    specs = [
        pl.BlockSpec((tokens, 2 * BLOCK), lambda p: (0, p)),
        pl.BlockSpec(seg_row.shape, lambda p: (0, 0)),
    ]
    specs += [pl.BlockSpec((span, BLOCK), lambda p: (0, p))] * at.share
    specs += [pl.BlockSpec((span, BLOCK), lambda p: (0, PAIRS + p))] * at.share
    specs += [pl.BlockSpec((span, BLOCK), lambda p: (0, 0))] * at.share
    if causal:
        operands += [tiles, last_parts]
        specs += [
            pl.BlockSpec((2, *tiles.shape[1:]), lambda p: (p, 0, 0, 0)),
            whole_smem(),
        ]
    return keys, operands, specs


def attention_forward(at, queries, key_values, features, seg_row, tiles=None, last_parts=None):
    keys, operands, specs = attention_operands(
        at, queries, key_values, features, seg_row, tiles, last_parts
    )
    tokens = queries.shape[0]
    blocks = tokens // BLOCK
    length = keys.count * BLOCK
    work = sum(keys.blocks_for(i) for i in range(blocks)) * BLOCK * 2 * BLOCK * GROUPS
    return pl.pallas_call(
        functools.partial(forward_kernel, keys, near_kinds(at.share)),
        grid=(PAIRS,),
        out_shape=[
            jax.ShapeDtypeStruct((tokens, HEADS * HEAD_DIM), bf16),
            jax.ShapeDtypeStruct((GROUPS, blocks, 2 * BLOCK), f32),
        ],
        in_specs=specs,
        out_specs=[
            pl.BlockSpec((tokens, 2 * BLOCK), lambda p: (0, p)),
            pl.BlockSpec((2, blocks, 2 * BLOCK), lambda p: (p, 0, 0)),
        ],
        scratch_shapes=[
            pltpu.VMEM((length, 2 * HEAD_DIM), bf16),
            pltpu.VMEM((2 * HEAD_DIM, length), bf16),
            pltpu.VMEM((length, 2 * BLOCK), f32),
            pltpu.VMEM((length, 2 * BLOCK), bf16),
        ],
        compiler_params=params(32),
        cost_estimate=pl.CostEstimate(
            flops=work * 512, bytes_accessed=8 * MIB, transcendentals=work
        ),
        name="self_forward" if keys.causal else "cross_forward",
    )(*operands)


def attention_backward(
    at, queries, key_values, features, seg_row, logsum, grad_context, tiles=None, last_parts=None
):
    keys, operands, specs = attention_operands(
        at, queries, key_values, features, seg_row, tiles, last_parts
    )
    tokens = queries.shape[0]
    span = key_values[0].shape[0]
    blocks = tokens // BLOCK
    length = keys.count * BLOCK
    work = sum(keys.blocks_for(i) for i in range(blocks)) * BLOCK * 2 * BLOCK * GROUPS
    operands += [logsum, grad_context]
    specs += [
        pl.BlockSpec((2, blocks, 2 * BLOCK), lambda p: (p, 0, 0)),
        pl.BlockSpec((tokens, 2 * BLOCK), lambda p: (0, p)),
    ]
    out_shape = [jax.ShapeDtypeStruct((tokens, HEADS * HEAD_DIM), bf16)]
    out_specs = [pl.BlockSpec((tokens, 2 * BLOCK), lambda p: (0, p))]
    out_shape += [jax.ShapeDtypeStruct((2, span, GROUPS * HEAD_DIM), bf16)] * at.share
    out_specs += [pl.BlockSpec((2, span, BLOCK), lambda p: (0, 0, p))] * at.share
    if keys.causal:
        out_shape += [
            jax.ShapeDtypeStruct(tiles.shape, f32),
            jax.ShapeDtypeStruct((GROUPS, 8, 2 * BLOCK), f32),
        ]
        out_specs += [
            pl.BlockSpec((2, *tiles.shape[1:]), lambda p: (p, 0, 0, 0)),
            pl.BlockSpec((2, 8, 2 * BLOCK), lambda p: (p, 0, 0)),
        ]
    return pl.pallas_call(
        functools.partial(backward_kernel, keys, near_kinds(at.share)),
        grid=(PAIRS,),
        out_shape=out_shape,
        in_specs=specs,
        out_specs=out_specs,
        scratch_shapes=[
            pltpu.VMEM((length, 2 * HEAD_DIM), bf16),
            pltpu.VMEM((2 * HEAD_DIM, length), bf16),
            pltpu.VMEM((length, 2 * HEAD_DIM), bf16),
            pltpu.VMEM((length, 2 * BLOCK), f32),
            pltpu.VMEM((length, 2 * BLOCK), bf16),
            pltpu.VMEM((length, 2 * BLOCK), f32),
            pltpu.VMEM((2 * HEAD_DIM, length), f32),
            pltpu.VMEM((2 * HEAD_DIM, length), f32),
        ],
        compiler_params=params(40),
        cost_estimate=pl.CostEstimate(
            flops=work * 1024, bytes_accessed=16 * MIB, transcendentals=work
        ),
        name="self_backward" if keys.causal else "cross_backward",
    )(*operands)


def gelu_parts(v):
    slope = math.sqrt(2 / math.pi)
    square = v * v
    t = jnp.tanh(slope * v * (1.0 + 0.044715 * square))
    half = 0.5 * (1.0 + t)
    derivative = half + 0.5 * v * (1.0 - t * t) * slope * (1.0 + 3 * 0.044715 * square)
    return v * half, derivative


def ffn_kernel(at, *refs):
    n_pieces = at.z_count * at.dp
    held_refs, cot_refs = refs[0:2], refs[2:4]
    pieces = refs[4 : 4 + n_pieces]
    out_refs = refs[4 + n_pieces : 8 + n_pieces]
    grad_refs = refs[8 + n_pieces : 12 + n_pieces]
    weights, acts, held, cot, out_stage, back_stage, in_sems, w_sems, out_sems = refs[
        12 + n_pieces :
    ]
    d = lax.axis_index("dp")
    tokens = held_refs[0].shape[0]
    width = pieces[0].shape[2]
    rows = pieces[0].shape[1]

    def columns(s):
        return pl.ds(pl.multiple_of(xor_static(d, s, at.dp) * width, width), width)

    loads = []
    for which, (sources, target) in enumerate(((held_refs, held), (cot_refs, cot))):
        for half in range(2):
            for s in range(at.dp):
                loads.append(
                    pltpu.make_async_copy(
                        sources[half].at[:, columns(s)],
                        target.at[pl.ds(half * tokens, tokens), pl.ds(s * width, width)],
                        in_sems.at[(which * 2 + half) * at.dp + s],
                    )
                )
    for k in range(at.z_count):
        for s in range(at.dp):
            number = k * at.dp + s
            loads.append(
                pltpu.make_async_copy(
                    pieces[number],
                    weights.at[:, pl.ds(k * rows, rows), pl.ds(s * width, width)],
                    w_sems.at[number],
                )
            )
    for copy in loads:
        copy.start()
    for copy in loads:
        copy.wait()

    tile = 256

    def step(index, carry):
        here = pl.ds(pl.multiple_of(index * tile, tile), tile)
        held_tile, cot_tile = held[here, :], cot[here, :]
        gate = nt(held_tile, weights[0])
        up = nt(held_tile, weights[1])
        grad_hidden = nt(cot_tile, weights[2])
        active, slope = gelu_parts(gate)
        hidden = (active * up).astype(bf16)
        acts[2, here, :] = hidden
        out_stage[here, :] = nn(hidden, weights[2]).astype(bf16)
        grad_gate = (grad_hidden * up * slope).astype(bf16)
        grad_up = (grad_hidden * active).astype(bf16)
        acts[0, here, :] = grad_gate
        acts[1, here, :] = grad_up
        back_stage[here, :] = (nn(grad_gate, weights[0]) + nn(grad_up, weights[1])).astype(bf16)
        return carry

    lax.fori_loop(0, 2 * tokens // tile, step, 0)

    stores = []
    for which, stage in enumerate((out_stage, back_stage)):
        for half in range(2):
            for s in range(at.dp):
                stores.append(
                    pltpu.make_async_copy(
                        stage.at[pl.ds(half * tokens, tokens), pl.ds(s * width, width)],
                        out_refs[which * 2 + half].at[:, columns(s)],
                        out_sems.at[(which * 2 + half) * at.dp + s],
                    )
                )
    for copy in stores:
        copy.start()

    hidden_rows = rows * at.z_count
    half_rows = hidden_rows // 2
    for start in range(0, hidden_rows, BLOCK):
        size = min(BLOCK, hidden_rows - start)
        for m in range(3):
            right = cot if m == 2 else held
            grad = tn(acts[m, :, start : start + size], right[...]).astype(bf16)
            low = max(0, min(size, half_rows - start))
            for part, (first, last) in enumerate(((0, low), (low, size))):
                if first == last:
                    continue
                order, _ = half_order(at.dp, part == 0)
                target = start + first - part * half_rows
                for place, s in enumerate(order):
                    sent, slot = divmod(place, at.dp // 2)
                    grad_refs[part * 2 + sent][
                        slot, m, target : target + last - first, :
                    ] = grad[first:last, s * width : (s + 1) * width]
    for copy in stores:
        copy.wait()


def ffn(at, held_own, held_other, cot_own, cot_other, pieces):
    tokens, features = held_own.shape
    rows, width = pieces[0].shape[1:]
    hidden = rows * at.z_count
    grad_shape = jax.ShapeDtypeStruct((at.dp // 2, 3, hidden // 2, width), bf16)
    token_shape = jax.ShapeDtypeStruct((tokens, features), bf16)
    return pl.pallas_call(
        functools.partial(ffn_kernel, at),
        out_shape=[token_shape] * 4 + [grad_shape] * 4,
        in_specs=[any_space()] * (4 + len(pieces)),
        out_specs=[any_space()] * 4 + [whole_vmem()] * 4,
        scratch_shapes=[
            pltpu.VMEM((3, hidden, features), bf16),
            pltpu.VMEM((3, 2 * tokens, hidden), bf16),
            pltpu.VMEM((2 * tokens, features), bf16),
            pltpu.VMEM((2 * tokens, features), bf16),
            pltpu.VMEM((2 * tokens, features), bf16),
            pltpu.VMEM((2 * tokens, features), bf16),
            pltpu.SemaphoreType.DMA((4 * at.dp,)),
            pltpu.SemaphoreType.DMA((len(pieces),)),
            pltpu.SemaphoreType.DMA((4 * at.dp,)),
        ],
        compiler_params=params(58),
        cost_estimate=pl.CostEstimate(
            flops=18 * 2 * tokens * features * hidden,
            bytes_accessed=40 * MIB,
            transcendentals=2 * tokens * hidden,
        ),
        name="ffn",
    )(held_own, held_other, cot_own, cot_other, *pieces)


def weight_grad_kernel(at, widths, *refs):
    n = len(widths)
    lefts, rights, outs = refs[:n], refs[n : 2 * n], refs[2 * n :]
    d = lax.axis_index("dp")
    core = lax.axis_index("tp") % 2
    rows = lefts[0].shape[1] // at.dp
    quarter = sum(widths) // 4
    for sent in range(2):
        half = core if sent == 0 else 1 - core
        offset = 0
        for left, right, total in zip(lefts, rights, widths):
            width = total // 2
            block = right[:, pl.ds(pl.multiple_of(half * width, width), width)]
            for s in range(at.dp):
                chosen = pl.ds(pl.multiple_of(xor_static(d, s, at.dp) * rows, rows), rows)
                grad = tn(left[:, chosen], block).astype(bf16)
                done = 0
                while done < width:
                    part, inside = divmod(offset + done, quarter)
                    take = min(width - done, quarter - inside)
                    order, _ = half_order(at.dp, part == 0)
                    outs[part * 2 + sent][order.index(s), :, inside : inside + take] = grad[
                        :, done : done + take
                    ]
                    done += take
            offset += width


def weight_grads(at, pairs):
    lefts = [left for left, _ in pairs]
    rights = [right for _, right in pairs]
    widths = [right.shape[1] for right in rights]
    features = lefts[0].shape[1]
    quarter = sum(widths) // 4
    shape = jax.ShapeDtypeStruct((at.dp, features // at.dp, quarter), bf16)
    low_keep, low_send, high_keep, high_send = pl.pallas_call(
        functools.partial(weight_grad_kernel, at, widths),
        out_shape=[shape] * 4,
        in_specs=[whole_vmem()] * (2 * len(pairs)),
        out_specs=[whole_vmem()] * 4,
        compiler_params=params(48),
        cost_estimate=pl.CostEstimate(
            flops=2 * lefts[0].shape[0] * features * sum(widths),
            bytes_accessed=16 * MIB,
            transcendentals=0,
        ),
        name="weight_grads",
    )(*lefts, *rights)
    core = lax.axis_index("tp") % 2
    mine = []
    for part, (keep, send) in enumerate(((low_keep, low_send), (high_keep, high_send))):
        received = lax.ppermute(send, "tp", at.core_perm())
        half = at.dp // 2
        keep, send = added(keep[:half], received[:half]), added(keep[half:], received[half:])
        total = reduce_dp(at, keep, send, part == 0)
        chunks = total.reshape(at.z_count, -1, quarter)
        z = lax.axis_index("tp") // 2
        result = lax.dynamic_index_in_dim(chunks, z, 0, keepdims=False).astype(f32)
        for k in range(1, at.z_count):
            chunk = lax.dynamic_index_in_dim(chunks, (z + k) % at.z_count, 0, keepdims=False)
            result = result + lax.ppermute(chunk, "tp", at.z_perm(k)).astype(f32)
        mine.append(result)
    joined = jnp.concatenate(mine, axis=1).astype(bf16)
    joined = joined.reshape(2, -1, joined.shape[-1])
    own = lax.dynamic_index_in_dim(joined, core, 0, keepdims=False)
    other = lax.ppermute(
        lax.dynamic_index_in_dim(joined, 1 - core, 0, keepdims=False), "tp", at.core_perm()
    )
    first = jnp.where(core == 0, own, other).astype(f32)
    second = jnp.where(core == 0, other, own).astype(f32)
    results, offset = [], 0
    for total in widths:
        inside = slice(offset, offset + total // 2)
        results.append(jnp.concatenate([first[:, inside], second[:, inside]], axis=1))
        offset += total // 2
    return results


def added(left, right):
    return (left.astype(f32) + right.astype(f32)).astype(bf16)


def reduce_dp(at, keep, send, first_low):
    _, bits = half_order(at.dp, first_low)
    for place, bit in enumerate(bits):
        received = lax.ppermute(send, "dp", at.dp_perm(1 << bit))
        half = keep.shape[0] // 2
        if half:
            keep, send = added(keep[:half], received[:half]), added(keep[half:], received[half:])
        else:
            return added(keep[0], received[0])


def reduce_ffn_grads(at, grads):
    low_keep, low_send, high_keep, high_send = grads
    low = reduce_dp(at, low_keep, low_send, True)
    high = reduce_dp(at, high_keep, high_send, False)
    half = at.z_count // 2
    chunks = []
    for total in (low, high):
        split = total.reshape(3, half, -1, total.shape[-1])
        chunks += [split[:, k] for k in range(half)]
    result = chunks[0].astype(f32)
    for k in range(1, at.z_count):
        result = result + lax.ppermute(chunks[k], "tp", at.z_perm(-k)).astype(f32)
    return result


def reduce_small(at, vector):
    core = lax.axis_index("tp") % 2
    z = lax.axis_index("tp") // 2
    d = lax.axis_index("dp")
    pick = lambda array, index: lax.dynamic_index_in_dim(array, index, 0, keepdims=False)
    array = vector.reshape(at.dp * at.z_count, 2, -1).transpose(1, 0, 2)
    array = pick(array, core) + lax.ppermute(pick(array, 1 - core), "tp", at.core_perm())
    array = array.reshape(at.dp, at.z_count, -1)
    total = pick(array, d)
    for s in range(1, at.dp):
        total = total + lax.ppermute(
            pick(array, xor_static(d, s, at.dp)), "dp", at.dp_perm(s)
        )
    result = pick(total, z)
    for k in range(1, at.z_count):
        result = result + lax.ppermute(
            pick(total, (z + k) % at.z_count), "tp", at.z_perm(k)
        )
    return result


def gather_ffn(at, own, after):
    pieces = []
    current = own
    for k in range(at.z_count):
        if k == 1:
            current, _ = lax.optimization_barrier((current, after))
        if k:
            current = lax.ppermute(current, "tp", at.z_perm(1))
        held = {0: current}
        _, bits = half_order(at.dp, k % 2 == 0)
        for bit in bits:
            for s in list(held):
                held[s | 1 << bit] = lax.ppermute(held[s], "dp", at.dp_perm(1 << bit))
        pieces += [held[s] for s in range(at.dp)]
    return pieces, current


def relative_grad(at, dtiles, dfar):
    kinds = near_kinds(at.share)
    onehots = []
    for kind in kinds:
        distance = tile_distance(at, kind)
        bucket = jnp.where(distance < 0, -1, bucket_of(jnp.maximum(distance, 0)))
        onehots.append(bucket[:, :, None] == jnp.arange(BUCKETS, dtype=jnp.int32))
    onehot = jnp.stack(onehots).astype(f32)
    tiles = dtiles.reshape(GROUPS, len(kinds), BLOCK, 2, BLOCK)
    near = jnp.einsum(
        "nkqb,gnkjq->bgj", onehot, tiles, precision=lax.Precision.HIGHEST
    ).reshape(BUCKETS, HEADS)
    far = jnp.sum(dfar.reshape(GROUPS, 8, 2, BLOCK), axis=(1, 3)).reshape(HEADS)
    return near.at[BUCKETS - 1].add(far)


def on_device(
    inputs,
    memory,
    segments,
    memory_segments,
    gain_self,
    gain_cross,
    gain_ffn,
    relative_bias,
    self_query,
    self_key,
    self_value,
    self_out,
    cross_query,
    cross_key,
    cross_value,
    cross_out,
    ffn_gate,
    ffn_up,
    ffn_down,
    cotangent,
):
    rows, seq, features = inputs.shape
    mem_seq = memory.shape[1]
    at = Places(rows)
    tokens = rows * seq
    mem_tokens = rows * mem_seq
    key_width = GROUPS * HEAD_DIM
    width = features // at.dp
    d = lax.axis_index("dp")

    x_pieces = exchange_rows(at, inputs)
    seg_parts = exchange_segments(at, jnp.concatenate([segments, memory_segments], axis=1))
    own_columns = lambda w: lax.dynamic_slice_in_dim(w, d * width, width, 1)
    own_rows = lambda w: lax.dynamic_slice_in_dim(w, d * width, width, 0).T
    own_piece = jnp.stack([own_rows(ffn_gate), own_rows(ffn_up), own_columns(ffn_down)])
    tiles = bias_tiles(at, relative_bias.reshape(-1))

    x_pieces, memory_in = lax.optimization_barrier((x_pieces, memory))
    mem_pieces = exchange_rows(at, memory_in)
    ffn_pieces, ring_end = gather_ffn(at, own_piece, mem_pieces)
    cot_in, _ = lax.optimization_barrier((cotangent, ring_end))
    cot_pieces = exchange_rows(at, cot_in)

    x = place_rows(at, inputs, x_pieces).reshape(tokens, features).astype(f32)

    last = relative_bias[BUCKETS - 1]
    high = lax.reduce_precision(last, 8, 7)
    mid = lax.reduce_precision(last - high, 8, 7)
    low = lax.reduce_precision(last - high - mid, 8, 7)
    last_parts = jnp.concatenate([high, mid, low])

    def key_features(seg):
        lane = jnp.arange(2 * HEAD_DIM, dtype=jnp.int32) % HEAD_DIM
        column = seg.reshape(-1, 1)
        return jnp.where(
            lane < 3, (column == lane).astype(f32), ((lane >= 3) & (lane < 6)).astype(f32)
        ).astype(bf16)

    self_features = [key_features(seg[:, :seq]) for seg in seg_parts]
    mem_features = [key_features(seg[:, seq:]) for seg in seg_parts]
    seg_row = seg_parts[0][:, :seq].reshape(1, tokens)

    held_self = (x * norm_scale(x) * gain_self).astype(bf16)
    queries = (nn(held_self, self_query) * SCALE).astype(bf16)
    kv = jnp.concatenate([nn(held_self, self_key), nn(held_self, self_value)], axis=1).astype(bf16)
    kvs = [kv] + [lax.ppermute(kv, "tp", at.part_perm(s)) for s in range(1, at.share)]
    mem = place_rows(at, memory, mem_pieces).reshape(mem_tokens, features)
    mem_kv = jnp.concatenate([nn(mem, cross_key), nn(mem, cross_value)], axis=1).astype(bf16)
    mem_kvs = [mem_kv] + [
        lax.ppermute(mem_kv, "tp", at.part_perm(s)) for s in range(1, at.share)
    ]
    self_context, self_log = attention_forward(
        at, queries, kvs, self_features, seg_row, tiles, last_parts
    )
    stream_one = x + nn(self_context, self_out)

    held_cross = (stream_one * norm_scale(stream_one) * gain_cross).astype(bf16)
    cross_queries = (nn(held_cross, cross_query) * SCALE).astype(bf16)
    cross_context, cross_log = attention_forward(
        at, cross_queries, mem_kvs, mem_features, seg_row
    )
    stream_two = stream_one + nn(cross_context, cross_out)

    held_ffn = (stream_two * norm_scale(stream_two) * gain_ffn).astype(bf16)
    cot = place_rows(at, cotangent, cot_pieces).reshape(tokens, features)
    cot_other = lax.ppermute(cot, "tp", at.core_perm())
    held_other = lax.ppermute(held_ffn, "tp", at.core_perm())
    out_own, out_other, back_own, back_other, *ffn_grads = ffn(
        at, held_ffn, held_other, cot, cot_other, ffn_pieces
    )
    back_received = lax.ppermute(back_other, "tp", at.core_perm())
    out_received = lax.ppermute(out_other, "tp", at.core_perm())
    ffn_sum = reduce_ffn_grads(at, ffn_grads)

    grad_held = back_own.astype(f32) + back_received.astype(f32)
    grad_stream, gain_ffn_part = norm_back(stream_two, gain_ffn, grad_held)
    grad_two = cot.astype(f32) + grad_stream
    output = (stream_two + (out_own.astype(f32) + out_received.astype(f32))).astype(bf16)
    output = output.reshape(rows, seq, features)
    output_pieces = exchange_rows(at, output)

    cross_branch = grad_two.astype(bf16)
    grad_cross_context = nt(cross_branch, cross_out).astype(bf16)
    grad_cross_queries, *grad_mem_kvs = attention_backward(
        at, cross_queries, mem_kvs, mem_features, seg_row, cross_log, grad_cross_context
    )

    def gathered_grads(parts):
        total = parts[0].astype(f32)
        for s in range(1, at.share):
            total = total + lax.ppermute(
                parts[s], "tp", at.part_perm(at.share - s)
            ).astype(f32)
        return total[0].astype(bf16), total[1].astype(bf16)

    grad_mem_keys, grad_mem_values = gathered_grads(grad_mem_kvs)
    grad_stream, gain_cross_part = norm_back(
        stream_one, gain_cross, nt(grad_cross_queries, cross_query)
    )
    grad_one = grad_two + grad_stream
    self_branch = grad_one.astype(bf16)
    grad_self_context = nt(self_branch, self_out).astype(bf16)
    memory_grad = (nt(grad_mem_keys, cross_key) + nt(grad_mem_values, cross_value)).astype(bf16)
    memory_grad = memory_grad.reshape(rows, mem_seq, features)
    memory_pieces = exchange_rows(at, memory_grad)
    cross_out_grad, cross_query_grad, self_out_grad, cross_key_grad, cross_value_grad = (
        weight_grads(
            at,
            [
                (cross_context, cross_branch),
                (held_cross, grad_cross_queries),
                (self_context, self_branch),
                (mem, grad_mem_keys),
                (mem, grad_mem_values),
            ],
        )
    )

    grad_queries, *more = attention_backward(
        at, queries, kvs, self_features, seg_row, self_log, grad_self_context, tiles, last_parts
    )
    grad_keys, grad_values = gathered_grads(more[: at.share])
    self_query_grad, self_key_grad, self_value_grad = weight_grads(
        at, [(held_self, grad_queries), (held_self, grad_keys), (held_self, grad_values)]
    )
    grad_stream, gain_self_part = norm_back(
        x,
        gain_self,
        nt(grad_queries, self_query) + nt(grad_keys, self_key) + nt(grad_values, self_value),
    )
    input_grad = (grad_one + grad_stream).astype(bf16).reshape(rows, seq, features)
    input_pieces = exchange_rows(at, input_grad)
    relative_part = relative_grad(at, more[at.share], more[at.share + 1])

    shards = at.dp * at.tp
    small = jnp.concatenate(
        [
            part.reshape(shards, -1)
            for part in (gain_self_part, gain_cross_part, gain_ffn_part, relative_part)
        ],
        axis=1,
    )
    small = reduce_small(at, small)
    g = features // shards
    return (
        place_rows(at, output, output_pieces),
        place_wide(at, input_grad, input_pieces),
        place_wide(at, memory_grad, memory_pieces),
        small[:g],
        small[g : 2 * g],
        small[2 * g : 3 * g],
        small[3 * g :],
        self_query_grad,
        self_key_grad,
        self_value_grad,
        self_out_grad,
        cross_query_grad,
        cross_key_grad,
        cross_value_grad,
        cross_out_grad,
        ffn_sum[0].T,
        ffn_sum[1].T,
        ffn_sum[2],
    )


def solution(mesh):
    placed = (
        P("dp", "tp", None),
        P("dp", "tp", None),
        P("dp", "tp"),
        P("dp", "tp"),
        P(),
        P(),
        P(),
        P(),
        P(),
        P(),
        P(),
        P(),
        P(),
        P(),
        P(),
        P(),
        P(None, "tp"),
        P(None, "tp"),
        P("tp", None),
        P("dp", "tp", None),
    )
    return jax.shard_map(
        on_device,
        mesh=mesh,
        in_specs=placed,
        out_specs=(
            P("dp", "tp", None),
            P("dp", "tp", None),
            P("dp", "tp", None),
            P(("dp", "tp")),
            P(("dp", "tp")),
            P(("dp", "tp")),
            P(("dp", "tp")),
            P(("dp", "tp"), None),
            P(("dp", "tp"), None),
            P(("dp", "tp"), None),
            P(("dp", "tp"), None),
            P(("dp", "tp"), None),
            P(("dp", "tp"), None),
            P(("dp", "tp"), None),
            P(("dp", "tp"), None),
            P("dp", "tp"),
            P("dp", "tp"),
            P("tp", "dp"),
        ),
        check_vma=False,
    )
```

```python
import functools
import math

import jax
import jax.numpy as jnp
from jax import lax
from jax.experimental import pallas as pl
from jax.experimental.pallas import tpu as pltpu
from jax.sharding import PartitionSpec as P

HEADS = 16
HEAD_DIM = 64
GROUPS = 8
BUCKETS = 32
MAX_DIST = 128
BLOCK = 128
PAIRS = GROUPS // 2
FAR = -1e30
SCALE = HEAD_DIM ** (-0.5)
MIB = 1 << 20

norm_epsilon = 1e-06
f32 = jnp.float32
bf16 = jnp.bfloat16


def nn(left, right):
    return lax.dot_general(left, right, (((1,), (0,)), ((), ())), preferred_element_type=f32)


def nt(left, right):
    return lax.dot_general(left, right, (((1,), (1,)), ((), ())), preferred_element_type=f32)


def tn(left, right):
    return lax.dot_general(left, right, (((0,), (0,)), ((), ())), preferred_element_type=f32)


def bits_of(count):
    return count.bit_length() - 1


def xor_static(value, flips, count):
    result = value
    for bit in range(bits_of(count)):
        if flips >> bit & 1:
            result = result + (1 << bit) * (1 - 2 * ((value // (1 << bit)) % 2))
    return result


def half_order(count, first_low):
    nb = bits_of(count)
    bits = list(range(nb)) if first_low else list(range(nb))[::-1]
    order = []
    for index in range(count):
        s = 0
        for place, bit in enumerate(bits):
            if index >> (nb - 1 - place) & 1:
                s |= 1 << bit
        order.append(s)
    return order, bits


def norm_scale(v):
    return lax.rsqrt(jnp.mean(v * v, axis=-1, keepdims=True) + norm_epsilon)


def norm_back(v, gain, dy):
    s = norm_scale(v)
    gained = dy * gain
    grad = s * gained - v * (s * s * s * jnp.mean(gained * v, axis=-1, keepdims=True))
    return grad, jnp.sum(dy * v * s, axis=0, keepdims=True)


def bucket_of(distance):
    exact = BUCKETS // 2
    bucket_count = jnp.zeros_like(distance)
    for step_index in range(1, exact):
        threshold = math.ceil(exact * (MAX_DIST / exact) ** (step_index / exact))
        bucket_count = bucket_count + (distance >= threshold).astype(jnp.int32)
    return jnp.where(distance < exact, distance, exact + bucket_count)


def whole_vmem():
    return pl.BlockSpec(memory_space=pltpu.VMEM)


def whole_smem():
    return pl.BlockSpec(memory_space=pltpu.SMEM)


def any_space():
    return pl.BlockSpec(memory_space=pl.ANY)


def params(limit_mib, **more):
    return pltpu.CompilerParams(vmem_limit_bytes=limit_mib * MIB, **more)


class Places:
    def __init__(self, rows):
        self.tp = lax.axis_size("tp")
        self.dp = lax.axis_size("dp")
        self.rows = rows
        self.share = self.tp // rows
        self.z_count = self.tp // 2

    def row(self):
        return lax.axis_index("tp") // self.share

    def part(self):
        return lax.axis_index("tp") % self.share

    def row_perm(self, k):
        share = self.share
        return [(t, ((t // share) ^ k) * share + t % share) for t in range(self.tp)]

    def part_perm(self, shift):
        share = self.share
        return [
            (t // share * share + (t % share + shift) % share, t) for t in range(self.tp)
        ]

    def core_perm(self):
        return [(t, t ^ 1) for t in range(self.tp)]

    def z_perm(self, shift):
        z_count = self.z_count
        return [(t, (t // 2 + shift) % z_count * 2 + t % 2) for t in range(self.tp)]

    def dp_perm(self, flips):
        return [(d, d ^ flips) for d in range(self.dp)]


def exchange_rows(at, array):
    row = at.row()
    received = []
    for k in range(1, at.rows):
        chunk = lax.dynamic_index_in_dim(array, xor_static(row, k, at.rows), 0, keepdims=False)
        received.append(lax.ppermute(chunk, "tp", at.row_perm(k)))
    return received


def place_kernel(at, *refs):
    own, pieces, out = refs[0], refs[1 : at.rows], refs[at.rows]
    row = at.row()
    out[row] = own[row]
    for k in range(1, at.rows):
        out[xor_static(row, k, at.rows)] = pieces[k - 1][...]


def place_rows(at, own, pieces):
    return pl.pallas_call(
        functools.partial(place_kernel, at),
        out_shape=jax.ShapeDtypeStruct(own.shape, own.dtype),
        in_specs=[whole_vmem()] * at.rows,
        out_specs=whole_vmem(),
        compiler_params=params(16),
        name="place_rows",
    )(own, *pieces)


def place_wide_kernel(at, *refs):
    own, pieces, out = refs[0], refs[1 : at.rows], refs[at.rows]
    row = at.row()
    out[row] = own[row].astype(f32)
    for k in range(1, at.rows):
        out[xor_static(row, k, at.rows)] = pieces[k - 1][...].astype(f32)


def place_wide(at, own, pieces):
    return pl.pallas_call(
        functools.partial(place_wide_kernel, at),
        out_shape=jax.ShapeDtypeStruct(own.shape, f32),
        in_specs=[whole_vmem()] * at.rows,
        out_specs=whole_vmem(),
        compiler_params=params(24),
        name="place_wide",
    )(own, *pieces)


def exchange_segments(at, packed):
    row = at.row()
    pieces = [lax.dynamic_index_in_dim(packed, row, 0, keepdims=False)]
    pieces += exchange_rows(at, packed)
    blocks = jnp.stack(pieces)
    for bit in range(bits_of(at.rows)):
        grouped = blocks.reshape(-1, 2, 1 << bit, blocks.shape[-1])
        flipped = grouped[:, ::-1]
        blocks = jnp.where((row // (1 << bit)) % 2 == 1, flipped, grouped).reshape(blocks.shape)
    return [blocks] + [
        lax.ppermute(blocks, "tp", at.part_perm(s)) for s in range(1, at.share)
    ]


def near_kinds(share):
    kinds = [(s, 0) for s in range(share)]
    return kinds + [(s, 1) for s in range(share) if s > 0 or share == 1]


def kind_distance(at, kind):
    s, back = kind
    part = at.part()
    return part - (part + s) % at.share + at.share * back


def tile_distance(at, kind):
    key = lax.broadcasted_iota(jnp.int32, (BLOCK, BLOCK), 0)
    query = lax.broadcasted_iota(jnp.int32, (BLOCK, BLOCK), 1)
    return BLOCK * kind_distance(at, kind) + query - key


def bias_tiles_kernel(at, table, out):
    group = pl.program_id(0)
    for number, kind in enumerate(near_kinds(at.share)):
        distance = tile_distance(at, kind)
        bucket = bucket_of(jnp.maximum(distance, 0))
        for j in range(2):
            head = group * 2 + j
            last = table[(BUCKETS - 1) * HEADS + head]
            value = jnp.zeros((BLOCK, BLOCK), f32)
            for b in range(BUCKETS - 1):
                value = jnp.where(bucket == b, table[b * HEADS + head] - last, value)
            out[0, number, :, j * BLOCK : (j + 1) * BLOCK] = jnp.where(distance < 0, FAR, value)


def bias_tiles(at, table):
    kinds = len(near_kinds(at.share))
    return pl.pallas_call(
        functools.partial(bias_tiles_kernel, at),
        grid=(GROUPS,),
        out_shape=jax.ShapeDtypeStruct((GROUPS, kinds, BLOCK, 2 * BLOCK), f32),
        in_specs=[whole_smem()],
        out_specs=pl.BlockSpec((1, kinds, BLOCK, 2 * BLOCK), lambda g: (g, 0, 0, 0)),
        name="bias_tiles",
    )(table)


def query_features(seg_block, last_parts, group):
    shape = (HEAD_DIM, 2 * BLOCK)
    row = lax.broadcasted_iota(jnp.int32, shape, 0)
    seg = jnp.concatenate([seg_block, seg_block], axis=1)
    feature = jnp.where((row < 3) & (seg != row), FAR, 0.0)
    if last_parts is not None:
        lane = lax.broadcasted_iota(jnp.int32, shape, 1)
        for part in range(3):
            first = last_parts[part * HEADS + group * 2]
            second = last_parts[part * HEADS + group * 2 + 1]
            feature = jnp.where(row == 3 + part, jnp.where(lane < BLOCK, first, second), feature)
    return feature.astype(bf16)


def turned(block):
    return block.astype(f32).T.astype(block.dtype)


def stacked_heads(pair):
    t = turned(pair)
    return jnp.concatenate([t[:HEAD_DIM], t[HEAD_DIM:]], axis=1)


def unstacked_heads(wide):
    return jnp.concatenate([wide[:, :BLOCK], wide[:, BLOCK:]], axis=0).T


def with_other(half, other, odd):
    return jnp.concatenate([other, half] if odd else [half, other], axis=0)


def fold_rows(tile):
    return tile.reshape(tile.shape[0] // 8, 8, tile.shape[1])


class Keys:
    def __init__(self, share, blocks, causal):
        self.share, self.blocks, self.causal = share, blocks, causal
        self.count = share * blocks

    def blocks_for(self, i):
        return (i + 1 if self.causal else self.blocks) * self.share

    def near(self, i, index, kinds):
        if not self.causal:
            return None
        j, s = divmod(index, self.share)
        kind = (s, i - j)
        return kinds.index(kind) if kind in kinds else None


def load_keys(keys, k_refs, feat_refs, odd, kaug):
    lane = lax.broadcasted_iota(jnp.int32, (BLOCK, 2 * HEAD_DIM), 1)
    own = (lane >= HEAD_DIM) if odd else (lane < HEAD_DIM)
    for index in range(keys.count):
        j, s = divmod(index, keys.share)
        rows = pl.ds(j * BLOCK, BLOCK)
        kaug[pl.ds(index * BLOCK, BLOCK), :] = jnp.where(
            own, k_refs[s][rows, :].astype(f32), feat_refs[s][rows, :].astype(f32)
        ).astype(bf16)


def turn_keys(keys, refs, target):
    for index in range(keys.count):
        j, s = divmod(index, keys.share)
        target[:, pl.ds(index * BLOCK, BLOCK)] = turned(refs[s][pl.ds(j * BLOCK, BLOCK), :])


def forward_kernel(keys, kinds, *refs):
    refs = list(refs)
    take = lambda n: [refs.pop(0) for _ in range(n)]
    q_ref, seg_ref = take(2)
    k_refs, v_refs, feat_refs = take(keys.share), take(keys.share), take(keys.share)
    tiles, last_parts = take(2) if keys.causal else (None, None)
    ctx_ref, log_ref, kaug, vt, sbuf, pbuf = refs
    pair = pl.program_id(0)
    turn_keys(keys, v_refs, vt)
    for gi in range(2):
        load_keys(keys, k_refs, feat_refs, gi, kaug)
        for i in range(q_ref.shape[0] // BLOCK):
            tokens = pl.ds(i * BLOCK, BLOCK)
            lanes = pl.ds(gi * BLOCK, BLOCK)
            features = query_features(seg_ref[:, tokens], last_parts, pair * 2 + gi)
            right = with_other(stacked_heads(q_ref[tokens, lanes]), features, gi)
            count = keys.blocks_for(i)
            top = jnp.full((8, 2 * BLOCK), -jnp.inf, f32)
            for index in range(count):
                rows = pl.ds(index * BLOCK, BLOCK)
                scores = nn(kaug[rows, :], right)
                near = keys.near(i, index, kinds)
                if near is not None:
                    scores = scores + tiles[gi, near]
                sbuf[rows, :] = scores
                top = jnp.maximum(top, jnp.max(fold_rows(scores), axis=0))
            top = jnp.max(top, axis=0, keepdims=True)
            total = jnp.zeros((8, 2 * BLOCK), f32)
            for index in range(count):
                rows = pl.ds(index * BLOCK, BLOCK)
                exponent = jnp.exp(sbuf[rows, :] - top)
                total = total + jnp.sum(fold_rows(exponent), axis=0)
                pbuf[rows, :] = exponent.astype(bf16)
            total = jnp.sum(total, axis=0, keepdims=True)
            length = count * BLOCK
            context = nn(vt[pl.ds(gi * HEAD_DIM, HEAD_DIM), :length], pbuf[:length, :])
            ctx_ref[tokens, lanes] = unstacked_heads(context * (1.0 / total)).astype(bf16)
            log_ref[gi, pl.ds(i, 1), :] = top + jnp.log(total)


def diagonal_sums(tile):
    row = lax.broadcasted_iota(jnp.int32, (BLOCK, BLOCK), 0)
    lane = lax.broadcasted_iota(jnp.int32, (BLOCK, BLOCK), 1)
    turn = (row + lane == BLOCK - 1).astype(f32).astype(bf16)
    high = tile.astype(bf16)
    rest = tile - high.astype(f32)
    mid = rest.astype(bf16)
    low = (rest - mid.astype(f32)).astype(bf16)
    turned_rows = nn(turn, high) + nn(turn, mid) + nn(turn, low)
    sums = []
    for j in range(2):
        part = turned_rows[:, j * BLOCK : (j + 1) * BLOCK]
        wide = jnp.concatenate([part, jnp.zeros_like(part)], axis=1)
        rolled = pltpu.roll(wide, 0, 1, stride=1, stride_axis=0)
        sums.append(jnp.sum(rolled, axis=0, keepdims=True))
    return jnp.concatenate(sums, axis=0)


def backward_kernel(keys, kinds, *refs):
    refs = list(refs)
    take = lambda n: [refs.pop(0) for _ in range(n)]
    q_ref, seg_ref = take(2)
    k_refs, v_refs, feat_refs = take(keys.share), take(keys.share), take(keys.share)
    tiles, last_parts = take(2) if keys.causal else (None, None)
    log_ref, dctx_ref = take(2)
    (dq_ref,) = take(1)
    dkv_refs = take(keys.share)
    diagonals, dfar = take(2) if keys.causal else (None, None)
    kaug, kt, vn, sbuf, pbuf, gbuf, dk_acc, dv_acc, dtiles = refs
    pair = pl.program_id(0)
    turn_keys(keys, k_refs, kt)
    for index in range(keys.count):
        j, s = divmod(index, keys.share)
        vn[pl.ds(index * BLOCK, BLOCK), :] = v_refs[s][pl.ds(j * BLOCK, BLOCK), :]
    for gi in range(2):
        load_keys(keys, k_refs, feat_refs, gi, kaug)
        group_rows = pl.ds(gi * HEAD_DIM, HEAD_DIM)
        seen = set()
        far = jnp.zeros((8, 2 * BLOCK), f32)
        n_blocks = q_ref.shape[0] // BLOCK
        for i in reversed(range(n_blocks)):
            tokens = pl.ds(i * BLOCK, BLOCK)
            lanes = pl.ds(gi * BLOCK, BLOCK)
            features = query_features(seg_ref[:, tokens], last_parts, pair * 2 + gi)
            queries = stacked_heads(q_ref[tokens, lanes])
            right = with_other(queries, features, gi)
            grads = stacked_heads(dctx_ref[tokens, lanes])
            grads_right = with_other(grads, jnp.zeros_like(grads), gi)
            logsum = log_ref[gi, pl.ds(i, 1), :]
            count = keys.blocks_for(i)
            middle = jnp.zeros((8, 2 * BLOCK), f32)
            for index in range(count):
                rows = pl.ds(index * BLOCK, BLOCK)
                scores = nn(kaug[rows, :], right)
                near = keys.near(i, index, kinds)
                if near is not None:
                    scores = scores + tiles[gi, near]
                probs = jnp.exp(scores - logsum)
                grad_probs = nn(vn[rows, :], grads_right)
                middle = middle + jnp.sum(fold_rows(probs * grad_probs), axis=0)
                sbuf[rows, :] = probs
                gbuf[rows, :] = grad_probs
                pbuf[rows, :] = probs.astype(bf16)
            middle = jnp.sum(middle, axis=0, keepdims=True)
            length = count * BLOCK
            grad_v = nt(grads, pbuf[:length, :])
            for index in range(count):
                rows = pl.ds(index * BLOCK, BLOCK)
                grad_scores = (sbuf[rows, :] * (gbuf[rows, :] - middle)).astype(bf16)
                pbuf[rows, :] = grad_scores
                if keys.causal:
                    wide = grad_scores.astype(f32)
                    near = keys.near(i, index, kinds)
                    if near is None:
                        far = far + jnp.sum(fold_rows(wide), axis=0)
                    elif near in seen:
                        dtiles[near] = dtiles[near] + wide
                    else:
                        dtiles[near] = wide
                        seen.add(near)
            grad_k = nt(queries, pbuf[:length, :])
            grad_q = nn(kt[group_rows, :length], pbuf[:length, :])
            dq_ref[tokens, lanes] = unstacked_heads(grad_q * SCALE).astype(bf16)
            if i == n_blocks - 1:
                dk_acc[group_rows, :length] = grad_k
                dv_acc[group_rows, :length] = grad_v
            else:
                dk_acc[group_rows, :length] += grad_k
                dv_acc[group_rows, :length] += grad_v
        if keys.causal:
            dfar[gi] = far
            for near in range(len(kinds)):
                diagonals[gi, 2 * near : 2 * near + 2, :] = diagonal_sums(dtiles[near])
    for index in range(keys.count):
        j, s = divmod(index, keys.share)
        columns = pl.ds(index * BLOCK, BLOCK)
        rows = pl.ds(j * BLOCK, BLOCK)
        dkv_refs[s][0, rows, :] = dk_acc[:, columns].T.astype(bf16)
        dkv_refs[s][1, rows, :] = dv_acc[:, columns].T.astype(bf16)


def attention_operands(at, queries, key_values, features, seg_row, tiles, last_parts):
    causal = tiles is not None
    tokens = queries.shape[0]
    span = key_values[0].shape[0]
    keys = Keys(at.share, span // BLOCK, causal)
    operands = [queries, seg_row, *key_values, *key_values, *features]
    specs = [
        pl.BlockSpec((tokens, 2 * BLOCK), lambda p: (0, p)),
        pl.BlockSpec(seg_row.shape, lambda p: (0, 0)),
    ]
    specs += [pl.BlockSpec((span, BLOCK), lambda p: (0, p))] * at.share
    specs += [pl.BlockSpec((span, BLOCK), lambda p: (0, PAIRS + p))] * at.share
    specs += [pl.BlockSpec((span, BLOCK), lambda p: (0, 0))] * at.share
    if causal:
        operands += [tiles, last_parts]
        specs += [
            pl.BlockSpec((2, *tiles.shape[1:]), lambda p: (p, 0, 0, 0)),
            whole_smem(),
        ]
    return keys, operands, specs


def attention_forward(at, queries, key_values, features, seg_row, tiles=None, last_parts=None):
    keys, operands, specs = attention_operands(
        at, queries, key_values, features, seg_row, tiles, last_parts
    )
    tokens = queries.shape[0]
    blocks = tokens // BLOCK
    length = keys.count * BLOCK
    work = sum(keys.blocks_for(i) for i in range(blocks)) * BLOCK * 2 * BLOCK * GROUPS
    return pl.pallas_call(
        functools.partial(forward_kernel, keys, near_kinds(at.share)),
        grid=(PAIRS,),
        out_shape=[
            jax.ShapeDtypeStruct((tokens, HEADS * HEAD_DIM), bf16),
            jax.ShapeDtypeStruct((GROUPS, blocks, 2 * BLOCK), f32),
        ],
        in_specs=specs,
        out_specs=[
            pl.BlockSpec((tokens, 2 * BLOCK), lambda p: (0, p)),
            pl.BlockSpec((2, blocks, 2 * BLOCK), lambda p: (p, 0, 0)),
        ],
        scratch_shapes=[
            pltpu.VMEM((length, 2 * HEAD_DIM), bf16),
            pltpu.VMEM((2 * HEAD_DIM, length), bf16),
            pltpu.VMEM((length, 2 * BLOCK), f32),
            pltpu.VMEM((length, 2 * BLOCK), bf16),
        ],
        compiler_params=params(32),
        cost_estimate=pl.CostEstimate(
            flops=work * 512, bytes_accessed=8 * MIB, transcendentals=work
        ),
        name="self_forward" if keys.causal else "cross_forward",
    )(*operands)


def attention_backward(
    at, queries, key_values, features, seg_row, logsum, grad_context, tiles=None, last_parts=None
):
    keys, operands, specs = attention_operands(
        at, queries, key_values, features, seg_row, tiles, last_parts
    )
    tokens = queries.shape[0]
    span = key_values[0].shape[0]
    blocks = tokens // BLOCK
    length = keys.count * BLOCK
    work = sum(keys.blocks_for(i) for i in range(blocks)) * BLOCK * 2 * BLOCK * GROUPS
    operands += [logsum, grad_context]
    specs += [
        pl.BlockSpec((2, blocks, 2 * BLOCK), lambda p: (p, 0, 0)),
        pl.BlockSpec((tokens, 2 * BLOCK), lambda p: (0, p)),
    ]
    out_shape = [jax.ShapeDtypeStruct((tokens, HEADS * HEAD_DIM), bf16)]
    out_specs = [pl.BlockSpec((tokens, 2 * BLOCK), lambda p: (0, p))]
    out_shape += [jax.ShapeDtypeStruct((2, span, GROUPS * HEAD_DIM), bf16)] * at.share
    out_specs += [pl.BlockSpec((2, span, BLOCK), lambda p: (0, 0, p))] * at.share
    if keys.causal:
        out_shape += [
            jax.ShapeDtypeStruct((GROUPS, 2 * tiles.shape[1], 2 * BLOCK), f32),
            jax.ShapeDtypeStruct((GROUPS, 8, 2 * BLOCK), f32),
        ]
        out_specs += [
            pl.BlockSpec((2, 2 * tiles.shape[1], 2 * BLOCK), lambda p: (p, 0, 0)),
            pl.BlockSpec((2, 8, 2 * BLOCK), lambda p: (p, 0, 0)),
        ]
    return pl.pallas_call(
        functools.partial(backward_kernel, keys, near_kinds(at.share)),
        grid=(PAIRS,),
        out_shape=out_shape,
        in_specs=specs,
        out_specs=out_specs,
        scratch_shapes=[
            pltpu.VMEM((length, 2 * HEAD_DIM), bf16),
            pltpu.VMEM((2 * HEAD_DIM, length), bf16),
            pltpu.VMEM((length, 2 * HEAD_DIM), bf16),
            pltpu.VMEM((length, 2 * BLOCK), f32),
            pltpu.VMEM((length, 2 * BLOCK), bf16),
            pltpu.VMEM((length, 2 * BLOCK), f32),
            pltpu.VMEM((2 * HEAD_DIM, length), f32),
            pltpu.VMEM((2 * HEAD_DIM, length), f32),
            pltpu.VMEM((len(near_kinds(at.share)), BLOCK, 2 * BLOCK), f32),
        ],
        compiler_params=params(40),
        cost_estimate=pl.CostEstimate(
            flops=work * 1024, bytes_accessed=16 * MIB, transcendentals=work
        ),
        name="self_backward" if keys.causal else "cross_backward",
    )(*operands)


def gelu_parts(v):
    slope = math.sqrt(2 / math.pi)
    square = v * v
    t = jnp.tanh(slope * v * (1.0 + 0.044715 * square))
    half = 0.5 * (1.0 + t)
    derivative = half + 0.5 * v * (1.0 - t * t) * slope * (1.0 + 3 * 0.044715 * square)
    return v * half, derivative


def ffn_kernel(at, *refs):
    n_pieces = at.z_count * at.dp
    held_refs, cot_refs = refs[0:2], refs[2:4]
    pieces = refs[4 : 4 + n_pieces]
    out_refs = refs[4 + n_pieces : 8 + n_pieces]
    grad_ref = refs[8 + n_pieces]
    weights, acts, held, cot, out_stage, back_stage, in_sems, w_sems, out_sems = refs[
        9 + n_pieces :
    ]
    d = lax.axis_index("dp")
    z = lax.axis_index("tp") // 2
    tokens = held_refs[0].shape[0]
    width = pieces[0].shape[2]
    rows = pieces[0].shape[1]

    def columns(s):
        return pl.ds(pl.multiple_of(xor_static(d, s, at.dp) * width, width), width)

    loads = []
    for which, (sources, target) in enumerate(((held_refs, held), (cot_refs, cot))):
        for half in range(2):
            for s in range(at.dp):
                loads.append(
                    pltpu.make_async_copy(
                        sources[half].at[:, columns(s)],
                        target.at[pl.ds(half * tokens, tokens), pl.ds(s * width, width)],
                        in_sems.at[(which * 2 + half) * at.dp + s],
                    )
                )
    for k in range(at.z_count):
        for s in range(at.dp):
            number = k * at.dp + s
            loads.append(
                pltpu.make_async_copy(
                    pieces[number],
                    weights.at[
                        :,
                        pl.ds(pl.multiple_of((z + at.z_count - k) % at.z_count * rows, rows), rows),
                        pl.ds(s * width, width),
                    ],
                    w_sems.at[number],
                )
            )
    for copy in loads:
        copy.start()
    for copy in loads:
        copy.wait()

    tile = 256

    def step(index, carry):
        here = pl.ds(pl.multiple_of(index * tile, tile), tile)
        held_tile, cot_tile = held[here, :], cot[here, :]
        gate = nt(held_tile, weights[0])
        up = nt(held_tile, weights[1])
        grad_hidden = nt(cot_tile, weights[2])
        active, slope = gelu_parts(gate)
        hidden = (active * up).astype(bf16)
        acts[2, here, :] = hidden
        out_stage[here, :] = nn(hidden, weights[2]).astype(bf16)
        grad_gate = (grad_hidden * up * slope).astype(bf16)
        grad_up = (grad_hidden * active).astype(bf16)
        acts[0, here, :] = grad_gate
        acts[1, here, :] = grad_up
        back_stage[here, :] = (nn(grad_gate, weights[0]) + nn(grad_up, weights[1])).astype(bf16)
        return carry

    lax.fori_loop(0, 2 * tokens // tile, step, 0)

    stores = []
    for which, stage in enumerate((out_stage, back_stage)):
        for half in range(2):
            for s in range(at.dp):
                stores.append(
                    pltpu.make_async_copy(
                        stage.at[pl.ds(half * tokens, tokens), pl.ds(s * width, width)],
                        out_refs[which * 2 + half].at[:, columns(s)],
                        out_sems.at[(which * 2 + half) * at.dp + s],
                    )
                )
    for copy in stores:
        copy.start()

    hidden_rows = rows * at.z_count
    for start in range(0, hidden_rows, BLOCK):
        size = min(BLOCK, hidden_rows - start)
        for m in range(3):
            right = cot if m == 2 else held
            grad = tn(acts[m, :, start : start + size], right[...]).astype(bf16)
            first = start
            while first < start + size:
                chunk, inside = divmod(first, rows)
                last = min(start + size, (chunk + 1) * rows)
                for s in range(at.dp):
                    grad_ref[
                        xor_static(d, s, at.dp), chunk, m, inside : inside + last - first, :
                    ] = grad[first - start : last - start, s * width : (s + 1) * width]
                first = last
    for copy in stores:
        copy.wait()


def ffn(at, held_own, held_other, cot_own, cot_other, pieces):
    tokens, features = held_own.shape
    rows, width = pieces[0].shape[1:]
    hidden = rows * at.z_count
    grad_shape = jax.ShapeDtypeStruct((at.dp, at.z_count, 3, rows, width), bf16)
    token_shape = jax.ShapeDtypeStruct((tokens, features), bf16)
    return pl.pallas_call(
        functools.partial(ffn_kernel, at),
        out_shape=[token_shape] * 4 + [grad_shape],
        in_specs=[any_space()] * (4 + len(pieces)),
        out_specs=[any_space()] * 4 + [whole_vmem()],
        scratch_shapes=[
            pltpu.VMEM((3, hidden, features), bf16),
            pltpu.VMEM((3, 2 * tokens, hidden), bf16),
            pltpu.VMEM((2 * tokens, features), bf16),
            pltpu.VMEM((2 * tokens, features), bf16),
            pltpu.VMEM((2 * tokens, features), bf16),
            pltpu.VMEM((2 * tokens, features), bf16),
            pltpu.SemaphoreType.DMA((4 * at.dp,)),
            pltpu.SemaphoreType.DMA((len(pieces),)),
            pltpu.SemaphoreType.DMA((4 * at.dp,)),
        ],
        compiler_params=params(58),
        cost_estimate=pl.CostEstimate(
            flops=18 * 2 * tokens * features * hidden,
            bytes_accessed=40 * MIB,
            transcendentals=2 * tokens * hidden,
        ),
        name="ffn",
    )(held_own, held_other, cot_own, cot_other, *pieces)


def weight_grad_kernel(at, widths, *refs):
    n = len(widths)
    lefts, rights, outs = refs[:n], refs[n : 2 * n], refs[2 * n :]
    d = lax.axis_index("dp")
    core = lax.axis_index("tp") % 2
    rows = lefts[0].shape[1] // at.dp
    quarter = sum(widths) // 4
    for sent in range(2):
        half = core if sent == 0 else 1 - core
        offset = 0
        for left, right, total in zip(lefts, rights, widths):
            width = total // 2
            block = right[:, pl.ds(pl.multiple_of(half * width, width), width)]
            for s in range(at.dp):
                chosen = pl.ds(pl.multiple_of(xor_static(d, s, at.dp) * rows, rows), rows)
                grad = tn(left[:, chosen], block).astype(bf16)
                done = 0
                while done < width:
                    part, inside = divmod(offset + done, quarter)
                    take = min(width - done, quarter - inside)
                    order, _ = half_order(at.dp, part == 0)
                    outs[part * 2 + sent][order.index(s), :, inside : inside + take] = grad[
                        :, done : done + take
                    ]
                    done += take
            offset += width


def weight_products(at, pairs):
    lefts = [left for left, _ in pairs]
    rights = [right for _, right in pairs]
    widths = [right.shape[1] for right in rights]
    features = lefts[0].shape[1]
    quarter = sum(widths) // 4
    shape = jax.ShapeDtypeStruct((at.dp, features // at.dp, quarter), bf16)
    return pl.pallas_call(
        functools.partial(weight_grad_kernel, at, widths),
        out_shape=[shape] * 4,
        in_specs=[whole_vmem()] * (2 * len(pairs)),
        out_specs=[whole_vmem()] * 4,
        compiler_params=params(48),
        cost_estimate=pl.CostEstimate(
            flops=2 * lefts[0].shape[0] * features * sum(widths),
            bytes_accessed=16 * MIB,
            transcendentals=0,
        ),
        name="weight_grads",
    )(*lefts, *rights)


def reduce_ffn_grads(at, total):
    groups = [[z * 2 + core for z in range(at.z_count)] for core in range(2)]
    return lax.psum_scatter(
        total, "tp", scatter_dimension=0, tiled=True, axis_index_groups=groups
    )[0].astype(f32)


def remote(source, target, sems, number, axis, index):
    send, receive = sems
    return pltpu.make_async_remote_copy(
        src_ref=source,
        dst_ref=target,
        send_sem=send.at[number],
        recv_sem=receive.at[number],
        device_id={axis: index},
        device_id_type=pl.DeviceIdType.MESH,
    )


def tp_at(at, z):
    return z * 2 + lax.axis_index("tp") % 2


def other_core():
    t = lax.axis_index("tp")
    return t + 1 - 2 * (t % 2)


class Reduction:
    def __init__(self, at, first_low, buffers):
        self.at = at
        self.first, self.halves, self.z_in, self.done, self.last_in, *self.sems = buffers
        _, self.bits = half_order(at.dp, first_low)
        self.z = lax.axis_index("tp") // 2
        self.core = lax.axis_index("tp") % 2
        self.rows = self.first.shape[1] // at.z_count
        self.copies = {}

    @staticmethod
    def scratch(at, rows, columns):
        n = at.dp // 2
        messages = 1 + bits_of(at.dp) + at.z_count
        return [
            pltpu.VMEM((at.dp, rows, columns), bf16),
            pltpu.VMEM((max(2 * n - 1, 1), rows, columns), bf16),
            pltpu.VMEM((at.z_count - 1, rows // at.z_count, columns), bf16),
            pltpu.VMEM((rows // at.z_count, columns), f32),
            pltpu.VMEM((rows // at.z_count // 2, columns), f32),
            pltpu.SemaphoreType.DMA((messages,)),
            pltpu.SemaphoreType.DMA((messages,)),
        ]

    BUFFERS = 7

    def start(self, key, copy):
        self.copies[key] = copy
        copy.start()

    def start_core(self, source):
        self.start("core", remote(source, self.first, self.sems, 0, "tp", other_core()))

    def end_core(self, keep):
        self.copies["core"].wait()
        for s in range(self.at.dp):
            self.first[s] = self.first[s] + keep[s]

    def half_at(self, place):
        n = self.at.dp >> (place + 1)
        return n, self.at.dp - 2 * n

    def start_half(self, place):
        n, offset = self.half_at(place)
        d = lax.axis_index("dp")
        self.start(
            ("half", place),
            remote(
                self.first.at[pl.ds(n, n)],
                self.halves.at[pl.ds(offset, n)],
                self.sems,
                1 + place,
                "dp",
                xor_static(d, 1 << self.bits[place], self.at.dp),
            ),
        )

    def end_half(self, place):
        self.copies["half", place].wait()
        n, offset = self.half_at(place)
        for s in range(n):
            self.first[s] = self.first[s] + self.halves[offset + s]

    def start_z(self):
        base = 1 + len(self.bits)
        for k in range(1, self.at.z_count):
            z = (self.z + k) % self.at.z_count
            rows = pl.ds(pl.multiple_of(z * self.rows, self.rows), self.rows)
            self.start(
                ("z", k),
                remote(
                    self.first.at[0, rows, :],
                    self.z_in.at[k - 1],
                    self.sems,
                    base + k - 1,
                    "tp",
                    tp_at(self.at, z),
                ),
            )

    def end_z(self):
        rows = pl.ds(pl.multiple_of(self.z * self.rows, self.rows), self.rows)
        total = self.first[0, rows, :].astype(f32)
        for k in range(1, self.at.z_count):
            self.copies["z", k].wait()
            total = total + self.z_in[k - 1].astype(f32)
        self.done[...] = total

    def part(self, core):
        rows = self.rows // 2
        return pl.ds(pl.multiple_of(core * rows, rows), rows)

    def start_last(self):
        number = len(self.bits) + self.at.z_count
        self.start(
            "last",
            remote(
                self.done.at[self.part(1 - self.core), :],
                self.last_in,
                self.sems,
                number,
                "tp",
                other_core(),
            ),
        )

    def end_last(self, out, columns):
        out[0, :, columns] = self.done[self.part(self.core), :]
        self.copies["last"].wait()
        out[1, :, columns] = self.last_in[...]


def greet(at):
    barrier = pltpu.get_barrier_semaphore()
    t, d = lax.axis_index("tp"), lax.axis_index("dp")
    if at.share == 2:
        others = [other_core()]
        others += [tp_at(at, (t // 2 + k) % at.z_count) for k in range(1, at.z_count)]
    else:
        others = [(t + k) % at.tp for k in range(1, at.tp)]
    targets = [{"tp": other} for other in others]
    targets += [{"dp": xor_static(d, 1 << bit, at.dp)} for bit in range(bits_of(at.dp))]
    for target in targets:
        pl.semaphore_signal(
            barrier, inc=1, device_id=target, device_id_type=pl.DeviceIdType.MESH
        )
    pl.semaphore_wait(barrier, len(targets))


def tail_kernel(at, *refs):
    refs = list(refs)
    take = lambda n: [refs.pop(0) for _ in range(n)]
    held, dq, own_kv = take(3)
    other_kv = take(at.share - 1)
    x_ref, grad_ref, gain, wq, wk, wv = take(6)
    keep_low, keep_high, send_low, send_high, small_in = take(5)
    input_out, small_out, middle_out, last_out = take(4)
    middle = [
        Reduction(at, True, take(Reduction.BUFFERS)),
        Reduction(at, False, take(Reduction.BUFFERS)),
    ]
    last = [
        Reduction(at, True, take(Reduction.BUFFERS)),
        Reduction(at, False, take(Reduction.BUFFERS)),
    ]
    product_keep, product_send, kv_in, kv_sum, grad_rows, row_in, small, small_ins = take(8)
    kv_sems, row_sems, small_sems = take(2), take(2), take(2)
    d = lax.axis_index("dp")
    t = lax.axis_index("tp")
    z, core = t // 2, t % 2
    row, part = at.row(), at.part()
    features = held.shape[1]
    rows = features // at.dp
    bits = list(range(bits_of(at.dp)))

    greet(at)
    kv_copies = []
    for s in range(1, at.share):
        kv_copies.append(
            remote(
                other_kv[s - 1],
                kv_in.at[s - 1],
                kv_sems,
                s - 1,
                "tp",
                row * at.share + (part + s) % at.share,
            )
        )
    for copy in kv_copies:
        copy.start()
    middle[0].start_core(send_low)
    middle[1].start_core(send_high)

    def products(number, right, offset):
        width = right.shape[1] // 2
        order, _ = half_order(at.dp, number == 0)
        for sent, target in enumerate((product_keep, product_send)):
            half = core if sent == 0 else 1 - core
            block = right[:, pl.ds(pl.multiple_of(half * width, width), width)]
            for place, s in enumerate(order):
                chosen = pl.ds(pl.multiple_of(xor_static(d, s, at.dp) * rows, rows), rows)
                target[number, place, :, offset : offset + width] = tn(
                    held[:, chosen], block
                ).astype(bf16)

    products(0, dq, 0)
    last[0].start_core(product_send.at[0])
    for copy in kv_copies:
        copy.wait()
    for which in range(2):
        total = own_kv[which].astype(f32)
        for s in range(1, at.share):
            total = total + kv_in[s - 1, which].astype(f32)
        kv_sum[which] = total.astype(bf16)
    for which in range(2):
        products(1, kv_sum.at[which], which * (own_kv.shape[2] // 2))
    last[1].start_core(product_send.at[1])
    for number, keep in enumerate((keep_low, keep_high)):
        middle[number].end_core(keep)
        middle[number].start_half(0)

    seq = input_out.shape[1]
    row_copies = {}
    gain_sum = jnp.zeros((1, features), f32)
    gain_row = gain[...]
    for i in range(at.rows):
        here = pl.ds(i * seq, seq)
        dy = nt(dq[here, :], wq[...]) + nt(kv_sum[0, here, :], wk[...]) + nt(
            kv_sum[1, here, :], wv[...]
        )
        grad, gain_part = norm_back(x_ref[here, :].astype(f32), gain_row, dy)
        gain_sum = gain_sum + gain_part
        grad_rows[i] = (grad_ref[here, :] + grad).astype(bf16)
    for k in range(1, at.rows):
        target = xor_static(row, k, at.rows)
        row_copies[k] = remote(
            grad_rows.at[target],
            row_in.at[k - 1],
            row_sems,
            k - 1,
            "tp",
            target * at.share + part,
        )
        row_copies[k].start()
    for number in range(2):
        last[number].end_core(product_keep.at[number])
        last[number].start_half(0)

    small[0:8, :] = small_in[...]
    small[0:1, :] = gain_sum
    steps = [("tp", other_core())]
    steps += [("dp", xor_static(d, 1 << bit, at.dp)) for bit in bits]
    for number, (axis, index) in enumerate(steps):
        copy = remote(
            small.at[pl.ds(8 * number, 8)], small_ins.at[number], small_sems, number, axis, index
        )
        copy.start()
        copy.wait()
        small[8 * number + 8 : 8 * number + 16, :] = (
            small[8 * number : 8 * number + 8, :] + small_ins[number]
        )
    final = len(steps)
    small_copies = []
    for k in range(1, at.z_count):
        small_copies.append(
            remote(
                small.at[pl.ds(8 * final, 8)],
                small_ins.at[final + k - 1],
                small_sems,
                final + k - 1,
                "tp",
                tp_at(at, (z + k) % at.z_count),
            )
        )
    for copy in small_copies:
        copy.start()

    for place in range(1, len(bits)):
        for reduction in middle + last:
            reduction.end_half(place - 1)
            reduction.start_half(place)
    for reduction in middle + last:
        reduction.end_half(len(bits) - 1)
        reduction.start_z()
    input_out[row] = grad_rows[row].astype(f32)
    for k in range(1, at.rows):
        row_copies[k].wait()
        input_out[xor_static(row, k, at.rows)] = row_in[k - 1].astype(f32)
    total = small[8 * final : 8 * final + 8, :]
    for k, copy in enumerate(small_copies):
        copy.wait()
        total = total + small_ins[final + k]
    small_out[...] = total
    for reduction in middle + last:
        reduction.end_z()
        reduction.start_last()
    for reductions, out in ((middle, middle_out), (last, last_out)):
        columns = out.shape[2] // 2
        for number, reduction in enumerate(reductions):
            reduction.end_last(out, slice(number * columns, (number + 1) * columns))


def tail(at, held, dq, key_value_grads, x_low, grad_one, gain, weights, middle, small):
    keep_low, send_low, keep_high, send_high = middle
    tokens, features = held.shape
    _, rows, middle_columns = keep_low.shape
    key_width = key_value_grads[0].shape[2]
    last_columns = features // 2
    share_rows = rows // at.z_count // 2
    seq = tokens // at.rows
    steps = 1 + bits_of(at.dp)
    out_shape = [
        jax.ShapeDtypeStruct((at.rows, seq, features), f32),
        jax.ShapeDtypeStruct((8, features), f32),
        jax.ShapeDtypeStruct((2, share_rows, 2 * middle_columns), f32),
        jax.ShapeDtypeStruct((2, share_rows, 2 * last_columns), f32),
    ]
    scratch = []
    for columns in (middle_columns, middle_columns, last_columns, last_columns):
        scratch += Reduction.scratch(at, rows, columns)
    dma = lambda n: [pltpu.SemaphoreType.DMA((n,))] * 2
    scratch += [
        pltpu.VMEM((2, at.dp, rows, last_columns), bf16),
        pltpu.VMEM((2, at.dp, rows, last_columns), bf16),
        pltpu.VMEM((at.share - 1, 2, tokens, key_width), bf16),
        pltpu.VMEM((2, tokens, key_width), bf16),
        pltpu.VMEM((at.rows, seq, features), bf16),
        pltpu.VMEM((at.rows - 1, seq, features), bf16),
        pltpu.VMEM((8 * (steps + 1), features), f32),
        pltpu.VMEM((steps + at.z_count - 1, 8, features), f32),
        *dma(at.share - 1),
        *dma(at.rows - 1),
        *dma(steps + at.z_count - 1),
    ]
    return pl.pallas_call(
        functools.partial(tail_kernel, at),
        out_shape=out_shape,
        in_specs=[whole_vmem()] * 3
        + [any_space()] * (at.share - 1)
        + [whole_vmem()] * 8
        + [any_space()] * 2
        + [whole_vmem()],
        out_specs=[whole_vmem()] * 4,
        scratch_shapes=scratch,
        compiler_params=params(60, collective_id=1, has_side_effects=True),
        cost_estimate=pl.CostEstimate(
            flops=8 * tokens * features * features,
            bytes_accessed=100 * MIB,
            transcendentals=0,
        ),
        name="tail",
    )(
        held,
        dq,
        *key_value_grads,
        x_low,
        grad_one,
        gain,
        *weights,
        keep_low,
        keep_high,
        send_low,
        send_high,
        small,
    )


def own_and_other(pair, widths):
    core = lax.axis_index("tp") % 2
    first = jnp.where(core == 0, pair[0], pair[1])
    second = jnp.where(core == 0, pair[1], pair[0])
    results, offset = [], 0
    for width in widths:
        inside = slice(offset, offset + width // 2)
        results.append(jnp.concatenate([first[:, inside], second[:, inside]], axis=1))
        offset += width // 2
    return results


def gather_ffn(at, own, after):
    pieces = []
    current = own
    for k in range(at.z_count):
        if k == 1:
            current, _ = lax.optimization_barrier((current, after))
        if k:
            current = lax.ppermute(current, "tp", at.z_perm(1))
        held = {0: current}
        _, bits = half_order(at.dp, k % 2 == 0)
        for bit in bits:
            for s in list(held):
                held[s | 1 << bit] = lax.ppermute(held[s], "dp", at.dp_perm(1 << bit))
        pieces += [held[s] for s in range(at.dp)]
    return pieces, current


def relative_grad(at, diagonals, dfar):
    kinds = near_kinds(at.share)
    offset = jnp.arange(2 * BLOCK, dtype=jnp.int32) - (BLOCK - 1)
    distance = jnp.stack([BLOCK * kind_distance(at, kind) + offset for kind in kinds])
    bucket = bucket_of(jnp.maximum(distance, 0))
    onehot = (bucket[:, :, None] == jnp.arange(BUCKETS, dtype=jnp.int32)).astype(f32)
    sums = diagonals.reshape(GROUPS, len(kinds), 2, 2 * BLOCK)
    near = jnp.einsum(
        "ndb,gnjd->bgj", onehot, sums, precision=lax.Precision.HIGHEST
    ).reshape(BUCKETS, HEADS)
    far = jnp.sum(dfar.reshape(GROUPS, 8, 2, BLOCK), axis=(1, 3)).reshape(HEADS)
    return near.at[BUCKETS - 1].add(far)


def on_device(
    inputs,
    memory,
    segments,
    memory_segments,
    gain_self,
    gain_cross,
    gain_ffn,
    relative_bias,
    self_query,
    self_key,
    self_value,
    self_out,
    cross_query,
    cross_key,
    cross_value,
    cross_out,
    ffn_gate,
    ffn_up,
    ffn_down,
    cotangent,
):
    rows, seq, features = inputs.shape
    mem_seq = memory.shape[1]
    at = Places(rows)
    tokens = rows * seq
    mem_tokens = rows * mem_seq
    key_width = GROUPS * HEAD_DIM
    width = features // at.dp
    d = lax.axis_index("dp")

    x_pieces = exchange_rows(at, inputs)
    seg_parts = exchange_segments(at, jnp.concatenate([segments, memory_segments], axis=1))
    own_columns = lambda w: lax.dynamic_slice_in_dim(w, d * width, width, 1)
    own_rows = lambda w: lax.dynamic_slice_in_dim(w, d * width, width, 0).T
    own_piece = jnp.stack([own_rows(ffn_gate), own_rows(ffn_up), own_columns(ffn_down)])
    tiles = bias_tiles(at, relative_bias.reshape(-1))

    x_pieces, memory_in = lax.optimization_barrier((x_pieces, memory))
    mem_pieces = exchange_rows(at, memory_in)
    ffn_pieces, ring_end = gather_ffn(at, own_piece, mem_pieces)
    cot_in, _ = lax.optimization_barrier((cotangent, ring_end))
    cot_pieces = exchange_rows(at, cot_in)

    x_low = place_rows(at, inputs, x_pieces).reshape(tokens, features)
    x = x_low.astype(f32)

    last = relative_bias[BUCKETS - 1]
    high = lax.reduce_precision(last, 8, 7)
    mid = lax.reduce_precision(last - high, 8, 7)
    low = lax.reduce_precision(last - high - mid, 8, 7)
    last_parts = jnp.concatenate([high, mid, low])

    def key_features(seg):
        lane = jnp.arange(2 * HEAD_DIM, dtype=jnp.int32) % HEAD_DIM
        column = seg.reshape(-1, 1)
        return jnp.where(
            lane < 3, (column == lane).astype(f32), ((lane >= 3) & (lane < 6)).astype(f32)
        ).astype(bf16)

    self_features = [key_features(seg[:, :seq]) for seg in seg_parts]
    mem_features = [key_features(seg[:, seq:]) for seg in seg_parts]
    seg_row = seg_parts[0][:, :seq].reshape(1, tokens)

    held_self = (x * norm_scale(x) * gain_self).astype(bf16)
    queries = (nn(held_self, self_query) * SCALE).astype(bf16)
    kv = jnp.concatenate([nn(held_self, self_key), nn(held_self, self_value)], axis=1).astype(bf16)
    kvs = [kv] + [lax.ppermute(kv, "tp", at.part_perm(s)) for s in range(1, at.share)]
    mem = place_rows(at, memory, mem_pieces).reshape(mem_tokens, features)
    mem_kv = jnp.concatenate([nn(mem, cross_key), nn(mem, cross_value)], axis=1).astype(bf16)
    mem_kvs = [mem_kv] + [
        lax.ppermute(mem_kv, "tp", at.part_perm(s)) for s in range(1, at.share)
    ]
    self_context, self_log = attention_forward(
        at, queries, kvs, self_features, seg_row, tiles, last_parts
    )
    stream_one = x + nn(self_context, self_out)

    held_cross = (stream_one * norm_scale(stream_one) * gain_cross).astype(bf16)
    cross_queries = (nn(held_cross, cross_query) * SCALE).astype(bf16)
    cross_context, cross_log = attention_forward(
        at, cross_queries, mem_kvs, mem_features, seg_row
    )
    stream_two = stream_one + nn(cross_context, cross_out)

    held_ffn = (stream_two * norm_scale(stream_two) * gain_ffn).astype(bf16)
    cot = place_rows(at, cotangent, cot_pieces).reshape(tokens, features)
    cot_other = lax.ppermute(cot, "tp", at.core_perm())
    held_other = lax.ppermute(held_ffn, "tp", at.core_perm())
    out_own, out_other, back_own, back_other, ffn_grads = ffn(
        at, held_ffn, held_other, cot, cot_other, ffn_pieces
    )
    back_received = lax.ppermute(back_other, "tp", at.core_perm())
    out_received = lax.ppermute(out_other, "tp", at.core_perm())
    ffn_total = lax.psum_scatter(ffn_grads, "dp", scatter_dimension=0, tiled=True)[0]

    grad_held = back_own.astype(f32) + back_received.astype(f32)
    grad_stream, gain_ffn_part = norm_back(stream_two, gain_ffn, grad_held)
    grad_two = cot.astype(f32) + grad_stream
    output = (stream_two + (out_own.astype(f32) + out_received.astype(f32))).astype(bf16)
    output = output.reshape(rows, seq, features)
    output_pieces = exchange_rows(at, output)

    cross_branch = grad_two.astype(bf16)
    grad_cross_context = nt(cross_branch, cross_out).astype(bf16)
    grad_cross_queries, *grad_mem_kvs = attention_backward(
        at, cross_queries, mem_kvs, mem_features, seg_row, cross_log, grad_cross_context
    )

    def gathered_grads(parts):
        total = parts[0].astype(f32)
        for s in range(1, at.share):
            total = total + lax.ppermute(
                parts[s], "tp", at.part_perm(at.share - s)
            ).astype(f32)
        return total[0].astype(bf16), total[1].astype(bf16)

    grad_mem_keys, grad_mem_values = gathered_grads(grad_mem_kvs)
    grad_stream, gain_cross_part = norm_back(
        stream_one, gain_cross, nt(grad_cross_queries, cross_query)
    )
    grad_one = grad_two + grad_stream
    self_branch = grad_one.astype(bf16)
    grad_self_context = nt(self_branch, self_out).astype(bf16)
    memory_grad = (nt(grad_mem_keys, cross_key) + nt(grad_mem_values, cross_value)).astype(bf16)
    memory_grad = memory_grad.reshape(rows, mem_seq, features)
    memory_pieces = exchange_rows(at, memory_grad)
    middle_products = weight_products(
        at,
        [
            (cross_context, cross_branch),
            (held_cross, grad_cross_queries),
            (self_context, self_branch),
            (mem, grad_mem_keys),
            (mem, grad_mem_values),
        ],
    )
    grad_self_context, middle_products = lax.optimization_barrier(
        (grad_self_context, middle_products)
    )
    grad_queries, *more = attention_backward(
        at, queries, kvs, self_features, seg_row, self_log, grad_self_context, tiles, last_parts
    )
    grad_queries, output_pieces, memory_pieces, ffn_total = lax.optimization_barrier(
        (grad_queries, output_pieces, memory_pieces, ffn_total)
    )
    ffn_sum = reduce_ffn_grads(at, ffn_total)
    relative_part = relative_grad(at, more[at.share], more[at.share + 1]).reshape(1, -1)
    small = jnp.concatenate(
        [
            jnp.zeros((1, features), f32),
            gain_cross_part.reshape(1, -1),
            gain_ffn_part.reshape(1, -1),
            jnp.pad(relative_part, ((0, 0), (0, features - relative_part.shape[1]))),
            jnp.zeros((4, features), f32),
        ]
    )
    input_grad, small, middle_pair, last_pair = tail(
        at,
        held_self,
        grad_queries,
        more[: at.share],
        x_low,
        grad_one,
        gain_self.reshape(1, -1),
        (self_query, self_key, self_value),
        middle_products,
        small,
    )
    wide, narrow = features, key_width
    cross_out_grad, cross_query_grad, self_out_grad, cross_key_grad, cross_value_grad = (
        own_and_other(middle_pair, [wide, wide, wide, narrow, narrow])
    )
    self_query_grad, self_key_grad, self_value_grad = own_and_other(
        last_pair, [wide, narrow, narrow]
    )
    shards = at.dp * at.tp
    shard = lax.axis_index("dp") * at.tp + lax.axis_index("tp")
    share_of = lambda index, size: lax.dynamic_slice_in_dim(
        small[index], shard * (size // shards), size // shards
    )
    return (
        place_rows(at, output, output_pieces),
        input_grad,
        place_wide(at, memory_grad, memory_pieces),
        share_of(0, features),
        share_of(1, features),
        share_of(2, features),
        share_of(3, BUCKETS * HEADS),
        self_query_grad,
        self_key_grad,
        self_value_grad,
        self_out_grad,
        cross_query_grad,
        cross_key_grad,
        cross_value_grad,
        cross_out_grad,
        ffn_sum[0].T,
        ffn_sum[1].T,
        ffn_sum[2],
    )


def solution(mesh):
    placed = (
        P("dp", "tp", None),
        P("dp", "tp", None),
        P("dp", "tp"),
        P("dp", "tp"),
        P(),
        P(),
        P(),
        P(),
        P(),
        P(),
        P(),
        P(),
        P(),
        P(),
        P(),
        P(),
        P(None, "tp"),
        P(None, "tp"),
        P("tp", None),
        P("dp", "tp", None),
    )
    return jax.shard_map(
        on_device,
        mesh=mesh,
        in_specs=placed,
        out_specs=(
            P("dp", "tp", None),
            P("dp", "tp", None),
            P("dp", "tp", None),
            P(("dp", "tp")),
            P(("dp", "tp")),
            P(("dp", "tp")),
            P(("dp", "tp")),
            P(("dp", "tp"), None),
            P(("dp", "tp"), None),
            P(("dp", "tp"), None),
            P(("dp", "tp"), None),
            P(("dp", "tp"), None),
            P(("dp", "tp"), None),
            P(("dp", "tp"), None),
            P(("dp", "tp"), None),
            P("dp", "tp"),
            P("dp", "tp"),
            P("tp", "dp"),
        ),
        check_vma=False,
    )
```

```python
import functools
import math
import types
import typing

import jax
import jax.numpy as jnp
from jax import lax
from jax.experimental import pallas as pl
from jax.experimental.pallas import tpu as pltpu
from jax.sharding import PartitionSpec as P

HEADS = 16
HEAD_DIM = 64
GROUPS = 8
BUCKETS = 32
MAX_DIST = 128
BLOCK = 128
PAIRS = GROUPS // 2
FAR = -1e30
SCALE = HEAD_DIM ** (-0.5)
MIB = 1 << 20

norm_epsilon = 1e-06
f32 = jnp.float32
bf16 = jnp.bfloat16


def nn(left, right):
    return lax.dot_general(left, right, (((1,), (0,)), ((), ())), preferred_element_type=f32)


def nt(left, right):
    return lax.dot_general(left, right, (((1,), (1,)), ((), ())), preferred_element_type=f32)


def tn(left, right):
    return lax.dot_general(left, right, (((0,), (0,)), ((), ())), preferred_element_type=f32)


def bits_of(count):
    return count.bit_length() - 1


def xor_static(value, flips, count):
    result = value
    for bit in range(bits_of(count)):
        if flips >> bit & 1:
            result = result + (1 << bit) * (1 - 2 * ((value // (1 << bit)) % 2))
    return result


def half_order(count, first_low):
    nb = bits_of(count)
    bits = list(range(nb)) if first_low else list(range(nb))[::-1]
    order = []
    for index in range(count):
        s = 0
        for place, bit in enumerate(bits):
            if index >> (nb - 1 - place) & 1:
                s |= 1 << bit
        order.append(s)
    return order, bits


def norm_scale(v):
    return lax.rsqrt(jnp.mean(v * v, axis=-1, keepdims=True) + norm_epsilon)


def norm_back(v, gain, dy):
    s = norm_scale(v)
    gained = dy * gain
    grad = s * gained - v * (s * s * s * jnp.mean(gained * v, axis=-1, keepdims=True))
    return grad, jnp.sum(dy * v * s, axis=0, keepdims=True)


def bucket_of(distance):
    exact = BUCKETS // 2
    bucket_count = jnp.zeros_like(distance)
    for step_index in range(1, exact):
        threshold = math.ceil(exact * (MAX_DIST / exact) ** (step_index / exact))
        bucket_count = bucket_count + (distance >= threshold).astype(jnp.int32)
    return jnp.where(distance < exact, distance, exact + bucket_count)


def whole_vmem():
    return pl.BlockSpec(memory_space=pltpu.VMEM)


def whole_smem():
    return pl.BlockSpec(memory_space=pltpu.SMEM)


def any_space():
    return pl.BlockSpec(memory_space=pl.ANY)


def params(limit_mib, **more):
    return pltpu.CompilerParams(vmem_limit_bytes=limit_mib * MIB, **more)


class Places:
    def __init__(self, rows):
        self.tp = lax.axis_size("tp")
        self.dp = lax.axis_size("dp")
        self.rows = rows
        self.share = self.tp // rows
        self.z_count = self.tp // 2

    def row(self):
        return lax.axis_index("tp") // self.share

    def part(self):
        return lax.axis_index("tp") % self.share

    def row_perm(self, k):
        share = self.share
        return [(t, ((t // share) ^ k) * share + t % share) for t in range(self.tp)]

    def part_perm(self, shift):
        share = self.share
        return [
            (t // share * share + (t % share + shift) % share, t) for t in range(self.tp)
        ]

    def core_perm(self):
        return [(t, t ^ 1) for t in range(self.tp)]

    def z_perm(self, shift):
        z_count = self.z_count
        return [(t, (t // 2 + shift) % z_count * 2 + t % 2) for t in range(self.tp)]

    def dp_perm(self, flips):
        return [(d, d ^ flips) for d in range(self.dp)]


def near_kinds(share):
    kinds = [(s, 0) for s in range(share)]
    return kinds + [(s, 1) for s in range(share) if s > 0 or share == 1]


def kind_distance(at, kind):
    s, back = kind
    part = at.part()
    return part - (part + s) % at.share + at.share * back


def tile_distance(at, kind):
    key = lax.broadcasted_iota(jnp.int32, (BLOCK, BLOCK), 0)
    query = lax.broadcasted_iota(jnp.int32, (BLOCK, BLOCK), 1)
    return BLOCK * kind_distance(at, kind) + query - key


def fill_bias_tiles(at, table, tiles):
    kinds = near_kinds(at.share)

    def one_group(group, carry):
        for number, kind in enumerate(kinds):
            distance = tile_distance(at, kind)
            bucket = bucket_of(jnp.maximum(distance, 0))
            for j in range(2):
                head = group * 2 + j
                last = table[(BUCKETS - 1) * HEADS + head]
                value = jnp.zeros((BLOCK, BLOCK), f32)
                for b in range(BUCKETS - 1):
                    value = jnp.where(bucket == b, table[b * HEADS + head] - last, value)
                tiles[group, number, :, j * BLOCK : (j + 1) * BLOCK] = jnp.where(
                    distance < 0, FAR, value
                )
        return carry

    lax.fori_loop(0, GROUPS, one_group, 0)


def query_features(seg_block, last_parts, group):
    shape = (HEAD_DIM, 2 * BLOCK)
    row = lax.broadcasted_iota(jnp.int32, shape, 0)
    seg = jnp.concatenate([seg_block, seg_block], axis=1)
    feature = jnp.where((row < 3) & (seg != row), FAR, 0.0)
    if last_parts is not None:
        lane = lax.broadcasted_iota(jnp.int32, shape, 1)
        for part in range(3):
            first = last_parts[part * HEADS + group * 2]
            second = last_parts[part * HEADS + group * 2 + 1]
            feature = jnp.where(row == 3 + part, jnp.where(lane < BLOCK, first, second), feature)
    return feature.astype(bf16)


def turned(block):
    return block.astype(f32).T.astype(block.dtype)


def stacked_heads(pair):
    t = turned(pair)
    return jnp.concatenate([t[:HEAD_DIM], t[HEAD_DIM:]], axis=1)


def unstacked_heads(wide):
    return jnp.concatenate([wide[:, :BLOCK], wide[:, BLOCK:]], axis=0).T


def with_other(half, other, odd):
    return jnp.concatenate([other, half] if odd else [half, other], axis=0)


def fold_rows(tile):
    return tile.reshape(tile.shape[0] // 8, 8, tile.shape[1])


class Keys:
    def __init__(self, share, blocks, causal):
        self.share, self.blocks, self.causal = share, blocks, causal
        self.count = share * blocks

    def blocks_for(self, i):
        return (i + 1 if self.causal else self.blocks) * self.share

    def near(self, i, index, kinds):
        if not self.causal:
            return None
        j, s = divmod(index, self.share)
        kind = (s, i - j)
        return kinds.index(kind) if kind in kinds else None


def load_keys(keys, k_refs, feat_refs, odd, kaug):
    lane = lax.broadcasted_iota(jnp.int32, (BLOCK, 2 * HEAD_DIM), 1)
    own = (lane >= HEAD_DIM) if odd else (lane < HEAD_DIM)
    for index in range(keys.count):
        j, s = divmod(index, keys.share)
        rows = pl.ds(j * BLOCK, BLOCK)
        kaug[pl.ds(index * BLOCK, BLOCK), :] = jnp.where(
            own, k_refs[s][rows, :].astype(f32), feat_refs[s][rows, :].astype(f32)
        ).astype(bf16)


def turn_keys(keys, refs, target):
    for index in range(keys.count):
        j, s = divmod(index, keys.share)
        target[:, pl.ds(index * BLOCK, BLOCK)] = turned(refs[s][pl.ds(j * BLOCK, BLOCK), :])


def forward_pair(
    keys, kinds, pair, q_ref, seg_ref, kv_refs, feat_refs, tiles, last_parts, ctx_ref, log_ref, scratch
):
    kaug, vt, sbuf, pbuf = scratch
    lanes_at = lambda start, width: pl.ds(pl.multiple_of(start, BLOCK), width)
    k_refs = [ref.at[:, lanes_at(pair * BLOCK, BLOCK)] for ref in kv_refs]
    v_refs = [
        ref.at[:, lanes_at(GROUPS * HEAD_DIM + pair * BLOCK, BLOCK)] for ref in kv_refs
    ]
    turn_keys(keys, v_refs, vt)
    for gi in range(2):
        load_keys(keys, k_refs, feat_refs, gi, kaug)
        for i in range(q_ref.shape[0] // BLOCK):
            tokens = pl.ds(i * BLOCK, BLOCK)
            lanes = lanes_at((pair * 2 + gi) * BLOCK, BLOCK)
            features = query_features(seg_ref[:, tokens], last_parts, pair * 2 + gi)
            right = with_other(stacked_heads(q_ref[tokens, lanes]), features, gi)
            count = keys.blocks_for(i)
            top = jnp.full((8, 2 * BLOCK), -jnp.inf, f32)
            for index in range(count):
                rows = pl.ds(index * BLOCK, BLOCK)
                scores = nn(kaug[rows, :], right)
                near = keys.near(i, index, kinds)
                if near is not None:
                    scores = scores + tiles[pair * 2 + gi, near]
                sbuf[rows, :] = scores
                top = jnp.maximum(top, jnp.max(fold_rows(scores), axis=0))
            top = jnp.max(top, axis=0, keepdims=True)
            total = jnp.zeros((8, 2 * BLOCK), f32)
            for index in range(count):
                rows = pl.ds(index * BLOCK, BLOCK)
                exponent = jnp.exp(sbuf[rows, :] - top)
                total = total + jnp.sum(fold_rows(exponent), axis=0)
                pbuf[rows, :] = exponent.astype(bf16)
            total = jnp.sum(total, axis=0, keepdims=True)
            length = count * BLOCK
            context = nn(vt[pl.ds(gi * HEAD_DIM, HEAD_DIM), :length], pbuf[:length, :])
            ctx_ref[tokens, lanes] = unstacked_heads(context * (1.0 / total)).astype(bf16)
            log_ref[pair * 2 + gi, pl.ds(i, 1), :] = top + jnp.log(total)


def diagonal_sums(tile):
    row = lax.broadcasted_iota(jnp.int32, (BLOCK, BLOCK), 0)
    lane = lax.broadcasted_iota(jnp.int32, (BLOCK, BLOCK), 1)
    turn = (row + lane == BLOCK - 1).astype(f32).astype(bf16)
    high = tile.astype(bf16)
    rest = tile - high.astype(f32)
    mid = rest.astype(bf16)
    low = (rest - mid.astype(f32)).astype(bf16)
    turned_rows = nn(turn, high) + nn(turn, mid) + nn(turn, low)
    sums = []
    for j in range(2):
        part = turned_rows[:, j * BLOCK : (j + 1) * BLOCK]
        wide = jnp.concatenate([part, jnp.zeros_like(part)], axis=1)
        rolled = pltpu.roll(wide, 0, 1, stride=1, stride_axis=0)
        sums.append(jnp.sum(rolled, axis=0, keepdims=True))
    return jnp.concatenate(sums, axis=0)


def backward_body(
    keys,
    kinds,
    pair,
    q_ref,
    seg_ref,
    k_refs,
    v_refs,
    feat_refs,
    tiles,
    last_parts,
    log_ref,
    dctx_ref,
    dq_ref,
    dkv_refs,
    diagonals,
    dfar,
    scratch,
):
    kaug, kt, vn, sbuf, pbuf, gbuf, dk_acc, dv_acc, dtiles = scratch
    turn_keys(keys, k_refs, kt)
    for index in range(keys.count):
        j, s = divmod(index, keys.share)
        vn[pl.ds(index * BLOCK, BLOCK), :] = v_refs[s][pl.ds(j * BLOCK, BLOCK), :]
    for gi in range(2):
        load_keys(keys, k_refs, feat_refs, gi, kaug)
        group_rows = pl.ds(gi * HEAD_DIM, HEAD_DIM)
        seen = set()
        far = jnp.zeros((8, 2 * BLOCK), f32)
        n_blocks = q_ref.shape[0] // BLOCK
        for i in reversed(range(n_blocks)):
            tokens = pl.ds(i * BLOCK, BLOCK)
            lanes = pl.ds(gi * BLOCK, BLOCK)
            features = query_features(seg_ref[:, tokens], last_parts, pair * 2 + gi)
            queries = stacked_heads(q_ref[tokens, lanes])
            right = with_other(queries, features, gi)
            grads = stacked_heads(dctx_ref[tokens, lanes])
            grads_right = with_other(grads, jnp.zeros_like(grads), gi)
            logsum = log_ref[gi, pl.ds(i, 1), :]
            count = keys.blocks_for(i)
            middle = jnp.zeros((8, 2 * BLOCK), f32)
            for index in range(count):
                rows = pl.ds(index * BLOCK, BLOCK)
                scores = nn(kaug[rows, :], right)
                near = keys.near(i, index, kinds)
                if near is not None:
                    scores = scores + tiles[gi, near]
                probs = jnp.exp(scores - logsum)
                grad_probs = nn(vn[rows, :], grads_right)
                middle = middle + jnp.sum(fold_rows(probs * grad_probs), axis=0)
                sbuf[rows, :] = probs
                gbuf[rows, :] = grad_probs
                pbuf[rows, :] = probs.astype(bf16)
            middle = jnp.sum(middle, axis=0, keepdims=True)
            length = count * BLOCK
            grad_v = nt(grads, pbuf[:length, :])
            for index in range(count):
                rows = pl.ds(index * BLOCK, BLOCK)
                grad_scores = (sbuf[rows, :] * (gbuf[rows, :] - middle)).astype(bf16)
                pbuf[rows, :] = grad_scores
                if keys.causal:
                    wide = grad_scores.astype(f32)
                    near = keys.near(i, index, kinds)
                    if near is None:
                        far = far + jnp.sum(fold_rows(wide), axis=0)
                    elif near in seen:
                        dtiles[near] = dtiles[near] + wide
                    else:
                        dtiles[near] = wide
                        seen.add(near)
            grad_k = nt(queries, pbuf[:length, :])
            grad_q = nn(kt[group_rows, :length], pbuf[:length, :])
            dq_ref[tokens, lanes] = unstacked_heads(grad_q * SCALE).astype(bf16)
            if i == n_blocks - 1:
                dk_acc[group_rows, :length] = grad_k
                dv_acc[group_rows, :length] = grad_v
            else:
                dk_acc[group_rows, :length] += grad_k
                dv_acc[group_rows, :length] += grad_v
        if keys.causal:
            dfar[gi] = far
            for near in range(len(kinds)):
                diagonals[gi, 2 * near : 2 * near + 2, :] = diagonal_sums(dtiles[near])
    for index in range(keys.count):
        j, s = divmod(index, keys.share)
        columns = pl.ds(index * BLOCK, BLOCK)
        rows = pl.ds(j * BLOCK, BLOCK)
        dkv_refs[s][0, rows, :] = dk_acc[:, columns].T.astype(bf16)
        dkv_refs[s][1, rows, :] = dv_acc[:, columns].T.astype(bf16)


class DpSum:
    def __init__(self, at):
        self.at = at
        self.bits = [half_order(at.dp, half == 0)[1] for half in range(2)]
        self.d = lax.axis_index("dp")

    def held(self, half, step):
        gone = self.bits[half][:step]
        return [s for s in range(self.at.dp) if not any(s >> bit & 1 for bit in gone)]

    def sent(self, half, step):
        bit = self.bits[half][step]
        return [(s, s ^ 1 << bit) for s in self.held(half, step) if s >> bit & 1]

    def count(self, step):
        return len(self.held(0, step))

    def partner(self, half, step):
        return xor_static(self.d, 1 << self.bits[half][step], self.at.dp)

    def copies(self, step, source_of, landing, sems):
        made = []
        for half in range(2):
            for sent, joined in self.sent(half, step):
                slot = self.held(half, step + 1).index(joined)
                made.append(
                    remote(
                        source_of(half, sent),
                        landing.at[half, slot],
                        sems,
                        half * self.count(step + 1) + slot,
                        "dp",
                        self.partner(half, step),
                    )
                )
        return made


def first_step_scratch(at, half_shape):
    return [
        pltpu.VMEM(half_shape, bf16),
        pltpu.VMEM(half_shape, bf16),
        pltpu.SemaphoreType.DMA((at.dp,)),
        pltpu.SemaphoreType.DMA((at.dp,)),
        pltpu.SemaphoreType.DMA((at.dp,)),
    ]


def half_shape_of(at, grads):
    return (2, at.dp // 2, at.z_count // 2, *grads.shape[2:])


class FirstStep:
    BUFFERS = 5

    def __init__(self, at, source, out, buffers):
        self.at, self.source, self.out = at, source, out
        self.landing, self.own, *self.sems, self.own_sems = buffers

    def copies(self):
        total = DpSum(self.at)
        half_z = self.at.z_count // 2
        entry = lambda half, s: self.source.at[
            xor_static(total.d, s, self.at.dp), pl.ds(half * half_z, half_z)
        ]
        made = total.copies(0, entry, self.landing, self.sems)
        for half in range(2):
            for slot, s in enumerate(total.held(half, 1)):
                made.append(
                    pltpu.make_async_copy(
                        entry(half, s),
                        self.own.at[half, slot],
                        self.own_sems.at[half * total.count(1) + slot],
                    )
                )
        return made

    def start(self):
        for copy in self.copies():
            copy.start()

    def end(self):
        for copy in self.copies():
            copy.wait()
        for half in range(2):
            for slot in range(self.at.dp // 2):
                for chunk in range(self.at.z_count // 2):
                    for m in range(3):
                        self.out[half, slot, chunk, m] = (
                            self.own[half, slot, chunk, m] + self.landing[half, slot, chunk, m]
                        )


def cross_backward_kernel(at, keys, *refs):
    refs = list(refs)
    take = lambda n: [refs.pop(0) for _ in range(n)]
    q_ref, seg_ref = take(2)
    k_refs, v_refs, feat_refs = take(keys.share), take(keys.share), take(keys.share)
    log_ref, dctx_ref, ffn_in, output_in = take(4)
    (dq_ref,) = take(1)
    dkv_refs = take(keys.share)
    ffn_out, output_out = take(2)
    first = FirstStep(at, ffn_in, ffn_out, take(FirstStep.BUFFERS))
    return_buffers = take(RowReturn.BUFFERS)

    @pl.when(pl.program_id(0) == 0)
    def _():
        greet(at)
        first.start()
        RowReturn(at, output_in, output_out, return_buffers).start()

    backward_body(
        keys,
        None,
        pl.program_id(0),
        q_ref,
        seg_ref,
        k_refs,
        v_refs,
        feat_refs,
        None,
        None,
        log_ref,
        dctx_ref,
        dq_ref,
        dkv_refs,
        None,
        None,
        (*refs, None),
    )

    @pl.when(pl.program_id(0) == PAIRS - 1)
    def _():
        first.end()
        RowReturn(at, output_in, output_out, return_buffers).end()


def backward_scratch(length):
    return [
        pltpu.VMEM((length, 2 * HEAD_DIM), bf16),
        pltpu.VMEM((2 * HEAD_DIM, length), bf16),
        pltpu.VMEM((length, 2 * HEAD_DIM), bf16),
        pltpu.VMEM((length, 2 * BLOCK), f32),
        pltpu.VMEM((length, 2 * BLOCK), bf16),
        pltpu.VMEM((length, 2 * BLOCK), f32),
        pltpu.VMEM((2 * HEAD_DIM, length), f32),
        pltpu.VMEM((2 * HEAD_DIM, length), f32),
    ]


def cross_backward(
    at, queries, key_values, features, seg_row, logsum, grad_context, ffn_grads, output
):
    tokens = queries.shape[0]
    span = key_values[0].shape[0]
    blocks = tokens // BLOCK
    keys = Keys(at.share, span // BLOCK, False)
    length = keys.count * BLOCK
    work = blocks * length * 2 * BLOCK * GROUPS
    token_spec = pl.BlockSpec((tokens, 2 * BLOCK), lambda p: (0, p))
    specs = [token_spec, pl.BlockSpec(seg_row.shape, lambda p: (0, 0))]
    specs += [pl.BlockSpec((span, BLOCK), lambda p: (0, p))] * at.share
    specs += [pl.BlockSpec((span, BLOCK), lambda p: (0, PAIRS + p))] * at.share
    specs += [pl.BlockSpec((span, BLOCK), lambda p: (0, 0))] * at.share
    specs += [pl.BlockSpec((2, blocks, 2 * BLOCK), lambda p: (p, 0, 0)), token_spec]
    specs += [any_space()] * 2
    half_shape = half_shape_of(at, ffn_grads)
    return pl.pallas_call(
        functools.partial(cross_backward_kernel, at, keys),
        grid=(PAIRS,),
        out_shape=[jax.ShapeDtypeStruct((tokens, HEADS * HEAD_DIM), bf16)]
        + [jax.ShapeDtypeStruct((2, span, GROUPS * HEAD_DIM), bf16)] * at.share
        + [jax.ShapeDtypeStruct(half_shape, bf16), jax.ShapeDtypeStruct(output.shape, bf16)],
        in_specs=specs,
        out_specs=[token_spec]
        + [pl.BlockSpec((2, span, BLOCK), lambda p: (0, 0, p))] * at.share
        + [whole_vmem()] * 2,
        scratch_shapes=[
            *first_step_scratch(at, half_shape),
            *RowReturn.scratch(at, output),
            *backward_scratch(length),
        ],
        compiler_params=params(48, collective_id=4, has_side_effects=True),
        cost_estimate=pl.CostEstimate(
            flops=work * 1024, bytes_accessed=16 * MIB, transcendentals=work
        ),
        name="cross_backward",
    )(
        queries,
        seg_row,
        *key_values,
        *key_values,
        *features,
        logsum,
        grad_context,
        ffn_grads,
        output,
    )


def remote(source, target, sems, number, axis, index):
    send, receive = sems
    return pltpu.make_async_remote_copy(
        src_ref=source,
        dst_ref=target,
        send_sem=send.at[number],
        recv_sem=receive.at[number],
        device_id={axis: index},
        device_id_type=pl.DeviceIdType.MESH,
    )


def tp_at(at, z):
    return z * 2 + lax.axis_index("tp") % 2


def other_core():
    t = lax.axis_index("tp")
    return t + 1 - 2 * (t % 2)


def greet(at):
    barrier = pltpu.get_barrier_semaphore()
    t, d = lax.axis_index("tp"), lax.axis_index("dp")
    if at.share == 2:
        others = [other_core()]
        others += [tp_at(at, (t // 2 + k) % at.z_count) for k in range(1, at.z_count)]
    else:
        others = [(t + k) % at.tp for k in range(1, at.tp)]
    targets = [{"tp": other} for other in others]
    targets += [{"dp": xor_static(d, 1 << bit, at.dp)} for bit in range(bits_of(at.dp))]
    for target in targets:
        pl.semaphore_signal(
            barrier, inc=1, device_id=target, device_id_type=pl.DeviceIdType.MESH
        )
    pl.semaphore_wait(barrier, len(targets))


def key_feature_tile(seg_line):
    column = jnp.broadcast_to(seg_line.astype(f32), (BLOCK, BLOCK)).T
    lane = lax.broadcasted_iota(jnp.int32, (BLOCK, BLOCK), 1) % HEAD_DIM
    same = jnp.where(column == lane.astype(f32), 1.0, 0.0)
    ones = jnp.where(lane < 6, 1.0, 0.0)
    return jnp.where(lane < 3, same, ones).astype(bf16)


def forward_messages(at):
    names = [(kind, k) for k in range(1, at.rows) for kind in ("x", "seg", "mem", "cot")]
    names += [(kind, s) for s in range(1, at.share) for kind in ("seg_part", "kv", "mem_kv")]
    names += [("ring", k) for k in range(1, at.z_count)]
    names += [("w", k, s) for k in range(at.z_count) for s in range(1, at.dp)]
    names += [("cot_core",), ("held",)]
    return {name: number for number, name in enumerate(names)}


class Gather:
    def __init__(self, at, start, copies, flush, own, gathered, out):
        self.at, self.start, self.copies, self.flush = at, start, copies, flush
        self.own, self.gathered, self.out = own, gathered, out
        self.z, self.d = lax.axis_index("tp") // 2, lax.axis_index("dp")

    def order(self, k):
        return half_order(self.at.dp, k % 2 == 0)[1]

    def held(self, k, s):
        return self.own if (k, s) == (0, 0) else self.gathered.at[k, s]

    def pass_on(self, k, s):
        bits = self.order(k)
        seen = [place for place, bit in enumerate(bits) if s >> bit & 1]
        for bit in bits[max(seen) + 1 if seen else 0 :]:
            self.start(
                ("w", k, s | 1 << bit),
                self.held(k, s),
                self.gathered.at[k, s | 1 << bit],
                "dp",
                xor_static(self.d, 1 << bit, self.at.dp),
            )

    def ring(self, k):
        self.start(
            ("ring", k),
            self.held(k - 1, 0),
            self.gathered.at[k, 0],
            "tp",
            tp_at(self.at, (self.z + 1) % self.at.z_count),
        )

    def arrived(self, k, s):
        self.copies["w", k, s].wait()
        self.flush(self.gathered.at[k, s], self.out.at[k, s])

    def arrive_ring(self, k):
        self.copies["ring", k].wait()
        self.flush(self.gathered.at[k, 0], self.out.at[k, 0])
        if k + 1 < self.at.z_count:
            self.ring(k + 1)
        self.pass_on(k, 0)

    def relay(self, k):
        bits = self.order(k)
        held = [0]
        for bit in bits[:-1]:
            for s in list(held):
                self.arrived(k, s | 1 << bit)
                self.pass_on(k, s | 1 << bit)
                held.append(s | 1 << bit)

    def finish(self, k):
        last = self.order(k)[-1]
        for s in range(self.at.dp):
            if s >> last & 1:
                self.arrived(k, s)


class Kept(typing.NamedTuple):
    x: typing.Any
    held_self: typing.Any
    queries: typing.Any
    kv: typing.Any
    self_context: typing.Any
    self_log: typing.Any
    stream_one: typing.Any
    held_cross: typing.Any
    cross_queries: typing.Any
    mem: typing.Any
    mem_kv: typing.Any
    cross_context: typing.Any
    cross_log: typing.Any
    stream_two: typing.Any
    held_ffn: typing.Any
    tiles: typing.Any
    seg_row: typing.Any


def forward_kernel(at, shapes, *refs):
    refs = list(refs)
    take = lambda n: [refs.pop(0) for _ in range(n)]
    inputs, memory, cot_in, segs, piece = take(5)
    weight_refs = take(8)
    gains, table, last_parts = take(3)
    outs = Kept(*take(len(Kept._fields)))
    feat_outs, mem_feat_outs = take(at.share), take(at.share)
    kv_outs, mem_kv_outs = take(at.share - 1), take(at.share - 1)
    cot_out, cot_other_out, held_other_out, gathered_out = take(4)
    bufs = Kept(*take(len(Kept._fields)))
    feats, mem_feats = take(at.share), take(at.share)
    kv_others, mem_kv_others = take(at.share - 1), take(at.share - 1)
    weights = take(8)
    cot, cot_other, held_other, gathered = take(4)
    seg_buf, seg_others, kaug, vt, sbuf, pbuf = take(6)
    send_sems, recv_sems, load_sems, flush_sems = take(4)
    scratch = (kaug, vt, sbuf, pbuf)
    numbers = forward_messages(at)
    kinds = near_kinds(at.share)
    row, part = at.row(), at.part()
    z = lax.axis_index("tp") // 2
    seq, features = inputs.shape[1:]
    mem_seq = memory.shape[1]
    tokens, mem_tokens = at.rows * seq, at.rows * mem_seq
    key_width = GROUPS * HEAD_DIM
    copies, flushes = {}, []

    def start(name, source, target, axis, index):
        copies[name] = remote(source, target, (send_sems, recv_sems), numbers[name], axis, index)
        copies[name].start()

    def start_rows(kind, source, target, height):
        for k in range(1, at.rows):
            there = xor_static(row, k, at.rows)
            start(
                (kind, k),
                source.at[there],
                target.at[pl.ds(pl.multiple_of(row * height, height), height), :],
                "tp",
                there * at.share + part,
            )

    def start_parts(kind, source, targets):
        for s in range(1, at.share):
            start(
                (kind, s),
                source,
                targets[s - 1],
                "tp",
                row * at.share + (part + at.share - s) % at.share,
            )

    def wait(kind, count):
        for k in range(1, count):
            copies[kind, k].wait()

    def flush(source, target):
        copy = pltpu.make_async_copy(source, target, flush_sems.at[len(flushes)])
        flushes.append(copy)
        copy.start()
        return copy

    def local_rows(source, target, height, number):
        return pltpu.make_async_copy(
            source.at[row],
            target.at[pl.ds(pl.multiple_of(row * height, height), height), :],
            load_sems.at[number],
        )

    greet(at)
    start_rows("x", inputs, bufs.x, seq)
    for k in range(1, at.rows):
        there = xor_static(row, k, at.rows)
        start(
            ("seg", k), segs.at[there], seg_buf.at[row], "tp", there * at.share + part
        )
    gather = Gather(at, start, copies, flush, piece, gathered, gathered_out)
    gather.pass_on(0, 0)
    loads = [local_rows(inputs, bufs.x, seq, 8), local_rows(memory, bufs.mem, mem_seq, 9)]
    loads += [
        local_rows(cot_in, cot, seq, 10),
        pltpu.make_async_copy(segs.at[row], seg_buf.at[row], load_sems.at[11]),
    ]
    weight_loads = [
        pltpu.make_async_copy(source, target, load_sems.at[number])
        for number, (source, target) in enumerate(zip(weight_refs, weights))
    ]
    for copy in loads + weight_loads:
        copy.start()
    for copy in loads:
        copy.wait()
    flush(piece, gathered_out.at[0, 0])
    fill_bias_tiles(at, table, bufs.tiles)
    flush(bufs.tiles, outs.tiles)
    wait("seg", at.rows)
    start_parts("seg_part", seg_buf, [seg_others.at[s] for s in range(at.share - 1)])
    wait("seg_part", at.share)
    for s in range(at.share):
        for i in range(at.rows):
            line = lambda j: seg_buf[i, j : j + 1, :] if s == 0 else seg_others[s - 1, i, j : j + 1, :]
            feats[s][i * seq : (i + 1) * seq, :] = key_feature_tile(line(0))
            mem_feats[s][i * mem_seq : (i + 1) * mem_seq, :] = key_feature_tile(line(1))[:mem_seq]
            if s == 0:
                bufs.seg_row[:, i * seq : (i + 1) * seq] = line(0)
        flush(feats[s], feat_outs[s])
        flush(mem_feats[s], mem_feat_outs[s])
    flush(bufs.seg_row, outs.seg_row)
    gather.relay(0)
    for copy in weight_loads:
        copy.wait()
    sq, sk, sv, so, cq, ck, cv, co = weights

    def blocks(height):
        step = min(256, height)
        return [pl.ds(first, step) for first in range(0, height, step)]

    def normed(value, number):
        return (value * norm_scale(value) * gains[number : number + 1, :]).astype(bf16)

    wait("x", at.rows)
    gather.ring(1)
    flush(bufs.x, outs.x)
    for here in blocks(tokens):
        held = normed(bufs.x[here, :].astype(f32), 0)
        bufs.held_self[here, :] = held
        bufs.kv[here, :key_width] = nn(held, sk[...]).astype(bf16)
        bufs.kv[here, key_width:] = nn(held, sv[...]).astype(bf16)
    start_parts("kv", bufs.kv, kv_others)
    for here in blocks(tokens):
        bufs.queries[here, :] = (nn(bufs.held_self[here, :], sq[...]) * SCALE).astype(bf16)
    flush(bufs.held_self, outs.held_self)
    flush(bufs.kv, outs.kv)
    flush(bufs.queries, outs.queries)
    gather.arrive_ring(1)
    wait("kv", at.share)
    for s in range(at.share - 1):
        flush(kv_others[s], kv_outs[s])

    def self_pair(pair, carry):
        forward_pair(
            Keys(at.share, at.rows, True),
            kinds,
            pair,
            bufs.queries,
            bufs.seg_row,
            [bufs.kv, *kv_others],
            feats,
            bufs.tiles,
            last_parts,
            bufs.self_context,
            bufs.self_log,
            scratch,
        )
        return carry

    start_rows("mem", memory, bufs.mem, mem_seq)
    lax.fori_loop(0, 2, self_pair, 0)
    if at.z_count > 2:
        gather.arrive_ring(2)
    gather.relay(1)
    lax.fori_loop(2, PAIRS, self_pair, 0)
    for k in range(3, at.z_count):
        gather.arrive_ring(k)
        gather.relay(k - 1)
    start_rows("cot", cot_in, cot, seq)
    wait("mem", at.rows)
    flush(bufs.mem, outs.mem)
    flush(bufs.self_context, outs.self_context)
    flush(bufs.self_log, outs.self_log)
    for here in blocks(mem_tokens):
        rows = bufs.mem[here, :]
        bufs.mem_kv[here, :key_width] = nn(rows, ck[...]).astype(bf16)
        bufs.mem_kv[here, key_width:] = nn(rows, cv[...]).astype(bf16)
    start_parts("mem_kv", bufs.mem_kv, mem_kv_others)
    flush(bufs.mem_kv, outs.mem_kv)
    for here in blocks(tokens):
        stream = bufs.x[here, :].astype(f32) + nn(bufs.self_context[here, :], so[...])
        bufs.stream_one[here, :] = stream
        held = normed(stream, 1)
        bufs.held_cross[here, :] = held
        bufs.cross_queries[here, :] = (nn(held, cq[...]) * SCALE).astype(bf16)
    flush(bufs.stream_one, outs.stream_one)
    flush(bufs.held_cross, outs.held_cross)
    flush(bufs.cross_queries, outs.cross_queries)

    wait("mem_kv", at.share)
    for s in range(at.share - 1):
        flush(mem_kv_others[s], mem_kv_outs[s])

    def cross_pair(pair, carry):
        forward_pair(
            Keys(at.share, mem_tokens // BLOCK, False),
            kinds,
            pair,
            bufs.cross_queries,
            bufs.seg_row,
            [bufs.mem_kv, *mem_kv_others],
            mem_feats,
            None,
            None,
            bufs.cross_context,
            bufs.cross_log,
            scratch,
        )
        return carry

    lax.fori_loop(0, 2, cross_pair, 0)
    gather.relay(at.z_count - 1)
    lax.fori_loop(2, PAIRS, cross_pair, 0)
    flush(bufs.cross_context, outs.cross_context)
    flush(bufs.cross_log, outs.cross_log)
    for here in blocks(tokens):
        stream = bufs.stream_one[here, :] + nn(bufs.cross_context[here, :], co[...])
        bufs.stream_two[here, :] = stream
        bufs.held_ffn[here, :] = normed(stream, 2)
    start(("held",), bufs.held_ffn, held_other, "tp", other_core())
    flush(bufs.stream_two, outs.stream_two)
    flush(bufs.held_ffn, outs.held_ffn)
    for k in range(at.z_count):
        gather.finish(k)
    wait("cot", at.rows)
    start(("cot_core",), cot, cot_other, "tp", other_core())
    flush(cot, cot_out)
    copies[("held",)].wait()
    flush(held_other, held_other_out)
    copies[("cot_core",)].wait()
    flush(cot_other, cot_other_out)
    for copy in flushes:
        copy.wait()


def forward(at, inputs, memory, cotangent, segs, piece, weights, gains, table, last_parts):
    seq, features = inputs.shape[1:]
    mem_seq = memory.shape[1]
    tokens, mem_tokens = at.rows * seq, at.rows * mem_seq
    key_width = GROUPS * HEAD_DIM
    of = jax.ShapeDtypeStruct
    wide = of((tokens, features), bf16)
    log = of((GROUPS, at.rows, 2 * BLOCK), f32)
    kv, mem_kv = of((tokens, 2 * key_width), bf16), of((mem_tokens, 2 * key_width), bf16)
    shapes = Kept(
        x=wide,
        held_self=wide,
        queries=wide,
        kv=kv,
        self_context=wide,
        self_log=log,
        stream_one=of((tokens, features), f32),
        held_cross=wide,
        cross_queries=wide,
        mem=of((mem_tokens, features), bf16),
        mem_kv=mem_kv,
        cross_context=wide,
        cross_log=log,
        stream_two=of((tokens, features), f32),
        held_ffn=wide,
        tiles=of((GROUPS, len(near_kinds(at.share)), BLOCK, 2 * BLOCK), f32),
        seg_row=of((1, tokens), jnp.int32),
    )
    buffered = list(shapes)
    buffered += [of((tokens, 2 * HEAD_DIM), bf16)] * at.share
    buffered += [of((mem_tokens, 2 * HEAD_DIM), bf16)] * at.share
    buffered += [kv] * (at.share - 1) + [mem_kv] * (at.share - 1)
    gathered = of((at.z_count, at.dp, *piece.shape), bf16)
    length = max(tokens, mem_tokens) * at.share
    messages = len(forward_messages(at))
    results = pl.pallas_call(
        functools.partial(forward_kernel, at, shapes),
        out_shape=buffered + [wide, wide, wide, gathered],
        in_specs=[any_space()] * 4
        + [whole_vmem()]
        + [any_space()] * 8
        + [whole_vmem(), whole_smem(), whole_smem()],
        out_specs=[any_space()] * (len(buffered) + 4),
        scratch_shapes=[pltpu.VMEM(shape.shape, shape.dtype) for shape in buffered]
        + [pltpu.VMEM(weight.shape, bf16) for weight in weights]
        + [pltpu.VMEM((tokens, features), bf16)] * 3
        + [
            pltpu.VMEM(gathered.shape, bf16),
            pltpu.VMEM((at.rows, 8, BLOCK), jnp.int32),
            pltpu.VMEM((at.share - 1, at.rows, 8, BLOCK), jnp.int32),
            pltpu.VMEM((length, 2 * HEAD_DIM), bf16),
            pltpu.VMEM((2 * HEAD_DIM, length), bf16),
            pltpu.VMEM((length, 2 * BLOCK), f32),
            pltpu.VMEM((length, 2 * BLOCK), bf16),
            pltpu.SemaphoreType.DMA((messages,)),
            pltpu.SemaphoreType.DMA((messages,)),
            pltpu.SemaphoreType.DMA((12,)),
            pltpu.SemaphoreType.DMA((len(buffered) + 3 + at.z_count * at.dp,)),
        ],
        compiler_params=params(60, collective_id=2, has_side_effects=True),
        cost_estimate=pl.CostEstimate(
            flops=40 * tokens * features * features,
            bytes_accessed=60 * MIB,
            transcendentals=0,
        ),
        name="forward",
    )(inputs, memory, cotangent, segs, piece, *weights, gains, table, last_parts)
    results = list(results)
    take = lambda n: [results.pop(0) for _ in range(n)]
    kept = Kept(*take(len(Kept._fields)))
    self_features, mem_features = take(at.share), take(at.share)
    kvs = [kept.kv, *take(at.share - 1)]
    mem_kvs = [kept.mem_kv, *take(at.share - 1)]
    cot, cot_other, held_other, gathered = results
    return types.SimpleNamespace(
        **kept._asdict(),
        self_features=self_features,
        mem_features=mem_features,
        kvs=kvs,
        mem_kvs=mem_kvs,
        cot=cot,
        cot_other=cot_other,
        held_other=held_other,
        gathered=gathered,
    )


def gelu_parts(v):
    slope = math.sqrt(2 / math.pi)
    square = v * v
    t = jnp.tanh(slope * v * (1.0 + 0.044715 * square))
    half = 0.5 * (1.0 + t)
    derivative = half + 0.5 * v * (1.0 - t * t) * slope * (1.0 + 3 * 0.044715 * square)
    return v * half, derivative


def ffn_parts(rows):
    first = (rows // 2 + 15) // 16 * 16
    return (0, first), (first, rows - first)


def ffn_kernel(at, span, later, *refs):
    held_refs, cot_refs = refs[0:2], refs[2:4]
    gathered = refs[4]
    sums, earlier, refs = (refs[5:9], refs[9], refs[10:]) if later else (None, None, refs[5:])
    if later:
        beside = FirstStep(at, earlier, refs[3], refs[-FirstStep.BUFFERS :])
        landings, *swap_sems = refs[-FirstStep.BUFFERS - 3 : -FirstStep.BUFFERS]
        refs = (*refs[:2], None, None, refs[2], *refs[4 : -FirstStep.BUFFERS - 3])
        greet(at)
        beside.start()
    out_refs = refs[0:4]
    grad_ref = refs[4]
    weights, acts, held, cot, out_stage, back_stage = refs[5:11]
    in_sems, w_sems, out_sems = refs[11:]
    d = lax.axis_index("dp")
    z = lax.axis_index("tp") // 2
    tokens = held_refs[0].shape[0]
    first_row, rows = span
    width = gathered.shape[4]

    def columns(s):
        return pl.ds(pl.multiple_of(xor_static(d, s, at.dp) * width, width), width)

    loads = []
    for which, (sources, target) in enumerate(((held_refs, held), (cot_refs, cot))):
        for half in range(2):
            for s in range(at.dp):
                loads.append(
                    pltpu.make_async_copy(
                        sources[half].at[:, columns(s)],
                        target.at[pl.ds(half * tokens, tokens), pl.ds(s * width, width)],
                        in_sems.at[(which * 2 + half) * at.dp + s],
                    )
                )
    stages = (out_stage, back_stage)
    if later:
        for which, target in enumerate(stages):
            for half in range(2):
                for s in range(at.dp):
                    loads.append(
                        pltpu.make_async_copy(
                            sums[which * 2 + half].at[:, columns(s)],
                            target.at[pl.ds(half * tokens, tokens), pl.ds(s * width, width)],
                            out_sems.at[(which * 2 + half) * at.dp + s],
                        )
                    )
    for k in range(at.z_count):
        for s in range(at.dp):
            number = k * at.dp + s
            loads.append(
                pltpu.make_async_copy(
                    gathered.at[k, s, :, pl.ds(first_row, rows), :],
                    weights.at[
                        :,
                        pl.ds(pl.multiple_of((z + at.z_count - k) % at.z_count * rows, rows), rows),
                        pl.ds(s * width, width),
                    ],
                    w_sems.at[number],
                )
            )
    for copy in loads:
        copy.start()
    for copy in loads:
        copy.wait()

    tile = 256

    def keep(stage, here, value):
        if later:
            value = value + stage[here, :].astype(f32)
        stage[here, :] = value.astype(bf16)

    def step(index, carry):
        here = pl.ds(pl.multiple_of(index * tile, tile), tile)
        held_tile, cot_tile = held[here, :], cot[here, :]
        gate = nt(held_tile, weights[0])
        up = nt(held_tile, weights[1])
        grad_hidden = nt(cot_tile, weights[2])
        active, slope = gelu_parts(gate)
        hidden = (active * up).astype(bf16)
        acts[2, here, :] = hidden
        keep(out_stage, here, nn(hidden, weights[2]))
        grad_gate = (grad_hidden * up * slope).astype(bf16)
        grad_up = (grad_hidden * active).astype(bf16)
        acts[0, here, :] = grad_gate
        acts[1, here, :] = grad_up
        keep(back_stage, here, nn(grad_gate, weights[0]) + nn(grad_up, weights[1]))
        return carry

    lax.fori_loop(0, 2 * tokens // tile, step, 0)

    swaps = []
    if later:
        for which, stage in enumerate(stages):
            swaps.append(
                remote(
                    stage.at[pl.ds(tokens, tokens), :],
                    landings.at[which],
                    swap_sems,
                    which,
                    "tp",
                    other_core(),
                )
            )
            swaps[which].start()

    stores = []
    for which, stage in enumerate(stages):
        for half in range(1 if later else 2):
            for s in range(at.dp):
                stores.append(
                    pltpu.make_async_copy(
                        stage.at[pl.ds(half * tokens, tokens), pl.ds(s * width, width)],
                        out_refs[which if later else which * 2 + half].at[:, columns(s)],
                        out_sems.at[(which * 2 + half) * at.dp + s],
                    )
                )
    if not later:
        for copy in stores:
            copy.start()

    hidden_rows = rows * at.z_count
    for start in range(0, hidden_rows, BLOCK):
        size = min(BLOCK, hidden_rows - start)
        for m in range(3):
            right = cot if m == 2 else held
            grad = tn(acts[m, :, start : start + size], right[...]).astype(bf16)
            first = start
            while first < start + size:
                chunk, inside = divmod(first, rows)
                last = min(start + size, (chunk + 1) * rows)
                for s in range(at.dp):
                    grad_ref[
                        xor_static(d, s, at.dp), chunk, m, inside : inside + last - first, :
                    ] = grad[first - start : last - start, s * width : (s + 1) * width]
                first = last
    if later:
        for which, stage in enumerate(stages):
            swaps[which].wait()
            for first in range(0, tokens, tile):
                here = pl.ds(first, tile)
                stage[here, :] = (
                    stage[here, :].astype(f32) + landings[which, here, :].astype(f32)
                ).astype(bf16)
        for copy in stores:
            copy.start()
    for copy in stores:
        copy.wait()
    if later:
        beside.end()


def ffn(at, span, held_own, held_other, cot_own, cot_other, gathered, sums=(), earlier=None):
    tokens, features = held_own.shape
    rows, width = span[1], gathered.shape[4]
    hidden = rows * at.z_count
    grad_shape = jax.ShapeDtypeStruct((at.dp, at.z_count, 3, rows, width), bf16)
    token_shape = jax.ShapeDtypeStruct((tokens, features), bf16)
    extra, extra_shape, extra_scratch, extra_params, results = [], [], [], {}, 4
    if sums:
        results = 2
        half_shape = half_shape_of(at, earlier)
        extra = [*sums, earlier]
        extra_shape = [jax.ShapeDtypeStruct(half_shape, bf16)]
        extra_scratch = [
            pltpu.VMEM((2, tokens, features), bf16),
            pltpu.SemaphoreType.DMA((2,)),
            pltpu.SemaphoreType.DMA((2,)),
            *first_step_scratch(at, half_shape),
        ]
        extra_params = dict(collective_id=5, has_side_effects=True)
    return pl.pallas_call(
        functools.partial(ffn_kernel, at, span, bool(sums)),
        out_shape=[token_shape] * results + [grad_shape] + extra_shape,
        in_specs=[any_space()] * (5 + len(extra)),
        out_specs=[any_space()] * results + [whole_vmem()] * (1 + len(extra_shape)),
        scratch_shapes=[
            pltpu.VMEM((3, hidden, features), bf16),
            pltpu.VMEM((3, 2 * tokens, hidden), bf16),
            pltpu.VMEM((2 * tokens, features), bf16),
            pltpu.VMEM((2 * tokens, features), bf16),
            pltpu.VMEM((2 * tokens, features), bf16),
            pltpu.VMEM((2 * tokens, features), bf16),
            pltpu.SemaphoreType.DMA((4 * at.dp,)),
            pltpu.SemaphoreType.DMA((at.z_count * at.dp,)),
            pltpu.SemaphoreType.DMA((4 * at.dp,)),
            *extra_scratch,
        ],
        compiler_params=params(58, **extra_params),
        cost_estimate=pl.CostEstimate(
            flops=18 * 2 * tokens * features * hidden,
            bytes_accessed=40 * MIB,
            transcendentals=2 * tokens * hidden,
        ),
        name="ffn",
    )(held_own, held_other, cot_own, cot_other, gathered, *extra)


def weight_grad_kernel(at, widths, *refs):
    n = len(widths)
    lefts, rights, outs = refs[:n], refs[n : 2 * n], refs[2 * n :]
    d = lax.axis_index("dp")
    core = lax.axis_index("tp") % 2
    rows = lefts[0].shape[1] // at.dp
    quarter = sum(widths) // 4
    offset = 0
    for left, right, total in zip(lefts, rights, widths):
        width = total // 2
        block = jnp.concatenate(
            [
                right[:, pl.ds(pl.multiple_of(half * width, width), width)]
                for half in (core, 1 - core)
            ],
            axis=1,
        )
        for s in range(at.dp):
            chosen = pl.ds(pl.multiple_of(xor_static(d, s, at.dp) * rows, rows), rows)
            grad = tn(left[:, chosen], block).astype(bf16)
            done = 0
            while done < width:
                part, inside = divmod(offset + done, quarter)
                taken = min(width - done, quarter - inside)
                place = half_order(at.dp, part == 0)[0].index(s)
                for sent in range(2):
                    first = sent * width + done
                    outs[part * 2 + sent][place, :, inside : inside + taken] = grad[
                        :, first : first + taken
                    ]
                done += taken
        offset += width


def weight_products(at, pairs):
    lefts = [left for left, _ in pairs]
    rights = [right for _, right in pairs]
    widths = [right.shape[1] for right in rights]
    features = lefts[0].shape[1]
    quarter = sum(widths) // 4
    shape = jax.ShapeDtypeStruct((at.dp, features // at.dp, quarter), bf16)
    return pl.pallas_call(
        functools.partial(weight_grad_kernel, at, widths),
        out_shape=[shape] * 4,
        in_specs=[whole_vmem()] * (2 * len(pairs)),
        out_specs=[whole_vmem()] * 4,
        compiler_params=params(48),
        cost_estimate=pl.CostEstimate(
            flops=2 * lefts[0].shape[0] * features * sum(widths),
            bytes_accessed=16 * MIB,
            transcendentals=0,
        ),
        name="weight_grads",
    )(*lefts, *rights)


def z_slots(at, bit):
    sent = [r for r in range(at.z_count) if r >> bit & 1 and r % (1 << bit) == 0]
    base = at.z_count - (at.z_count >> bit)
    return [(r, base + number) for number, r in enumerate(sent)]


class RowReturn:
    BUFFERS = 4

    def __init__(self, at, source, target, buffers):
        self.at, self.source, self.target = at, source, target
        self.landing, *sems, self.own_sem = buffers
        self.sems = tuple(sems)
        self.row, self.part = at.row(), at.part()

    @staticmethod
    def scratch(at, array):
        return [
            pltpu.VMEM(array.shape, array.dtype),
            pltpu.SemaphoreType.DMA((at.rows - 1,)),
            pltpu.SemaphoreType.DMA((at.rows - 1,)),
            pltpu.SemaphoreType.DMA((1,)),
        ]

    def copies(self):
        own = pltpu.make_async_copy(
            self.source.at[self.row], self.landing.at[self.row], self.own_sem.at[0]
        )
        made = [own]
        for k in range(1, self.at.rows):
            there = xor_static(self.row, k, self.at.rows)
            made.append(
                remote(
                    self.source.at[there],
                    self.landing.at[self.row],
                    self.sems,
                    k - 1,
                    "tp",
                    there * self.at.share + self.part,
                )
            )
        return made

    def start(self):
        for copy in self.copies():
            copy.start()

    def end(self):
        for copy in self.copies():
            copy.wait()
        for r in range(self.at.rows):
            self.target[r] = self.landing[r]


class Reduction:
    def __init__(self, at, first_low, buffers):
        self.at = at
        self.first, self.halves, self.z_in, self.done, self.last_in, *self.sems = buffers
        self.base = self.first
        _, self.bits = half_order(at.dp, first_low)
        self.z = lax.axis_index("tp") // 2
        self.core = lax.axis_index("tp") % 2
        self.rows = self.first.shape[1] // at.z_count
        self.copies = {}

    @staticmethod
    def scratch(at, rows, columns):
        n = at.dp // 2
        messages = 1 + bits_of(at.dp) + at.z_count
        return [
            pltpu.VMEM((at.dp, rows, columns), bf16),
            pltpu.VMEM((max(2 * n - 1, 1), rows, columns), bf16),
            pltpu.VMEM((at.z_count - 1, rows // at.z_count, columns), bf16),
            pltpu.VMEM((rows // at.z_count, columns), f32),
            pltpu.VMEM((rows // at.z_count // 2, columns), f32),
            pltpu.SemaphoreType.DMA((messages,)),
            pltpu.SemaphoreType.DMA((messages,)),
        ]

    BUFFERS = 7

    def start(self, key, copy):
        self.copies[key] = copy
        copy.start()

    def start_core(self, source):
        self.start("core", remote(source, self.first, self.sems, 0, "tp", other_core()))

    def end_core(self, keep):
        self.copies["core"].wait()
        for s in range(self.at.dp):
            self.first[s] = self.first[s] + keep[s]

    def half_at(self, place):
        n = self.at.dp >> (place + 1)
        return n, self.at.dp - 2 * n

    def start_half(self, place):
        n, offset = self.half_at(place)
        d = lax.axis_index("dp")
        self.start(
            ("half", place),
            remote(
                self.base.at[pl.ds(n, n)],
                self.halves.at[pl.ds(offset, n)],
                self.sems,
                1 + place,
                "dp",
                xor_static(d, 1 << self.bits[place], self.at.dp),
            ),
        )

    def end_half(self, place):
        self.copies["half", place].wait()
        n, offset = self.half_at(place)
        for s in range(n):
            self.first[s] = self.first[s] + self.halves[offset + s]
        self.base = self.first

    def z_rows(self, r):
        z = xor_static(self.z, r, self.at.z_count)
        return pl.ds(pl.multiple_of(z * self.rows, self.rows), self.rows)

    def start_z(self, bit):
        base = 1 + len(self.bits)
        partner = tp_at(self.at, xor_static(self.z, 1 << bit, self.at.z_count))
        for r, slot in z_slots(self.at, bit):
            self.start(
                ("z", slot),
                remote(
                    self.first.at[0, self.z_rows(r), :],
                    self.z_in.at[slot],
                    self.sems,
                    base + slot,
                    "tp",
                    partner,
                ),
            )

    def end_z(self, bit):
        for r, slot in z_slots(self.at, bit):
            self.copies["z", slot].wait()
            rows = self.z_rows(r ^ 1 << bit)
            total = self.first[0, rows, :].astype(f32) + self.z_in[slot].astype(f32)
            if 2 << bit == self.at.z_count:
                self.done[...] = total
            else:
                self.first[0, rows, :] = total.astype(bf16)

    def part(self, core):
        rows = self.rows // 2
        return pl.ds(pl.multiple_of(core * rows, rows), rows)

    def start_last(self):
        number = len(self.bits) + self.at.z_count
        self.start(
            "last",
            remote(
                self.done.at[self.part(1 - self.core), :],
                self.last_in,
                self.sems,
                number,
                "tp",
                other_core(),
            ),
        )

    def end_last(self, out, columns):
        out[0, :, columns] = self.done[self.part(self.core), :]
        self.copies["last"].wait()
        out[1, :, columns] = self.last_in[...]


def relative_sums(at, kinds, diagonals, dfar):
    lane = lax.broadcasted_iota(jnp.int32, (1, BLOCK), 1)
    onehots = []
    for kind in kinds:
        offset = lax.broadcasted_iota(jnp.int32, (2 * BLOCK, BLOCK), 0) - (BLOCK - 1)
        distance = BLOCK * kind_distance(at, kind) + offset
        bucket = bucket_of(jnp.maximum(distance, 0))
        column = lax.broadcasted_iota(jnp.int32, (2 * BLOCK, BLOCK), 1)
        onehots.append(jnp.where(bucket == column, 1.0, 0.0).astype(bf16))
    results = []
    for group in range(GROUPS):
        sums = jnp.zeros((2, BLOCK), f32)
        for number, onehot in enumerate(onehots):
            rest = diagonals[group, 2 * number : 2 * number + 2, :]
            for _ in range(3):
                part = rest.astype(bf16)
                sums = sums + nn(part, onehot)
                rest = rest - part.astype(f32)
        for j in range(2):
            far = jnp.sum(dfar[group, :, j * BLOCK : (j + 1) * BLOCK], axis=0, keepdims=True)
            far = jnp.sum(far, axis=1, keepdims=True)
            results.append(sums[j : j + 1] + jnp.where(lane == BUCKETS - 1, far, 0.0))
    return results


class CoreStep:
    BUFFERS = 4

    def __init__(self, at, first_low, buffers):
        self.at = at
        self.first, self.landing, *self.sems = buffers
        self.bit = half_order(at.dp, first_low)[1][0]

    @staticmethod
    def scratch(at, rows, columns, halves):
        return [
            pltpu.VMEM((at.dp, rows, columns), bf16),
            pltpu.VMEM((at.dp // 2 if halves else 1, rows if halves else 16, columns), bf16),
            pltpu.SemaphoreType.DMA((2,)),
            pltpu.SemaphoreType.DMA((2,)),
        ]

    def start_core(self, source):
        self.core = remote(source, self.first, self.sems, 0, "tp", other_core())
        self.core.start()

    def end_core(self, keep):
        self.core.wait()
        for s in range(self.at.dp):
            self.first[s] = self.first[s] + keep[s]

    def start_half(self):
        n = self.at.dp // 2
        partner = xor_static(lax.axis_index("dp"), 1 << self.bit, self.at.dp)
        self.half = remote(
            self.first.at[pl.ds(n, n)], self.landing, self.sems, 1, "dp", partner
        )
        self.half.start()

    def end_half(self, out):
        self.half.wait()
        for s in range(self.at.dp // 2):
            out[s] = self.first[s] + self.landing[s]


class FfnSum:
    def __init__(self, at, source, out, take):
        self.at, self.source, self.out = at, source, out
        self.total = DpSum(at)
        (self.work,) = take(1)
        self.landings = [take(3) for _ in range(1, bits_of(at.dp))]
        self.z_in, *self.z_sems, self.load_sems = take(4)
        self.z_sems = tuple(self.z_sems)
        self.z = lax.axis_index("tp") // 2
        self.copies = {}

    @staticmethod
    def scratch(at, half_shape):
        inner = half_shape[2:]
        scratch = [pltpu.VMEM((2, at.dp // 4, *inner), bf16)]
        for step in range(1, bits_of(at.dp)):
            count = at.dp >> (step + 1)
            scratch += [
                pltpu.VMEM((2, count, *inner), bf16),
                pltpu.SemaphoreType.DMA((2 * count,)),
                pltpu.SemaphoreType.DMA((2 * count,)),
            ]
        return scratch + [
            pltpu.VMEM((at.z_count - 1, *inner[1:]), bf16),
            pltpu.SemaphoreType.DMA((at.z_count - 1,)),
            pltpu.SemaphoreType.DMA((at.z_count - 1,)),
            pltpu.SemaphoreType.DMA((2 * (at.dp // 4),)),
        ]

    def start(self):
        total = self.total
        self.loads = []
        for half in range(2):
            for slot, s in enumerate(total.held(half, 2)):
                place = total.held(half, 1).index(s)
                self.loads.append(
                    pltpu.make_async_copy(
                        self.source.at[half, place],
                        self.work.at[half, slot],
                        self.load_sems.at[half * total.count(2) + slot],
                    )
                )
        entry = lambda half, s: self.source.at[half, total.held(half, 1).index(s)]
        self.send(1, entry)
        for copy in self.loads:
            copy.start()

    def send(self, step, entry):
        landing, *sems = self.landings[step - 1]
        self.dp_copies = self.total.copies(step, entry, landing, tuple(sems))
        for copy in self.dp_copies:
            copy.start()

    def to_z(self):
        total = self.total
        for copy in self.loads:
            copy.wait()
        for step in range(1, bits_of(self.at.dp)):
            for copy in self.dp_copies:
                copy.wait()
            landing = self.landings[step - 1][0]
            for half in range(2):
                for slot, s in enumerate(total.held(half, step + 1)):
                    place = total.held(half, 2).index(s)
                    for chunk in range(self.at.z_count // 2):
                        for m in range(3):
                            self.work[half, place, chunk, m] = (
                                self.work[half, place, chunk, m] + landing[half, slot, chunk, m]
                            )
            if step + 1 < bits_of(self.at.dp):
                self.send(
                    step + 1,
                    lambda half, s: self.work.at[half, total.held(half, 2).index(s)],
                )
        self.start_z(0)

    def chunk(self, r):
        z = xor_static(self.z, r, self.at.z_count)
        half_z = self.at.z_count // 2
        return self.work.at[z // half_z, 0, z % half_z]

    def start_z(self, bit):
        partner = tp_at(self.at, xor_static(self.z, 1 << bit, self.at.z_count))
        for r, slot in z_slots(self.at, bit):
            self.copies[slot] = remote(
                self.chunk(r), self.z_in.at[slot], self.z_sems, slot, "tp", partner
            )
            self.copies[slot].start()

    def end_z(self, bit):
        for r, slot in z_slots(self.at, bit):
            self.copies[slot].wait()
            kept = self.chunk(r ^ 1 << bit)
            for m in range(3):
                total = kept[m].astype(f32) + self.z_in[slot, m].astype(f32)
                if 2 << bit == self.at.z_count:
                    self.out[m] = total
                else:
                    kept[m] = total.astype(bf16)


def self_backward_kernel(at, *refs):
    refs = list(refs)
    take = lambda n: [refs.pop(0) for _ in range(n)]
    held, queries, seg_ref, logsum, grad_context, tiles, last_parts = take(7)
    kv_refs, feat_refs = take(at.share), take(at.share)
    gain, wq, wk, wv = take(4)
    late_sources = take(4)
    send_low, send_high = take(2)
    *ffn_ins, memory_in = take(3)
    flushed = take(5)
    gain_out, relative_out, *ffn_outs, memory_out = take(5)
    keep_low, keep_high, x_ref, grad_ref = late_targets = take(4)
    middle_outs, last_outs, (rows_out,) = buffers = take(2), take(2), take(1)
    late_sems, flush_sems = take(2)
    late_loads = [
        pltpu.make_async_copy(source, target, late_sems.at[number])
        for number, (source, target) in enumerate(zip(late_sources, late_targets))
    ]
    flushes = [
        pltpu.make_async_copy(source, target, flush_sems.at[number])
        for number, (source, target) in enumerate(zip(sum(buffers, []), flushed))
    ]
    middle = [CoreStep(at, half == 0, take(CoreStep.BUFFERS)) for half in range(2)]
    last = [CoreStep(at, half == 0, take(CoreStep.BUFFERS)) for half in range(2)]
    ffn_sums = [FfnSum(at, *pair, take) for pair in zip(ffn_ins, ffn_outs)]
    memory_return = RowReturn(at, memory_in, memory_out, take(RowReturn.BUFFERS))
    z_bits = range(bits_of(at.z_count))
    product_send, kv_in, dq, diagonals, dfar = take(5)
    own_kv, *other_kv = take(at.share)
    weight_sems, = take(1)
    kv_sems = take(2)
    d = lax.axis_index("dp")
    core = lax.axis_index("tp") % 2
    row, part = at.row(), at.part()
    features = held.shape[1]
    rows = features // at.dp
    kinds = near_kinds(at.share)
    keys = Keys(at.share, at.rows, True)
    lanes_at = lambda start, width: pl.ds(pl.multiple_of(start, BLOCK), width)

    def one_pair(scratch, pair, carry):
        four = lanes_at(pair * 2 * BLOCK, 2 * BLOCK)
        two = lanes_at(pair * BLOCK, BLOCK)
        values = lanes_at(GROUPS * HEAD_DIM + pair * BLOCK, BLOCK)
        both = pl.ds(pair * 2, 2)
        backward_body(
            keys,
            kinds,
            pair,
            queries.at[:, four],
            seg_ref,
            [ref.at[:, two] for ref in kv_refs],
            [ref.at[:, values] for ref in kv_refs],
            feat_refs,
            tiles.at[both],
            last_parts,
            logsum.at[both],
            grad_context.at[:, four],
            dq.at[:, four],
            [ref.at[:, :, two] for ref in (own_kv, *other_kv)],
            diagonals.at[both],
            dfar.at[both],
            scratch,
        )
        return carry

    def products(number, right, offset):
        width = right.shape[1] // 2
        order, _ = half_order(at.dp, number == 0)
        block = jnp.concatenate(
            [
                right[:, pl.ds(pl.multiple_of(half * width, width), width)]
                for half in (core, 1 - core)
            ],
            axis=1,
        )
        for place, s in enumerate(order):
            chosen = pl.ds(pl.multiple_of(xor_static(d, s, at.dp) * rows, rows), rows)
            both = tn(held[:, chosen], block).astype(bf16)
            last_outs[number][place, :, offset : offset + width] = both[:, :width]
            product_send[number, place, :, offset : offset + width] = both[:, width:]

    greet(at)
    for ffn_sum in ffn_sums:
        ffn_sum.start()
    middle[0].start_core(send_low)
    middle[1].start_core(send_high)
    memory_return.start()
    for copy in late_loads:
        copy.start()

    def attention(first, last):
        def pairs(*scratch):
            lax.fori_loop(first, last, functools.partial(one_pair, scratch), 0)

        pl.run_scoped(
            pairs,
            *backward_scratch(keys.count * BLOCK),
            pltpu.VMEM((len(kinds), BLOCK, 2 * BLOCK), f32),
        )

    attention(0, 2)
    ffn_sums[0].to_z()
    for copy in late_loads:
        copy.wait()
    for number, keep in enumerate((keep_low, keep_high)):
        middle[number].end_core(keep)
        middle[number].start_half()
    attention(2, PAIRS)
    ffn_sums[1].to_z()
    for bit in z_bits[1:]:
        ffn_sums[0].end_z(bit - 1)
        ffn_sums[0].start_z(bit)
    kv_copies = []
    for s in range(1, at.share):
        kv_copies.append(
            remote(
                other_kv[s - 1],
                kv_in.at[s - 1],
                kv_sems,
                s - 1,
                "tp",
                row * at.share + (part + s) % at.share,
            )
        )
    for copy in kv_copies:
        copy.start()
    products(0, dq, 0)
    last[0].start_core(product_send.at[0])
    for copy in kv_copies:
        copy.wait()
    for which in range(2):
        total = own_kv[which].astype(f32)
        for s in range(1, at.share):
            total = total + kv_in[s - 1, which].astype(f32)
        own_kv[which] = total.astype(bf16)
    for which in range(2):
        products(1, own_kv.at[which], which * (own_kv.shape[2] // 2))
    last[1].start_core(product_send.at[1])
    for bit in z_bits[1:]:
        ffn_sums[1].end_z(bit - 1)
        ffn_sums[1].start_z(bit)

    seq = rows_out.shape[1]

    def input_gradient(*weights):
        loads = [
            pltpu.make_async_copy(source, target, weight_sems.at[number])
            for number, (source, target) in enumerate(zip((wq, wk, wv), weights))
        ]
        for copy in loads:
            copy.start()
        for copy in loads:
            copy.wait()
        gain_sum = jnp.zeros((1, features), f32)
        gain_row = gain[...]
        for i in range(at.rows):
            here = pl.ds(i * seq, seq)
            dy = nt(dq[here, :], weights[0][...])
            dy = dy + nt(own_kv[0, here, :], weights[1][...])
            dy = dy + nt(own_kv[1, here, :], weights[2][...])
            grad, gain_part = norm_back(x_ref[here, :].astype(f32), gain_row, dy)
            gain_sum = gain_sum + gain_part
            rows_out[i] = (grad_ref[here, :] + grad).astype(bf16)
        gain_out[...] = gain_sum

    pl.run_scoped(input_gradient, *[pltpu.VMEM(w.shape, bf16) for w in (wq, wk, wv)])
    flushes[4].start()
    relative_out[...] = jnp.zeros(relative_out.shape, f32)
    for head, sums in enumerate(relative_sums(at, kinds, diagonals, dfar)):
        lane = head // 4 * BLOCK
        relative_out[head % 4 : head % 4 + 1, lane : lane + BLOCK] = sums
    for number in range(2):
        last[number].end_core(last_outs[number])
        for s in range(at.dp):
            last_outs[number][s] = last[number].first[s]
        flushes[2 + number].start()
    for number in range(2):
        middle[number].end_half(middle_outs[number])
        flushes[number].start()
    for ffn_sum in ffn_sums:
        ffn_sum.end_z(z_bits[-1])
    memory_return.end()
    for copy in flushes:
        copy.wait()


def self_backward(
    at,
    held,
    queries,
    kvs,
    features_of,
    seg_row,
    logsum,
    grad_context,
    tiles,
    last_parts,
    x_low,
    grad_one,
    gain,
    weights,
    middle,
    ffn_parts_now,
    memory_grad,
):
    keep_low, send_low, keep_high, send_high = middle
    tokens, features = held.shape
    _, rows, middle_columns = keep_low.shape
    key_width = kvs[0].shape[1] // 2
    last_columns = features // 2
    kinds = len(near_kinds(at.share))
    of = jax.ShapeDtypeStruct
    flushed = [of((at.dp // 2, rows, middle_columns), bf16)] * 2
    flushed += [of((at.dp, rows, last_columns), bf16)] * 2
    flushed += [of((at.rows, tokens // at.rows, features), bf16)]
    late = [keep_low, keep_high, x_low, grad_one]
    scratch = [pltpu.VMEM(array.shape, array.dtype) for array in late + flushed]
    scratch += [pltpu.SemaphoreType.DMA((len(late),)), pltpu.SemaphoreType.DMA((len(flushed),))]
    for columns, halves in ((middle_columns, True), (last_columns, False)):
        scratch += CoreStep.scratch(at, rows, columns, halves) * 2
    for part in ffn_parts_now:
        scratch += FfnSum.scratch(at, part.shape)
    scratch += RowReturn.scratch(at, memory_grad)
    scratch += [
        pltpu.VMEM((2, at.dp, rows, last_columns), bf16),
        pltpu.VMEM((at.share - 1, 2, tokens, key_width), bf16),
        pltpu.VMEM((tokens, features), bf16),
        pltpu.VMEM((GROUPS, 2 * kinds, 2 * BLOCK), f32),
        pltpu.VMEM((GROUPS, 8, 2 * BLOCK), f32),
        *[pltpu.VMEM((2, tokens, key_width), bf16)] * at.share,
        pltpu.SemaphoreType.DMA((3,)),
        pltpu.SemaphoreType.DMA((at.share - 1,)),
        pltpu.SemaphoreType.DMA((at.share - 1,)),
    ]
    return pl.pallas_call(
        functools.partial(self_backward_kernel, at),
        out_shape=flushed
        + [
            of((1, features), f32),
            of((4, features), f32),
            *[of(part.shape[3:], f32) for part in ffn_parts_now],
            of(memory_grad.shape, bf16),
        ],
        in_specs=[whole_vmem()] * 6
        + [whole_smem()]
        + [whole_vmem()] * (2 * at.share + 1)
        + [any_space()] * 12,
        out_specs=[any_space()] * len(flushed) + [whole_vmem()] * 5,
        scratch_shapes=scratch,
        compiler_params=params(62, collective_id=3, has_side_effects=True),
        cost_estimate=pl.CostEstimate(
            flops=20 * tokens * features * features,
            bytes_accessed=100 * MIB,
            transcendentals=0,
        ),
        name="self_backward",
    )(
        held,
        queries,
        seg_row,
        logsum,
        grad_context,
        tiles,
        last_parts,
        *kvs,
        *features_of,
        gain,
        *weights,
        *late,
        send_low,
        send_high,
        *ffn_parts_now,
        memory_grad,
    )


def tail_kernel(at, *refs):
    refs = list(refs)
    take = lambda n: [refs.pop(0) for _ in range(n)]
    middle_in, last_in = take(2), take(2)
    grad_rows, small_in = take(2)
    input_out, small_out, middle_out, last_out = take(4)
    middle = [
        Reduction(at, True, take(Reduction.BUFFERS)),
        Reduction(at, False, take(Reduction.BUFFERS)),
    ]
    last = [
        Reduction(at, True, take(Reduction.BUFFERS)),
        Reduction(at, False, take(Reduction.BUFFERS)),
    ]
    input_return = RowReturn(at, grad_rows, input_out, take(RowReturn.BUFFERS))
    small, small_ins = take(2)
    small_sems = take(2)
    (load_sems,) = take(1)
    d = lax.axis_index("dp")
    t = lax.axis_index("tp")
    z = t // 2
    bits = list(range(bits_of(at.dp)))
    z_bits = range(bits_of(at.z_count))

    loads = []
    for number, (source, reduction) in enumerate(zip(middle_in + last_in, middle + last)):
        reduction.base = source
        n = at.dp >> (2 if number < 2 else 1)
        loads.append(
            pltpu.make_async_copy(
                source.at[pl.ds(0, n)], reduction.first.at[pl.ds(0, n)], load_sems.at[number]
            )
        )
        loads[-1].start()
    greet(at)
    for reduction in middle:
        reduction.start_half(1)
    for reduction in last:
        reduction.start_half(0)
    input_return.start()
    for copy in loads:
        copy.wait()

    small[0:8, :] = small_in[...]
    steps = [("tp", other_core())]
    steps += [("dp", xor_static(d, 1 << bit, at.dp)) for bit in bits]
    small_copies = []

    def start_small(number):
        axis, index = steps[number]
        copy = remote(
            small.at[pl.ds(8 * number, 8)], small_ins.at[number], small_sems, number, axis, index
        )
        small_copies.append(copy)
        copy.start()

    def end_small(number):
        small_copies[number].wait()
        small[8 * number + 8 : 8 * number + 16, :] = (
            small[8 * number : 8 * number + 8, :] + small_ins[number]
        )

    start_small(0)
    end_small(0)
    start_small(1)
    for place in bits[1:]:
        for reduction in middle:
            reduction.end_half(place)
            if place + 1 < len(bits):
                reduction.start_half(place + 1)
            else:
                reduction.start_z(0)
        for reduction in last:
            reduction.end_half(place - 1)
            reduction.start_half(place)
        end_small(place)
        start_small(place + 1)
    for reduction in last:
        reduction.end_half(len(bits) - 1)
        reduction.start_z(0)
    final = len(steps)
    end_small(final - 1)
    z_copies = []
    for k in range(1, at.z_count):
        z_copies.append(
            remote(
                small.at[pl.ds(8 * final, 8)],
                small_ins.at[final + k - 1],
                small_sems,
                final + k - 1,
                "tp",
                tp_at(at, (z + k) % at.z_count),
            )
        )
    for copy in z_copies:
        copy.start()
    for bit in z_bits[1:]:
        for reduction in middle + last:
            reduction.end_z(bit - 1)
            reduction.start_z(bit)
    input_return.end()
    total = small[8 * final : 8 * final + 8, :]
    for k, copy in enumerate(z_copies):
        copy.wait()
        total = total + small_ins[final + k]
    small_out[...] = total
    for reduction in middle + last:
        reduction.end_z(z_bits[-1])
        reduction.start_last()
    for reductions, out in ((middle, middle_out), (last, last_out)):
        columns = out.shape[2] // 2
        for number, reduction in enumerate(reductions):
            reduction.end_last(out, slice(number * columns, (number + 1) * columns))


def tail(at, grad_rows, middle, last, small):
    _, rows, middle_columns = middle[0].shape
    last_columns = last[0].shape[2]
    share_rows = rows // at.z_count // 2
    steps = 1 + bits_of(at.dp)
    out_shape = [
        jax.ShapeDtypeStruct(grad_rows.shape, bf16),
        jax.ShapeDtypeStruct(small.shape, f32),
        jax.ShapeDtypeStruct((2, share_rows, 2 * middle_columns), f32),
        jax.ShapeDtypeStruct((2, share_rows, 2 * last_columns), f32),
    ]
    scratch = []
    for columns in (middle_columns, middle_columns, last_columns, last_columns):
        scratch += Reduction.scratch(at, rows, columns)
    scratch += RowReturn.scratch(at, grad_rows)
    dma = lambda n: [pltpu.SemaphoreType.DMA((n,))] * 2
    scratch += [
        pltpu.VMEM((8 * (steps + 1), small.shape[1]), f32),
        pltpu.VMEM((steps + at.z_count - 1, *small.shape), f32),
        *dma(steps + at.z_count - 1),
        pltpu.SemaphoreType.DMA((4,)),
    ]
    return pl.pallas_call(
        functools.partial(tail_kernel, at),
        out_shape=out_shape,
        in_specs=[any_space()] * 5 + [whole_vmem()],
        out_specs=[whole_vmem()] * 4,
        scratch_shapes=scratch,
        compiler_params=params(48, collective_id=1, has_side_effects=True),
        cost_estimate=pl.CostEstimate(
            flops=MIB, bytes_accessed=200 * MIB, transcendentals=0
        ),
        name="tail",
    )(*middle, *last, grad_rows, small)


def finish_kernel(widths, *refs):
    refs = list(refs)
    take = lambda n: [refs.pop(0) for _ in range(n)]
    input_in, memory_in = take(2)
    pairs = take(len(widths))
    parts = take(2)
    input_out, memory_out = take(2)
    outs = [take(len(group)) for group in widths]
    gate_out, up_out, down_out = take(3)
    (turn,) = take(1)
    core = lax.axis_index("tp") % 2
    for source, target in ((input_in, input_out), (memory_in, memory_out)):
        for r in range(source.shape[0]):
            target[r] = source[r].astype(f32)
    for pair, group, targets in zip(pairs, widths, outs):
        offset = 0
        for width, target in zip(group, targets):
            half = width // 2
            for place in range(2):
                columns = pl.ds(pl.multiple_of((core + place) % 2 * half, half), half)
                target[:, columns] = pair[place, :, offset : offset + half]
            offset += half
    first, rows = parts[0].shape[1], down_out.shape[0]
    for m, target in enumerate((gate_out, up_out, down_out)):
        if m == 2:
            target[:first, :] = parts[0][m]
            target[first:, :] = parts[1][m]
        else:
            turn[:first, :] = parts[0][m]
            turn[first:rows, :] = parts[1][m]
            target[...] = turn[...].T[:, :rows]


def finish(input_rows, memory_rows, pairs, widths, parts):
    of = jax.ShapeDtypeStruct
    rows, columns = parts[0].shape[1] + parts[1].shape[1], parts[0].shape[2]
    out_shape = [of(input_rows.shape, f32), of(memory_rows.shape, f32)]
    for pair, group in zip(pairs, widths):
        out_shape += [of((pair.shape[1], width), f32) for width in group]
    out_shape += [of((columns, rows), f32)] * 2 + [of((rows, columns), f32)]
    return pl.pallas_call(
        functools.partial(finish_kernel, widths),
        out_shape=out_shape,
        in_specs=[whole_vmem()] * (4 + len(pairs)),
        out_specs=[whole_vmem()] * len(out_shape),
        scratch_shapes=[pltpu.VMEM((-(-rows // BLOCK) * BLOCK, columns), f32)],
        compiler_params=params(32),
        name="finish",
    )(input_rows, memory_rows, *pairs, *parts)


def on_device(
    inputs,
    memory,
    segments,
    memory_segments,
    gain_self,
    gain_cross,
    gain_ffn,
    relative_bias,
    self_query,
    self_key,
    self_value,
    self_out,
    cross_query,
    cross_key,
    cross_value,
    cross_out,
    ffn_gate,
    ffn_up,
    ffn_down,
    cotangent,
):
    rows, seq, features = inputs.shape
    mem_seq = memory.shape[1]
    at = Places(rows)
    tokens = rows * seq
    mem_tokens = rows * mem_seq
    key_width = GROUPS * HEAD_DIM
    width = features // at.dp
    d = lax.axis_index("dp")

    own_columns = lambda w: lax.dynamic_slice_in_dim(w, d * width, width, 1)
    own_rows = lambda w: lax.dynamic_slice_in_dim(w, d * width, width, 0).T
    own_piece = jnp.stack([own_rows(ffn_gate), own_rows(ffn_up), own_columns(ffn_down)])
    segs = jnp.zeros((rows, 8, BLOCK), jnp.int32)
    segs = segs.at[:, 0, :].set(segments).at[:, 1, :mem_seq].set(memory_segments)

    last = relative_bias[BUCKETS - 1]
    high = lax.reduce_precision(last, 8, 7)
    mid = lax.reduce_precision(last - high, 8, 7)
    low = lax.reduce_precision(last - high - mid, 8, 7)
    last_parts = jnp.concatenate([high, mid, low])

    done = forward(
        at,
        inputs,
        memory,
        cotangent,
        segs,
        own_piece,
        [
            self_query,
            self_key,
            self_value,
            self_out,
            cross_query,
            cross_key,
            cross_value,
            cross_out,
        ],
        jnp.stack([gain_self, gain_cross, gain_ffn]),
        relative_bias.reshape(-1),
        last_parts,
    )
    x_low, held_self, queries, kvs = done.x, done.held_self, done.queries, done.kvs
    self_context, self_log, stream_one = done.self_context, done.self_log, done.stream_one
    held_cross, cross_queries, mem = done.held_cross, done.cross_queries, done.mem
    mem_kvs, cross_context, cross_log = done.mem_kvs, done.cross_context, done.cross_log
    stream_two, held_ffn, cot = done.stream_two, done.held_ffn, done.cot
    self_features, mem_features = done.self_features, done.mem_features
    seg_row, tiles = done.seg_row, done.tiles

    ffn_operands = (held_ffn, done.held_other, cot, done.cot_other, done.gathered)
    first_span, second_span = ffn_parts(done.gathered.shape[3])
    *ffn_sums, ffn_grads_first = ffn(at, first_span, *ffn_operands)
    ffn_out, ffn_back, ffn_grads_second, ffn_first = ffn(
        at, second_span, *ffn_operands, ffn_sums, ffn_grads_first
    )
    grad_stream, gain_ffn_part = norm_back(stream_two, gain_ffn, ffn_back.astype(f32))
    grad_two = cot.astype(f32) + grad_stream
    output = (stream_two + ffn_out.astype(f32)).astype(bf16)
    output = output.reshape(rows, seq, features)

    cross_branch = grad_two.astype(bf16)
    grad_cross_context = nt(cross_branch, cross_out).astype(bf16)
    grad_cross_queries, *grad_mem_kvs, ffn_second, output = cross_backward(
        at,
        cross_queries,
        mem_kvs,
        mem_features,
        seg_row,
        cross_log,
        grad_cross_context,
        ffn_grads_second,
        output,
    )

    def gathered_grads(parts):
        total = parts[0].astype(f32)
        for s in range(1, at.share):
            total = total + lax.ppermute(
                parts[s], "tp", at.part_perm(at.share - s)
            ).astype(f32)
        return total[0].astype(bf16), total[1].astype(bf16)

    grad_mem_keys, grad_mem_values = gathered_grads(grad_mem_kvs)
    grad_stream, gain_cross_part = norm_back(
        stream_one, gain_cross, nt(grad_cross_queries, cross_query)
    )
    grad_one = grad_two + grad_stream
    self_branch = grad_one.astype(bf16)
    grad_self_context = nt(self_branch, self_out).astype(bf16)
    memory_grad = (nt(grad_mem_keys, cross_key) + nt(grad_mem_values, cross_value)).astype(bf16)
    memory_grad = memory_grad.reshape(rows, mem_seq, features)
    middle_products = weight_products(
        at,
        [
            (cross_context, cross_branch),
            (held_cross, grad_cross_queries),
            (self_context, self_branch),
            (mem, grad_mem_keys),
            (mem, grad_mem_values),
        ],
    )
    grad_self_context, middle_products = lax.optimization_barrier(
        (grad_self_context, middle_products)
    )
    (
        *products,
        grad_rows,
        gain_self_part,
        relative_part,
        ffn_first,
        ffn_second,
        memory_rows,
    ) = self_backward(
        at,
        held_self,
        queries,
        kvs,
        self_features,
        seg_row,
        self_log,
        grad_self_context,
        tiles,
        last_parts,
        x_low,
        grad_one,
        gain_self.reshape(1, -1),
        (self_query, self_key, self_value),
        middle_products,
        (ffn_first, ffn_second),
        memory_grad,
    )
    small = jnp.concatenate(
        [gain_self_part, gain_cross_part, gain_ffn_part, jnp.zeros((1, features), f32), relative_part]
    )
    input_rows, small, middle_pair, last_pair = tail(
        at, grad_rows, products[:2], products[2:], small
    )
    wide, narrow = features, key_width
    (
        input_grad,
        memory_grad,
        cross_out_grad,
        cross_query_grad,
        self_out_grad,
        cross_key_grad,
        cross_value_grad,
        self_query_grad,
        self_key_grad,
        self_value_grad,
        ffn_gate_grad,
        ffn_up_grad,
        ffn_down_grad,
    ) = finish(
        input_rows,
        memory_rows,
        (middle_pair, last_pair),
        ((wide, wide, wide, narrow, narrow), (wide, narrow, narrow)),
        (ffn_first, ffn_second),
    )
    shards = at.dp * at.tp
    shard = lax.axis_index("dp") * at.tp + lax.axis_index("tp")
    share_of = lambda vector: lax.dynamic_slice_in_dim(
        vector, shard * (vector.size // shards), vector.size // shards
    )
    relative = small[4:8].reshape(4, -1, BLOCK)[:, : HEADS // 4, :BUCKETS]
    return (
        output,
        input_grad,
        memory_grad,
        share_of(small[0]),
        share_of(small[1]),
        share_of(small[2]),
        share_of(relative.transpose(2, 1, 0).reshape(-1)),
        self_query_grad,
        self_key_grad,
        self_value_grad,
        self_out_grad,
        cross_query_grad,
        cross_key_grad,
        cross_value_grad,
        cross_out_grad,
        ffn_gate_grad,
        ffn_up_grad,
        ffn_down_grad,
    )


def solution(mesh):
    placed = (
        P("dp", "tp", None),
        P("dp", "tp", None),
        P("dp", "tp"),
        P("dp", "tp"),
        P(),
        P(),
        P(),
        P(),
        P(),
        P(),
        P(),
        P(),
        P(),
        P(),
        P(),
        P(),
        P(None, "tp"),
        P(None, "tp"),
        P("tp", None),
        P("dp", "tp", None),
    )
    return jax.shard_map(
        on_device,
        mesh=mesh,
        in_specs=placed,
        out_specs=(
            P("dp", "tp", None),
            P("dp", "tp", None),
            P("dp", "tp", None),
            P(("dp", "tp")),
            P(("dp", "tp")),
            P(("dp", "tp")),
            P(("dp", "tp")),
            P(("dp", "tp"), None),
            P(("dp", "tp"), None),
            P(("dp", "tp"), None),
            P(("dp", "tp"), None),
            P(("dp", "tp"), None),
            P(("dp", "tp"), None),
            P(("dp", "tp"), None),
            P(("dp", "tp"), None),
            P("dp", "tp"),
            P("dp", "tp"),
            P("tp", "dp"),
        ),
        check_vma=False,
    )
```

```python
import functools
import math
import types
import typing

import jax
import jax.numpy as jnp
from jax import lax
from jax.experimental import pallas as pl
from jax.experimental.pallas import tpu as pltpu
from jax.sharding import PartitionSpec as P

HEADS = 16
HEAD_DIM = 64
GROUPS = 8
BUCKETS = 32
MAX_DIST = 128
BLOCK = 128
PAIRS = GROUPS // 2
FAR = -1e30
SCALE = HEAD_DIM ** (-0.5)
MIB = 1 << 20

norm_epsilon = 1e-06
f32 = jnp.float32
bf16 = jnp.bfloat16


def nn(left, right):
    return lax.dot_general(left, right, (((1,), (0,)), ((), ())), preferred_element_type=f32)


def nt(left, right):
    return lax.dot_general(left, right, (((1,), (1,)), ((), ())), preferred_element_type=f32)


def tn(left, right):
    return lax.dot_general(left, right, (((0,), (0,)), ((), ())), preferred_element_type=f32)


def bits_of(count):
    return count.bit_length() - 1


def xor_static(value, flips, count):
    result = value
    for bit in range(bits_of(count)):
        if flips >> bit & 1:
            result = result + (1 << bit) * (1 - 2 * ((value // (1 << bit)) % 2))
    return result


def half_order(count, first_low):
    nb = bits_of(count)
    bits = list(range(nb)) if first_low else list(range(nb))[::-1]
    order = []
    for index in range(count):
        s = 0
        for place, bit in enumerate(bits):
            if index >> (nb - 1 - place) & 1:
                s |= 1 << bit
        order.append(s)
    return order, bits


def norm_scale(v):
    return lax.rsqrt(jnp.mean(v * v, axis=-1, keepdims=True) + norm_epsilon)


def norm_back(v, gain, dy):
    s = norm_scale(v)
    gained = dy * gain
    grad = s * gained - v * (s * s * s * jnp.mean(gained * v, axis=-1, keepdims=True))
    return grad, jnp.sum(dy * v * s, axis=0, keepdims=True)


def bucket_of(distance):
    exact = BUCKETS // 2
    bucket_count = jnp.zeros_like(distance)
    for step_index in range(1, exact):
        threshold = math.ceil(exact * (MAX_DIST / exact) ** (step_index / exact))
        bucket_count = bucket_count + (distance >= threshold).astype(jnp.int32)
    return jnp.where(distance < exact, distance, exact + bucket_count)


def whole_vmem():
    return pl.BlockSpec(memory_space=pltpu.VMEM)


def whole_smem():
    return pl.BlockSpec(memory_space=pltpu.SMEM)


def any_space():
    return pl.BlockSpec(memory_space=pl.ANY)


def params(limit_mib, **more):
    return pltpu.CompilerParams(vmem_limit_bytes=limit_mib * MIB, **more)


class Places:
    def __init__(self, rows):
        self.tp = lax.axis_size("tp")
        self.dp = lax.axis_size("dp")
        self.rows = rows
        self.share = self.tp // rows
        self.z_count = self.tp // 2

    def row(self):
        return lax.axis_index("tp") // self.share

    def part(self):
        return lax.axis_index("tp") % self.share

    def row_perm(self, k):
        share = self.share
        return [(t, ((t // share) ^ k) * share + t % share) for t in range(self.tp)]

    def part_perm(self, shift):
        share = self.share
        return [
            (t // share * share + (t % share + shift) % share, t) for t in range(self.tp)
        ]

    def core_perm(self):
        return [(t, t ^ 1) for t in range(self.tp)]

    def z_perm(self, shift):
        z_count = self.z_count
        return [(t, (t // 2 + shift) % z_count * 2 + t % 2) for t in range(self.tp)]

    def dp_perm(self, flips):
        return [(d, d ^ flips) for d in range(self.dp)]


def near_kinds(share):
    kinds = [(s, 0) for s in range(share)]
    return kinds + [(s, 1) for s in range(share) if s > 0 or share == 1]


def kind_distance(at, kind):
    s, back = kind
    part = at.part()
    return part - (part + s) % at.share + at.share * back


def tile_distance(at, kind):
    key = lax.broadcasted_iota(jnp.int32, (BLOCK, BLOCK), 0)
    query = lax.broadcasted_iota(jnp.int32, (BLOCK, BLOCK), 1)
    return BLOCK * kind_distance(at, kind) + query - key


def fill_bias_tiles(at, table, tiles):
    kinds = near_kinds(at.share)

    def one_group(group, carry):
        for number, kind in enumerate(kinds):
            distance = tile_distance(at, kind)
            bucket = bucket_of(jnp.maximum(distance, 0))
            for j in range(2):
                head = group * 2 + j
                last = table[(BUCKETS - 1) * HEADS + head]
                value = jnp.zeros((BLOCK, BLOCK), f32)
                for b in range(BUCKETS - 1):
                    value = jnp.where(bucket == b, table[b * HEADS + head] - last, value)
                tiles[group, number, :, j * BLOCK : (j + 1) * BLOCK] = jnp.where(
                    distance < 0, FAR, value
                )
        return carry

    lax.fori_loop(0, GROUPS, one_group, 0)


def query_features(seg_block, table, group):
    shape = (HEAD_DIM, 2 * BLOCK)
    row = lax.broadcasted_iota(jnp.int32, shape, 0)
    seg = jnp.concatenate([seg_block, seg_block], axis=1)
    feature = jnp.where((row < 3) & (seg != row), FAR, 0.0)
    if table is not None:
        lane = lax.broadcasted_iota(jnp.int32, shape, 1)
        far = (BUCKETS - 1) * HEADS + group * 2
        rest = jnp.where(lane < BLOCK, table[far], table[far + 1])
        for part in range(3):
            rounded = rest.astype(bf16).astype(f32)
            feature = jnp.where(row == 3 + part, rounded, feature)
            rest = rest - rounded
    return feature.astype(bf16)


def turned(block):
    return block.astype(f32).T.astype(block.dtype)


def stacked_heads(pair):
    t = turned(pair)
    return jnp.concatenate([t[:HEAD_DIM], t[HEAD_DIM:]], axis=1)


def unstacked_heads(wide):
    return jnp.concatenate([wide[:, :BLOCK], wide[:, BLOCK:]], axis=0).T


def with_other(half, other, odd):
    return jnp.concatenate([other, half] if odd else [half, other], axis=0)


def fold_rows(tile):
    return tile.reshape(tile.shape[0] // 8, 8, tile.shape[1])


class Keys:
    def __init__(self, share, blocks, causal):
        self.share, self.blocks, self.causal = share, blocks, causal
        self.count = share * blocks

    def blocks_for(self, i):
        return (i + 1 if self.causal else self.blocks) * self.share

    def near(self, i, index, kinds):
        if not self.causal:
            return None
        j, s = divmod(index, self.share)
        kind = (s, i - j)
        return kinds.index(kind) if kind in kinds else None


def load_keys(keys, k_refs, feat_refs, odd, kaug):
    lane = lax.broadcasted_iota(jnp.int32, (BLOCK, 2 * HEAD_DIM), 1)
    own = (lane >= HEAD_DIM) if odd else (lane < HEAD_DIM)
    for index in range(keys.count):
        j, s = divmod(index, keys.share)
        rows = pl.ds(j * BLOCK, BLOCK)
        kaug[pl.ds(index * BLOCK, BLOCK), :] = jnp.where(
            own, k_refs[s][rows, :].astype(f32), feat_refs[s][rows, :].astype(f32)
        ).astype(bf16)


def turn_keys(keys, refs, target):
    for index in range(keys.count):
        j, s = divmod(index, keys.share)
        target[:, pl.ds(index * BLOCK, BLOCK)] = turned(refs[s][pl.ds(j * BLOCK, BLOCK), :])


def forward_pair(
    keys, kinds, pair, q_ref, seg_ref, kv_refs, feat_refs, tiles, last_parts, ctx_ref, log_ref, scratch
):
    kaug, vt, sbuf, pbuf = scratch
    lanes_at = lambda start, width: pl.ds(pl.multiple_of(start, BLOCK), width)
    k_refs = [ref.at[:, lanes_at(pair * BLOCK, BLOCK)] for ref in kv_refs]
    v_refs = [
        ref.at[:, lanes_at(GROUPS * HEAD_DIM + pair * BLOCK, BLOCK)] for ref in kv_refs
    ]
    turn_keys(keys, v_refs, vt)
    for gi in range(2):
        load_keys(keys, k_refs, feat_refs, gi, kaug)
        for i in range(q_ref.shape[0] // BLOCK):
            tokens = pl.ds(i * BLOCK, BLOCK)
            lanes = lanes_at((pair * 2 + gi) * BLOCK, BLOCK)
            features = query_features(seg_ref[:, tokens], last_parts, pair * 2 + gi)
            right = with_other(stacked_heads(q_ref[tokens, lanes]), features, gi)
            count = keys.blocks_for(i)
            top = jnp.full((8, 2 * BLOCK), -jnp.inf, f32)
            for index in range(count):
                rows = pl.ds(index * BLOCK, BLOCK)
                scores = nn(kaug[rows, :], right)
                near = keys.near(i, index, kinds)
                if near is not None:
                    scores = scores + tiles[pair * 2 + gi, near]
                sbuf[rows, :] = scores
                top = jnp.maximum(top, jnp.max(fold_rows(scores), axis=0))
            top = jnp.max(top, axis=0, keepdims=True)
            total = jnp.zeros((8, 2 * BLOCK), f32)
            for index in range(count):
                rows = pl.ds(index * BLOCK, BLOCK)
                exponent = jnp.exp(sbuf[rows, :] - top)
                total = total + jnp.sum(fold_rows(exponent), axis=0)
                pbuf[rows, :] = exponent.astype(bf16)
            total = jnp.sum(total, axis=0, keepdims=True)
            length = count * BLOCK
            context = nn(vt[pl.ds(gi * HEAD_DIM, HEAD_DIM), :length], pbuf[:length, :])
            ctx_ref[tokens, lanes] = unstacked_heads(context * (1.0 / total)).astype(bf16)
            log_ref[pair * 2 + gi, pl.ds(i, 1), :] = top + jnp.log(total)


def diagonal_sums(tile):
    row = lax.broadcasted_iota(jnp.int32, (BLOCK, BLOCK), 0)
    lane = lax.broadcasted_iota(jnp.int32, (BLOCK, BLOCK), 1)
    turn = (row + lane == BLOCK - 1).astype(f32).astype(bf16)
    high = tile.astype(bf16)
    rest = tile - high.astype(f32)
    mid = rest.astype(bf16)
    low = (rest - mid.astype(f32)).astype(bf16)
    turned_rows = nn(turn, high) + nn(turn, mid) + nn(turn, low)
    sums = []
    for j in range(2):
        part = turned_rows[:, j * BLOCK : (j + 1) * BLOCK]
        wide = jnp.concatenate([part, jnp.zeros_like(part)], axis=1)
        rolled = pltpu.roll(wide, 0, 1, stride=1, stride_axis=0)
        sums.append(jnp.sum(rolled, axis=0, keepdims=True))
    return jnp.concatenate(sums, axis=0)


def backward_body(
    keys,
    kinds,
    pair,
    q_ref,
    seg_ref,
    k_refs,
    v_refs,
    feat_refs,
    tiles,
    last_parts,
    log_ref,
    dctx_ref,
    dq_ref,
    dkv_refs,
    diagonals,
    dfar,
    scratch,
):
    kaug, kt, vn, sbuf, pbuf, gbuf, dk_acc, dv_acc, dtiles = scratch
    turn_keys(keys, k_refs, kt)
    for index in range(keys.count):
        j, s = divmod(index, keys.share)
        vn[pl.ds(index * BLOCK, BLOCK), :] = v_refs[s][pl.ds(j * BLOCK, BLOCK), :]
    for gi in range(2):
        load_keys(keys, k_refs, feat_refs, gi, kaug)
        group_rows = pl.ds(gi * HEAD_DIM, HEAD_DIM)
        seen = set()
        far = jnp.zeros((8, 2 * BLOCK), f32)
        n_blocks = q_ref.shape[0] // BLOCK
        for i in reversed(range(n_blocks)):
            tokens = pl.ds(i * BLOCK, BLOCK)
            lanes = pl.ds(gi * BLOCK, BLOCK)
            features = query_features(seg_ref[:, tokens], last_parts, pair * 2 + gi)
            queries = stacked_heads(q_ref[tokens, lanes])
            right = with_other(queries, features, gi)
            grads = stacked_heads(dctx_ref[tokens, lanes])
            grads_right = with_other(grads, jnp.zeros_like(grads), gi)
            logsum = log_ref[gi, pl.ds(i, 1), :]
            count = keys.blocks_for(i)
            middle = jnp.zeros((8, 2 * BLOCK), f32)
            for index in range(count):
                rows = pl.ds(index * BLOCK, BLOCK)
                scores = nn(kaug[rows, :], right)
                near = keys.near(i, index, kinds)
                if near is not None:
                    scores = scores + tiles[gi, near]
                probs = jnp.exp(scores - logsum)
                grad_probs = nn(vn[rows, :], grads_right)
                middle = middle + jnp.sum(fold_rows(probs * grad_probs), axis=0)
                sbuf[rows, :] = probs
                gbuf[rows, :] = grad_probs
                pbuf[rows, :] = probs.astype(bf16)
            middle = jnp.sum(middle, axis=0, keepdims=True)
            length = count * BLOCK
            grad_v = nt(grads, pbuf[:length, :])
            for index in range(count):
                rows = pl.ds(index * BLOCK, BLOCK)
                grad_scores = (sbuf[rows, :] * (gbuf[rows, :] - middle)).astype(bf16)
                pbuf[rows, :] = grad_scores
                if keys.causal:
                    wide = grad_scores.astype(f32)
                    near = keys.near(i, index, kinds)
                    if near is None:
                        far = far + jnp.sum(fold_rows(wide), axis=0)
                    elif near in seen:
                        dtiles[near] = dtiles[near] + wide
                    else:
                        dtiles[near] = wide
                        seen.add(near)
            grad_k = nt(queries, pbuf[:length, :])
            grad_q = nn(kt[group_rows, :length], pbuf[:length, :])
            dq_ref[tokens, lanes] = unstacked_heads(grad_q * SCALE).astype(bf16)
            if i == n_blocks - 1:
                dk_acc[group_rows, :length] = grad_k
                dv_acc[group_rows, :length] = grad_v
            else:
                dk_acc[group_rows, :length] += grad_k
                dv_acc[group_rows, :length] += grad_v
        if keys.causal:
            dfar[gi] = far
            for near in range(len(kinds)):
                diagonals[gi, 2 * near : 2 * near + 2, :] = diagonal_sums(dtiles[near])
    for index in range(keys.count):
        j, s = divmod(index, keys.share)
        columns = pl.ds(index * BLOCK, BLOCK)
        rows = pl.ds(j * BLOCK, BLOCK)
        dkv_refs[s][0, rows, :] = dk_acc[:, columns].T.astype(bf16)
        dkv_refs[s][1, rows, :] = dv_acc[:, columns].T.astype(bf16)


class DpSum:
    def __init__(self, at):
        self.at = at
        self.bits = [half_order(at.dp, half == 0)[1] for half in range(2)]
        self.d = lax.axis_index("dp")

    def held(self, half, step):
        gone = self.bits[half][:step]
        return [s for s in range(self.at.dp) if not any(s >> bit & 1 for bit in gone)]

    def sent(self, half, step):
        bit = self.bits[half][step]
        return [(s, s ^ 1 << bit) for s in self.held(half, step) if s >> bit & 1]

    def count(self, step):
        return len(self.held(0, step))

    def partner(self, half, step):
        return xor_static(self.d, 1 << self.bits[half][step], self.at.dp)

    def copies(self, step, source_of, landing, sems):
        made = []
        for half in range(2):
            for sent, joined in self.sent(half, step):
                slot = self.held(half, step + 1).index(joined)
                made.append(
                    remote(
                        source_of(half, sent),
                        landing.at[half, slot],
                        sems,
                        half * self.count(step + 1) + slot,
                        "dp",
                        self.partner(half, step),
                    )
                )
        return made


def first_step_scratch(at, half_shape):
    return [
        pltpu.VMEM(half_shape, bf16),
        pltpu.VMEM(half_shape, bf16),
        pltpu.SemaphoreType.DMA((at.dp,)),
        pltpu.SemaphoreType.DMA((at.dp,)),
        pltpu.SemaphoreType.DMA((at.dp,)),
    ]


def half_shape_of(at, grads):
    return (2, at.dp // 2, at.z_count // 2, *grads.shape[2:])


class FirstStep:
    BUFFERS = 5

    def __init__(self, at, source, out, buffers):
        self.at, self.source, self.out = at, source, out
        self.landing, self.own, *self.sems, self.own_sems = buffers

    def copies(self):
        total = DpSum(self.at)
        half_z = self.at.z_count // 2
        entry = lambda half, s: self.source.at[
            xor_static(total.d, s, self.at.dp), pl.ds(half * half_z, half_z)
        ]
        made = total.copies(0, entry, self.landing, self.sems)
        for half in range(2):
            for slot, s in enumerate(total.held(half, 1)):
                made.append(
                    pltpu.make_async_copy(
                        entry(half, s),
                        self.own.at[half, slot],
                        self.own_sems.at[half * total.count(1) + slot],
                    )
                )
        return made

    def start(self):
        for copy in self.copies():
            copy.start()

    def end(self):
        for copy in self.copies():
            copy.wait()
        for half in range(2):
            for slot in range(self.at.dp // 2):
                for chunk in range(self.at.z_count // 2):
                    for m in range(3):
                        self.out[half, slot, chunk, m] = (
                            self.own[half, slot, chunk, m] + self.landing[half, slot, chunk, m]
                        )


def cross_backward_kernel(at, keys, *refs):
    refs = list(refs)
    take = lambda n: [refs.pop(0) for _ in range(n)]
    q_ref, seg_ref = take(2)
    k_refs, v_refs, feat_refs = take(keys.share), take(keys.share), take(keys.share)
    log_ref, dctx_ref, ffn_in, output_in = take(4)
    (dq_ref,) = take(1)
    dkv_refs = take(keys.share)
    ffn_out, output_out = take(2)
    first = FirstStep(at, ffn_in, ffn_out, take(FirstStep.BUFFERS))
    return_buffers = take(RowReturn.BUFFERS)

    @pl.when(pl.program_id(0) == 0)
    def _():
        greet(at)
        first.start()
        RowReturn(at, output_in, output_out, return_buffers).start()

    backward_body(
        keys,
        None,
        pl.program_id(0),
        q_ref,
        seg_ref,
        k_refs,
        v_refs,
        feat_refs,
        None,
        None,
        log_ref,
        dctx_ref,
        dq_ref,
        dkv_refs,
        None,
        None,
        (*refs, None),
    )

    @pl.when(pl.program_id(0) == PAIRS - 1)
    def _():
        first.end()
        RowReturn(at, output_in, output_out, return_buffers).end()


def backward_scratch(length):
    return [
        pltpu.VMEM((length, 2 * HEAD_DIM), bf16),
        pltpu.VMEM((2 * HEAD_DIM, length), bf16),
        pltpu.VMEM((length, 2 * HEAD_DIM), bf16),
        pltpu.VMEM((length, 2 * BLOCK), f32),
        pltpu.VMEM((length, 2 * BLOCK), bf16),
        pltpu.VMEM((length, 2 * BLOCK), f32),
        pltpu.VMEM((2 * HEAD_DIM, length), f32),
        pltpu.VMEM((2 * HEAD_DIM, length), f32),
    ]


def cross_backward(
    at, queries, key_values, features, seg_row, logsum, grad_context, ffn_grads, output
):
    tokens = queries.shape[0]
    span = key_values[0].shape[0]
    blocks = tokens // BLOCK
    keys = Keys(at.share, span // BLOCK, False)
    length = keys.count * BLOCK
    work = blocks * length * 2 * BLOCK * GROUPS
    token_spec = pl.BlockSpec((tokens, 2 * BLOCK), lambda p: (0, p))
    specs = [token_spec, pl.BlockSpec(seg_row.shape, lambda p: (0, 0))]
    specs += [pl.BlockSpec((span, BLOCK), lambda p: (0, p))] * at.share
    specs += [pl.BlockSpec((span, BLOCK), lambda p: (0, PAIRS + p))] * at.share
    specs += [pl.BlockSpec((span, BLOCK), lambda p: (0, 0))] * at.share
    specs += [pl.BlockSpec((2, blocks, 2 * BLOCK), lambda p: (p, 0, 0)), token_spec]
    specs += [any_space()] * 2
    half_shape = half_shape_of(at, ffn_grads)
    return pl.pallas_call(
        functools.partial(cross_backward_kernel, at, keys),
        grid=(PAIRS,),
        out_shape=[jax.ShapeDtypeStruct((tokens, HEADS * HEAD_DIM), bf16)]
        + [jax.ShapeDtypeStruct((2, span, GROUPS * HEAD_DIM), bf16)] * at.share
        + [jax.ShapeDtypeStruct(half_shape, bf16), jax.ShapeDtypeStruct(output.shape, bf16)],
        in_specs=specs,
        out_specs=[token_spec]
        + [pl.BlockSpec((2, span, BLOCK), lambda p: (0, 0, p))] * at.share
        + [whole_vmem()] * 2,
        scratch_shapes=[
            *first_step_scratch(at, half_shape),
            *RowReturn.scratch(at, output),
            *backward_scratch(length),
        ],
        compiler_params=params(48, collective_id=4, has_side_effects=True),
        cost_estimate=pl.CostEstimate(
            flops=work * 1024, bytes_accessed=16 * MIB, transcendentals=work
        ),
        name="cross_backward",
    )(
        queries,
        seg_row,
        *key_values,
        *key_values,
        *features,
        logsum,
        grad_context,
        ffn_grads,
        output,
    )


def remote(source, target, sems, number, axis, index):
    send, receive = sems
    return pltpu.make_async_remote_copy(
        src_ref=source,
        dst_ref=target,
        send_sem=send.at[number],
        recv_sem=receive.at[number],
        device_id={axis: index},
        device_id_type=pl.DeviceIdType.MESH,
    )


def tp_at(at, z):
    return z * 2 + lax.axis_index("tp") % 2


def other_core():
    t = lax.axis_index("tp")
    return t + 1 - 2 * (t % 2)


def greet(at):
    barrier = pltpu.get_barrier_semaphore()
    t, d = lax.axis_index("tp"), lax.axis_index("dp")
    if at.share == 2:
        others = [other_core()]
        others += [tp_at(at, (t // 2 + k) % at.z_count) for k in range(1, at.z_count)]
    else:
        others = [(t + k) % at.tp for k in range(1, at.tp)]
    targets = [{"tp": other} for other in others]
    targets += [{"dp": xor_static(d, 1 << bit, at.dp)} for bit in range(bits_of(at.dp))]
    for target in targets:
        pl.semaphore_signal(
            barrier, inc=1, device_id=target, device_id_type=pl.DeviceIdType.MESH
        )
    pl.semaphore_wait(barrier, len(targets))


def key_feature_tile(seg_line):
    column = jnp.broadcast_to(seg_line.astype(f32), (BLOCK, BLOCK)).T
    lane = lax.broadcasted_iota(jnp.int32, (BLOCK, BLOCK), 1) % HEAD_DIM
    same = jnp.where(column == lane.astype(f32), 1.0, 0.0)
    ones = jnp.where(lane < 6, 1.0, 0.0)
    return jnp.where(lane < 3, same, ones).astype(bf16)


def forward_messages(at):
    names = [(kind, k) for k in range(1, at.rows) for kind in ("x", "seg", "mem", "cot")]
    names += [(kind, s) for s in range(1, at.share) for kind in ("seg_part", "kv", "mem_kv")]
    names += [("ring", k) for k in range(1, at.z_count)]
    names += [("w", k, s) for k in range(at.z_count) for s in range(1, at.dp)]
    names += [("cot_core",), ("held",)]
    return {name: number for number, name in enumerate(names)}


class Gather:
    def __init__(self, at, start, copies, flush, own, gathered, out):
        self.at, self.start, self.copies, self.flush = at, start, copies, flush
        self.own, self.gathered, self.out = own, gathered, out
        self.z, self.d = lax.axis_index("tp") // 2, lax.axis_index("dp")

    def order(self, k):
        return half_order(self.at.dp, k % 2 == 0)[1]

    def held(self, k, s):
        return self.own if (k, s) == (0, 0) else self.gathered.at[k, s]

    def pass_on(self, k, s):
        bits = self.order(k)
        seen = [place for place, bit in enumerate(bits) if s >> bit & 1]
        for bit in bits[max(seen) + 1 if seen else 0 :]:
            self.start(
                ("w", k, s | 1 << bit),
                self.held(k, s),
                self.gathered.at[k, s | 1 << bit],
                "dp",
                xor_static(self.d, 1 << bit, self.at.dp),
            )

    def ring(self, k):
        self.start(
            ("ring", k),
            self.held(k - 1, 0),
            self.gathered.at[k, 0],
            "tp",
            tp_at(self.at, (self.z + 1) % self.at.z_count),
        )

    def arrived(self, k, s):
        self.copies["w", k, s].wait()
        self.flush(self.gathered.at[k, s], self.out.at[k, s])

    def arrive_ring(self, k):
        self.copies["ring", k].wait()
        self.flush(self.gathered.at[k, 0], self.out.at[k, 0])
        if k + 1 < self.at.z_count:
            self.ring(k + 1)
        self.pass_on(k, 0)

    def relay(self, k):
        bits = self.order(k)
        held = [0]
        for bit in bits[:-1]:
            for s in list(held):
                self.arrived(k, s | 1 << bit)
                self.pass_on(k, s | 1 << bit)
                held.append(s | 1 << bit)

    def finish(self, k):
        last = self.order(k)[-1]
        for s in range(self.at.dp):
            if s >> last & 1:
                self.arrived(k, s)


class Kept(typing.NamedTuple):
    x: typing.Any
    held_self: typing.Any
    queries: typing.Any
    kv: typing.Any
    self_context: typing.Any
    self_log: typing.Any
    stream_one: typing.Any
    held_cross: typing.Any
    cross_queries: typing.Any
    mem: typing.Any
    mem_kv: typing.Any
    cross_context: typing.Any
    cross_log: typing.Any
    stream_two: typing.Any
    held_ffn: typing.Any
    tiles: typing.Any
    seg_row: typing.Any


def forward_kernel(at, shapes, *refs):
    refs = list(refs)
    take = lambda n: [refs.pop(0) for _ in range(n)]
    inputs, memory, cot_in, segs = take(4)
    piece_parts = take(3)
    weight_refs = take(8)
    *gains, table = take(4)
    outs = Kept(*take(len(Kept._fields)))
    feat_outs, mem_feat_outs = take(at.share), take(at.share)
    kv_outs, mem_kv_outs = take(at.share - 1), take(at.share - 1)
    cot_out, cot_other_out, held_other_out, gathered_out = take(4)
    bufs = Kept(*take(len(Kept._fields)))
    feats, mem_feats = take(at.share), take(at.share)
    kv_others, mem_kv_others = take(at.share - 1), take(at.share - 1)
    weights = take(8)
    cot, cot_other, held_other, piece, gathered = take(5)
    seg_buf, seg_others, kaug, vt, sbuf, pbuf = take(6)
    send_sems, recv_sems, load_sems, flush_sems = take(4)
    scratch = (kaug, vt, sbuf, pbuf)
    numbers = forward_messages(at)
    kinds = near_kinds(at.share)
    row, part = at.row(), at.part()
    z = lax.axis_index("tp") // 2
    seq, features = inputs.shape[1:]
    mem_seq = memory.shape[1]
    tokens, mem_tokens = at.rows * seq, at.rows * mem_seq
    key_width = GROUPS * HEAD_DIM
    copies, flushes = {}, []

    def start(name, source, target, axis, index):
        copies[name] = remote(source, target, (send_sems, recv_sems), numbers[name], axis, index)
        copies[name].start()

    def start_rows(kind, source, target, height):
        for k in range(1, at.rows):
            there = xor_static(row, k, at.rows)
            start(
                (kind, k),
                source.at[there],
                target.at[pl.ds(pl.multiple_of(row * height, height), height), :],
                "tp",
                there * at.share + part,
            )

    def start_parts(kind, source, targets):
        for s in range(1, at.share):
            start(
                (kind, s),
                source,
                targets[s - 1],
                "tp",
                row * at.share + (part + at.share - s) % at.share,
            )

    def wait(kind, count):
        for k in range(1, count):
            copies[kind, k].wait()

    def flush(source, target):
        copy = pltpu.make_async_copy(source, target, flush_sems.at[len(flushes)])
        flushes.append(copy)
        copy.start()
        return copy

    def local_rows(source, target, height, number):
        return pltpu.make_async_copy(
            source.at[row],
            target.at[pl.ds(pl.multiple_of(row * height, height), height), :],
            load_sems.at[number],
        )

    greet(at)
    start_rows("x", inputs, bufs.x, seq)
    for k in range(1, at.rows):
        there = xor_static(row, k, at.rows)
        start(
            ("seg", k), segs.at[there], seg_buf.at[row], "tp", there * at.share + part
        )
    for m in range(3):
        piece[m] = piece_parts[m][...]
    gather = Gather(at, start, copies, flush, piece, gathered, gathered_out)
    gather.pass_on(0, 0)
    loads = [local_rows(inputs, bufs.x, seq, 8), local_rows(memory, bufs.mem, mem_seq, 9)]
    loads += [
        local_rows(cot_in, cot, seq, 10),
        pltpu.make_async_copy(segs.at[row], seg_buf.at[row], load_sems.at[11]),
    ]
    weight_loads = [
        pltpu.make_async_copy(source, target, load_sems.at[number])
        for number, (source, target) in enumerate(zip(weight_refs, weights))
    ]
    for copy in loads + weight_loads:
        copy.start()
    for copy in loads:
        copy.wait()
    flush(piece, gathered_out.at[0, 0])
    fill_bias_tiles(at, table, bufs.tiles)
    flush(bufs.tiles, outs.tiles)
    wait("seg", at.rows)
    start_parts("seg_part", seg_buf, [seg_others.at[s] for s in range(at.share - 1)])
    wait("seg_part", at.share)
    for s in range(at.share):
        for i in range(at.rows):
            line = lambda j: seg_buf[i, j : j + 1, :] if s == 0 else seg_others[s - 1, i, j : j + 1, :]
            feats[s][i * seq : (i + 1) * seq, :] = key_feature_tile(line(0))
            mem_feats[s][i * mem_seq : (i + 1) * mem_seq, :] = key_feature_tile(line(1))[:mem_seq]
            if s == 0:
                bufs.seg_row[:, i * seq : (i + 1) * seq] = line(0)
        flush(feats[s], feat_outs[s])
        flush(mem_feats[s], mem_feat_outs[s])
    flush(bufs.seg_row, outs.seg_row)
    gather.relay(0)
    for copy in weight_loads:
        copy.wait()
    sq, sk, sv, so, cq, ck, cv, co = weights

    def blocks(height):
        step = min(256, height)
        return [pl.ds(first, step) for first in range(0, height, step)]

    def normed(value, number):
        return (value * norm_scale(value) * gains[number][...]).astype(bf16)

    wait("x", at.rows)
    gather.ring(1)
    flush(bufs.x, outs.x)
    for here in blocks(tokens):
        held = normed(bufs.x[here, :].astype(f32), 0)
        bufs.held_self[here, :] = held
        bufs.kv[here, :key_width] = nn(held, sk[...]).astype(bf16)
        bufs.kv[here, key_width:] = nn(held, sv[...]).astype(bf16)
    start_parts("kv", bufs.kv, kv_others)
    for here in blocks(tokens):
        bufs.queries[here, :] = (nn(bufs.held_self[here, :], sq[...]) * SCALE).astype(bf16)
    flush(bufs.held_self, outs.held_self)
    flush(bufs.kv, outs.kv)
    flush(bufs.queries, outs.queries)
    gather.arrive_ring(1)
    wait("kv", at.share)
    for s in range(at.share - 1):
        flush(kv_others[s], kv_outs[s])

    def self_pair(pair, carry):
        forward_pair(
            Keys(at.share, at.rows, True),
            kinds,
            pair,
            bufs.queries,
            bufs.seg_row,
            [bufs.kv, *kv_others],
            feats,
            bufs.tiles,
            table,
            bufs.self_context,
            bufs.self_log,
            scratch,
        )
        return carry

    start_rows("mem", memory, bufs.mem, mem_seq)
    lax.fori_loop(0, 2, self_pair, 0)
    if at.z_count > 2:
        gather.arrive_ring(2)
    gather.relay(1)
    lax.fori_loop(2, PAIRS, self_pair, 0)
    for k in range(3, at.z_count):
        gather.arrive_ring(k)
        gather.relay(k - 1)
    start_rows("cot", cot_in, cot, seq)
    wait("mem", at.rows)
    flush(bufs.mem, outs.mem)
    flush(bufs.self_context, outs.self_context)
    flush(bufs.self_log, outs.self_log)
    for here in blocks(mem_tokens):
        rows = bufs.mem[here, :]
        bufs.mem_kv[here, :key_width] = nn(rows, ck[...]).astype(bf16)
        bufs.mem_kv[here, key_width:] = nn(rows, cv[...]).astype(bf16)
    start_parts("mem_kv", bufs.mem_kv, mem_kv_others)
    flush(bufs.mem_kv, outs.mem_kv)
    for here in blocks(tokens):
        stream = bufs.x[here, :].astype(f32) + nn(bufs.self_context[here, :], so[...])
        bufs.stream_one[here, :] = stream
        held = normed(stream, 1)
        bufs.held_cross[here, :] = held
        bufs.cross_queries[here, :] = (nn(held, cq[...]) * SCALE).astype(bf16)
    flush(bufs.stream_one, outs.stream_one)
    flush(bufs.held_cross, outs.held_cross)
    flush(bufs.cross_queries, outs.cross_queries)

    wait("mem_kv", at.share)
    for s in range(at.share - 1):
        flush(mem_kv_others[s], mem_kv_outs[s])

    def cross_pair(pair, carry):
        forward_pair(
            Keys(at.share, mem_tokens // BLOCK, False),
            kinds,
            pair,
            bufs.cross_queries,
            bufs.seg_row,
            [bufs.mem_kv, *mem_kv_others],
            mem_feats,
            None,
            None,
            bufs.cross_context,
            bufs.cross_log,
            scratch,
        )
        return carry

    lax.fori_loop(0, 2, cross_pair, 0)
    gather.relay(at.z_count - 1)
    lax.fori_loop(2, PAIRS, cross_pair, 0)
    flush(bufs.cross_context, outs.cross_context)
    flush(bufs.cross_log, outs.cross_log)
    for here in blocks(tokens):
        stream = bufs.stream_one[here, :] + nn(bufs.cross_context[here, :], co[...])
        bufs.stream_two[here, :] = stream
        bufs.held_ffn[here, :] = normed(stream, 2)
    start(("held",), bufs.held_ffn, held_other, "tp", other_core())
    flush(bufs.stream_two, outs.stream_two)
    flush(bufs.held_ffn, outs.held_ffn)
    for k in range(at.z_count):
        gather.finish(k)
    wait("cot", at.rows)
    start(("cot_core",), cot, cot_other, "tp", other_core())
    flush(cot, cot_out)
    copies[("held",)].wait()
    flush(held_other, held_other_out)
    copies[("cot_core",)].wait()
    flush(cot_other, cot_other_out)
    for copy in flushes:
        copy.wait()


def forward(at, inputs, memory, cotangent, segs, piece_parts, weights, gains, table):
    seq, features = inputs.shape[1:]
    mem_seq = memory.shape[1]
    tokens, mem_tokens = at.rows * seq, at.rows * mem_seq
    key_width = GROUPS * HEAD_DIM
    of = jax.ShapeDtypeStruct
    wide = of((tokens, features), bf16)
    log = of((GROUPS, at.rows, 2 * BLOCK), f32)
    kv, mem_kv = of((tokens, 2 * key_width), bf16), of((mem_tokens, 2 * key_width), bf16)
    shapes = Kept(
        x=wide,
        held_self=wide,
        queries=wide,
        kv=kv,
        self_context=wide,
        self_log=log,
        stream_one=of((tokens, features), f32),
        held_cross=wide,
        cross_queries=wide,
        mem=of((mem_tokens, features), bf16),
        mem_kv=mem_kv,
        cross_context=wide,
        cross_log=log,
        stream_two=of((tokens, features), f32),
        held_ffn=wide,
        tiles=of((GROUPS, len(near_kinds(at.share)), BLOCK, 2 * BLOCK), f32),
        seg_row=of((1, tokens), jnp.int32),
    )
    buffered = list(shapes)
    buffered += [of((tokens, 2 * HEAD_DIM), bf16)] * at.share
    buffered += [of((mem_tokens, 2 * HEAD_DIM), bf16)] * at.share
    buffered += [kv] * (at.share - 1) + [mem_kv] * (at.share - 1)
    piece_shape = (3, *piece_parts[0].shape)
    gathered = of((at.z_count, at.dp, *piece_shape), bf16)
    length = max(tokens, mem_tokens) * at.share
    messages = len(forward_messages(at))
    results = pl.pallas_call(
        functools.partial(forward_kernel, at, shapes),
        out_shape=buffered + [wide, wide, wide, gathered],
        in_specs=[any_space()] * 4
        + [whole_vmem()] * 3
        + [any_space()] * 8
        + [whole_vmem()] * 3
        + [whole_smem()],
        out_specs=[any_space()] * (len(buffered) + 4),
        scratch_shapes=[pltpu.VMEM(shape.shape, shape.dtype) for shape in buffered]
        + [pltpu.VMEM(weight.shape, bf16) for weight in weights]
        + [pltpu.VMEM((tokens, features), bf16)] * 3
        + [
            pltpu.VMEM(piece_shape, bf16),
            pltpu.VMEM(gathered.shape, bf16),
            pltpu.VMEM((at.rows, 8, BLOCK), jnp.int32),
            pltpu.VMEM((at.share - 1, at.rows, 8, BLOCK), jnp.int32),
            pltpu.VMEM((length, 2 * HEAD_DIM), bf16),
            pltpu.VMEM((2 * HEAD_DIM, length), bf16),
            pltpu.VMEM((length, 2 * BLOCK), f32),
            pltpu.VMEM((length, 2 * BLOCK), bf16),
            pltpu.SemaphoreType.DMA((messages,)),
            pltpu.SemaphoreType.DMA((messages,)),
            pltpu.SemaphoreType.DMA((12,)),
            pltpu.SemaphoreType.DMA((len(buffered) + 3 + at.z_count * at.dp,)),
        ],
        compiler_params=params(60, collective_id=2, has_side_effects=True),
        cost_estimate=pl.CostEstimate(
            flops=40 * tokens * features * features,
            bytes_accessed=60 * MIB,
            transcendentals=0,
        ),
        name="forward",
    )(inputs, memory, cotangent, segs, *piece_parts, *weights, *gains, table)
    results = list(results)
    take = lambda n: [results.pop(0) for _ in range(n)]
    kept = Kept(*take(len(Kept._fields)))
    self_features, mem_features = take(at.share), take(at.share)
    kvs = [kept.kv, *take(at.share - 1)]
    mem_kvs = [kept.mem_kv, *take(at.share - 1)]
    cot, cot_other, held_other, gathered = results
    return types.SimpleNamespace(
        **kept._asdict(),
        self_features=self_features,
        mem_features=mem_features,
        kvs=kvs,
        mem_kvs=mem_kvs,
        cot=cot,
        cot_other=cot_other,
        held_other=held_other,
        gathered=gathered,
    )


def gelu_parts(v):
    slope = math.sqrt(2 / math.pi)
    square = v * v
    t = jnp.tanh(slope * v * (1.0 + 0.044715 * square))
    half = 0.5 * (1.0 + t)
    derivative = half + 0.5 * v * (1.0 - t * t) * slope * (1.0 + 3 * 0.044715 * square)
    return v * half, derivative


def ffn_parts(rows):
    first = (rows // 2 + 15) // 16 * 16
    return (0, first), (first, rows - first)


def ffn_kernel(at, span, later, *refs):
    held_refs, cot_refs = refs[0:2], refs[2:4]
    gathered = refs[4]
    sums, earlier, refs = (refs[5:9], refs[9], refs[10:]) if later else (None, None, refs[5:])
    if later:
        beside = FirstStep(at, earlier, refs[3], refs[-FirstStep.BUFFERS :])
        landings, *swap_sems = refs[-FirstStep.BUFFERS - 3 : -FirstStep.BUFFERS]
        refs = (*refs[:2], None, None, refs[2], *refs[4 : -FirstStep.BUFFERS - 3])
        greet(at)
        beside.start()
    out_refs = refs[0:4]
    grad_ref = refs[4]
    weights, acts, held, cot, out_stage, back_stage = refs[5:11]
    in_sems, w_sems, out_sems = refs[11:]
    d = lax.axis_index("dp")
    z = lax.axis_index("tp") // 2
    tokens = held_refs[0].shape[0]
    first_row, rows = span
    width = gathered.shape[4]

    def columns(s):
        return pl.ds(pl.multiple_of(xor_static(d, s, at.dp) * width, width), width)

    loads = []
    for which, (sources, target) in enumerate(((held_refs, held), (cot_refs, cot))):
        for half in range(2):
            for s in range(at.dp):
                loads.append(
                    pltpu.make_async_copy(
                        sources[half].at[:, columns(s)],
                        target.at[pl.ds(half * tokens, tokens), pl.ds(s * width, width)],
                        in_sems.at[(which * 2 + half) * at.dp + s],
                    )
                )
    stages = (out_stage, back_stage)
    if later:
        for which, target in enumerate(stages):
            for half in range(2):
                for s in range(at.dp):
                    loads.append(
                        pltpu.make_async_copy(
                            sums[which * 2 + half].at[:, columns(s)],
                            target.at[pl.ds(half * tokens, tokens), pl.ds(s * width, width)],
                            out_sems.at[(which * 2 + half) * at.dp + s],
                        )
                    )
    for k in range(at.z_count):
        for s in range(at.dp):
            number = k * at.dp + s
            loads.append(
                pltpu.make_async_copy(
                    gathered.at[k, s, :, pl.ds(first_row, rows), :],
                    weights.at[
                        :,
                        pl.ds(pl.multiple_of((z + at.z_count - k) % at.z_count * rows, rows), rows),
                        pl.ds(s * width, width),
                    ],
                    w_sems.at[number],
                )
            )
    for copy in loads:
        copy.start()
    for copy in loads:
        copy.wait()

    tile = 256

    def keep(stage, here, value):
        if later:
            value = value + stage[here, :].astype(f32)
        stage[here, :] = value.astype(bf16)

    def step(index, carry):
        here = pl.ds(pl.multiple_of(index * tile, tile), tile)
        held_tile, cot_tile = held[here, :], cot[here, :]
        gate = nt(held_tile, weights[0])
        up = nt(held_tile, weights[1])
        grad_hidden = nt(cot_tile, weights[2])
        active, slope = gelu_parts(gate)
        hidden = (active * up).astype(bf16)
        acts[2, here, :] = hidden
        keep(out_stage, here, nn(hidden, weights[2]))
        grad_gate = (grad_hidden * up * slope).astype(bf16)
        grad_up = (grad_hidden * active).astype(bf16)
        acts[0, here, :] = grad_gate
        acts[1, here, :] = grad_up
        keep(back_stage, here, nn(grad_gate, weights[0]) + nn(grad_up, weights[1]))
        return carry

    lax.fori_loop(0, 2 * tokens // tile, step, 0)

    swaps = []
    if later:
        for which, stage in enumerate(stages):
            swaps.append(
                remote(
                    stage.at[pl.ds(tokens, tokens), :],
                    landings.at[which],
                    swap_sems,
                    which,
                    "tp",
                    other_core(),
                )
            )
            swaps[which].start()

    stores = []
    for which, stage in enumerate(stages):
        for half in range(1 if later else 2):
            for s in range(at.dp):
                stores.append(
                    pltpu.make_async_copy(
                        stage.at[pl.ds(half * tokens, tokens), pl.ds(s * width, width)],
                        out_refs[which if later else which * 2 + half].at[:, columns(s)],
                        out_sems.at[(which * 2 + half) * at.dp + s],
                    )
                )
    if not later:
        for copy in stores:
            copy.start()

    hidden_rows = rows * at.z_count
    for start in range(0, hidden_rows, BLOCK):
        size = min(BLOCK, hidden_rows - start)
        for m in range(3):
            right = cot if m == 2 else held
            grad = tn(acts[m, :, start : start + size], right[...]).astype(bf16)
            first = start
            while first < start + size:
                chunk, inside = divmod(first, rows)
                last = min(start + size, (chunk + 1) * rows)
                for s in range(at.dp):
                    grad_ref[
                        xor_static(d, s, at.dp), chunk, m, inside : inside + last - first, :
                    ] = grad[first - start : last - start, s * width : (s + 1) * width]
                first = last
    if later:
        for which, stage in enumerate(stages):
            swaps[which].wait()
            for first in range(0, tokens, tile):
                here = pl.ds(first, tile)
                stage[here, :] = (
                    stage[here, :].astype(f32) + landings[which, here, :].astype(f32)
                ).astype(bf16)
        for copy in stores:
            copy.start()
    for copy in stores:
        copy.wait()
    if later:
        beside.end()


def ffn(at, span, held_own, held_other, cot_own, cot_other, gathered, sums=(), earlier=None):
    tokens, features = held_own.shape
    rows, width = span[1], gathered.shape[4]
    hidden = rows * at.z_count
    grad_shape = jax.ShapeDtypeStruct((at.dp, at.z_count, 3, rows, width), bf16)
    token_shape = jax.ShapeDtypeStruct((tokens, features), bf16)
    extra, extra_shape, extra_scratch, extra_params, results = [], [], [], {}, 4
    if sums:
        results = 2
        half_shape = half_shape_of(at, earlier)
        extra = [*sums, earlier]
        extra_shape = [jax.ShapeDtypeStruct(half_shape, bf16)]
        extra_scratch = [
            pltpu.VMEM((2, tokens, features), bf16),
            pltpu.SemaphoreType.DMA((2,)),
            pltpu.SemaphoreType.DMA((2,)),
            *first_step_scratch(at, half_shape),
        ]
        extra_params = dict(collective_id=5, has_side_effects=True)
    return pl.pallas_call(
        functools.partial(ffn_kernel, at, span, bool(sums)),
        out_shape=[token_shape] * results + [grad_shape] + extra_shape,
        in_specs=[any_space()] * (5 + len(extra)),
        out_specs=[any_space()] * results + [whole_vmem()] * (1 + len(extra_shape)),
        scratch_shapes=[
            pltpu.VMEM((3, hidden, features), bf16),
            pltpu.VMEM((3, 2 * tokens, hidden), bf16),
            pltpu.VMEM((2 * tokens, features), bf16),
            pltpu.VMEM((2 * tokens, features), bf16),
            pltpu.VMEM((2 * tokens, features), bf16),
            pltpu.VMEM((2 * tokens, features), bf16),
            pltpu.SemaphoreType.DMA((4 * at.dp,)),
            pltpu.SemaphoreType.DMA((at.z_count * at.dp,)),
            pltpu.SemaphoreType.DMA((4 * at.dp,)),
            *extra_scratch,
        ],
        compiler_params=params(58, **extra_params),
        cost_estimate=pl.CostEstimate(
            flops=18 * 2 * tokens * features * hidden,
            bytes_accessed=40 * MIB,
            transcendentals=2 * tokens * hidden,
        ),
        name="ffn",
    )(held_own, held_other, cot_own, cot_other, gathered, *extra)


def weight_grad_kernel(at, widths, *refs):
    n = len(widths)
    lefts, rights, outs = refs[:n], refs[n : 2 * n], refs[2 * n :]
    d = lax.axis_index("dp")
    core = lax.axis_index("tp") % 2
    rows = lefts[0].shape[1] // at.dp
    quarter = sum(widths) // 4
    offset = 0
    for left, right, total in zip(lefts, rights, widths):
        width = total // 2
        block = jnp.concatenate(
            [
                right[:, pl.ds(pl.multiple_of(half * width, width), width)]
                for half in (core, 1 - core)
            ],
            axis=1,
        )
        for s in range(at.dp):
            chosen = pl.ds(pl.multiple_of(xor_static(d, s, at.dp) * rows, rows), rows)
            grad = tn(left[:, chosen], block).astype(bf16)
            done = 0
            while done < width:
                part, inside = divmod(offset + done, quarter)
                taken = min(width - done, quarter - inside)
                place = half_order(at.dp, part == 0)[0].index(s)
                for sent in range(2):
                    first = sent * width + done
                    outs[part * 2 + sent][place, :, inside : inside + taken] = grad[
                        :, first : first + taken
                    ]
                done += taken
        offset += width


def weight_products(at, pairs):
    lefts = [left for left, _ in pairs]
    rights = [right for _, right in pairs]
    widths = [right.shape[1] for right in rights]
    features = lefts[0].shape[1]
    quarter = sum(widths) // 4
    shape = jax.ShapeDtypeStruct((at.dp, features // at.dp, quarter), bf16)
    return pl.pallas_call(
        functools.partial(weight_grad_kernel, at, widths),
        out_shape=[shape] * 4,
        in_specs=[whole_vmem()] * (2 * len(pairs)),
        out_specs=[whole_vmem()] * 4,
        compiler_params=params(48),
        cost_estimate=pl.CostEstimate(
            flops=2 * lefts[0].shape[0] * features * sum(widths),
            bytes_accessed=16 * MIB,
            transcendentals=0,
        ),
        name="weight_grads",
    )(*lefts, *rights)


def z_slots(at, bit):
    sent = [r for r in range(at.z_count) if r >> bit & 1 and r % (1 << bit) == 0]
    base = at.z_count - (at.z_count >> bit)
    return [(r, base + number) for number, r in enumerate(sent)]


class RowReturn:
    BUFFERS = 4

    def __init__(self, at, source, target, buffers):
        self.at, self.source, self.target = at, source, target
        self.landing, *sems, self.own_sem = buffers
        self.sems = tuple(sems)
        self.row, self.part = at.row(), at.part()

    @staticmethod
    def scratch(at, array):
        return [
            pltpu.VMEM(array.shape, array.dtype),
            pltpu.SemaphoreType.DMA((at.rows - 1,)),
            pltpu.SemaphoreType.DMA((at.rows - 1,)),
            pltpu.SemaphoreType.DMA((1,)),
        ]

    def copies(self):
        own = pltpu.make_async_copy(
            self.source.at[self.row], self.landing.at[self.row], self.own_sem.at[0]
        )
        made = [own]
        for k in range(1, self.at.rows):
            there = xor_static(self.row, k, self.at.rows)
            made.append(
                remote(
                    self.source.at[there],
                    self.landing.at[self.row],
                    self.sems,
                    k - 1,
                    "tp",
                    there * self.at.share + self.part,
                )
            )
        return made

    def start(self):
        for copy in self.copies():
            copy.start()

    def end(self):
        for copy in self.copies():
            copy.wait()
        for r in range(self.at.rows):
            self.target[r] = self.landing[r]


class Reduction:
    def __init__(self, at, first_low, buffers):
        self.at = at
        self.first, self.halves, self.z_in, self.done, self.last_in, *self.sems = buffers
        self.base = self.first
        _, self.bits = half_order(at.dp, first_low)
        self.z = lax.axis_index("tp") // 2
        self.core = lax.axis_index("tp") % 2
        self.rows = self.first.shape[1] // at.z_count
        self.copies = {}

    @staticmethod
    def scratch(at, rows, columns):
        n = at.dp // 2
        messages = 1 + bits_of(at.dp) + at.z_count
        return [
            pltpu.VMEM((at.dp, rows, columns), bf16),
            pltpu.VMEM((max(2 * n - 1, 1), rows, columns), bf16),
            pltpu.VMEM((at.z_count - 1, rows // at.z_count, columns), bf16),
            pltpu.VMEM((rows // at.z_count, columns), f32),
            pltpu.VMEM((rows // at.z_count // 2, columns), f32),
            pltpu.SemaphoreType.DMA((messages,)),
            pltpu.SemaphoreType.DMA((messages,)),
        ]

    BUFFERS = 7

    def start(self, key, copy):
        self.copies[key] = copy
        copy.start()

    def start_core(self, source):
        self.start("core", remote(source, self.first, self.sems, 0, "tp", other_core()))

    def end_core(self, keep):
        self.copies["core"].wait()
        for s in range(self.at.dp):
            self.first[s] = self.first[s] + keep[s]

    def half_at(self, place):
        n = self.at.dp >> (place + 1)
        return n, self.at.dp - 2 * n

    def start_half(self, place):
        n, offset = self.half_at(place)
        d = lax.axis_index("dp")
        self.start(
            ("half", place),
            remote(
                self.base.at[pl.ds(n, n)],
                self.halves.at[pl.ds(offset, n)],
                self.sems,
                1 + place,
                "dp",
                xor_static(d, 1 << self.bits[place], self.at.dp),
            ),
        )

    def end_half(self, place):
        self.copies["half", place].wait()
        n, offset = self.half_at(place)
        for s in range(n):
            self.first[s] = self.first[s] + self.halves[offset + s]
        self.base = self.first

    def z_rows(self, r):
        z = xor_static(self.z, r, self.at.z_count)
        return pl.ds(pl.multiple_of(z * self.rows, self.rows), self.rows)

    def start_z(self, bit):
        base = 1 + len(self.bits)
        partner = tp_at(self.at, xor_static(self.z, 1 << bit, self.at.z_count))
        for r, slot in z_slots(self.at, bit):
            self.start(
                ("z", slot),
                remote(
                    self.first.at[0, self.z_rows(r), :],
                    self.z_in.at[slot],
                    self.sems,
                    base + slot,
                    "tp",
                    partner,
                ),
            )

    def end_z(self, bit):
        for r, slot in z_slots(self.at, bit):
            self.copies["z", slot].wait()
            rows = self.z_rows(r ^ 1 << bit)
            total = self.first[0, rows, :].astype(f32) + self.z_in[slot].astype(f32)
            if 2 << bit == self.at.z_count:
                self.done[...] = total
            else:
                self.first[0, rows, :] = total.astype(bf16)

    def part(self, core):
        rows = self.rows // 2
        return pl.ds(pl.multiple_of(core * rows, rows), rows)

    def start_last(self):
        number = len(self.bits) + self.at.z_count
        self.start(
            "last",
            remote(
                self.done.at[self.part(1 - self.core), :],
                self.last_in,
                self.sems,
                number,
                "tp",
                other_core(),
            ),
        )

    def end_last(self, out, columns):
        out[0, :, columns] = self.done[self.part(self.core), :]
        self.copies["last"].wait()
        out[1, :, columns] = self.last_in[...]


def relative_sums(at, kinds, diagonals, dfar):
    lane = lax.broadcasted_iota(jnp.int32, (1, BLOCK), 1)
    onehots = []
    for kind in kinds:
        offset = lax.broadcasted_iota(jnp.int32, (2 * BLOCK, BLOCK), 0) - (BLOCK - 1)
        distance = BLOCK * kind_distance(at, kind) + offset
        bucket = bucket_of(jnp.maximum(distance, 0))
        column = lax.broadcasted_iota(jnp.int32, (2 * BLOCK, BLOCK), 1)
        onehots.append(jnp.where(bucket == column, 1.0, 0.0).astype(bf16))
    results = []
    for group in range(GROUPS):
        sums = jnp.zeros((2, BLOCK), f32)
        for number, onehot in enumerate(onehots):
            rest = diagonals[group, 2 * number : 2 * number + 2, :]
            for _ in range(3):
                part = rest.astype(bf16)
                sums = sums + nn(part, onehot)
                rest = rest - part.astype(f32)
        for j in range(2):
            far = jnp.sum(dfar[group, :, j * BLOCK : (j + 1) * BLOCK], axis=0, keepdims=True)
            far = jnp.sum(far, axis=1, keepdims=True)
            results.append(sums[j : j + 1] + jnp.where(lane == BUCKETS - 1, far, 0.0))
    return results


class CoreStep:
    BUFFERS = 4

    def __init__(self, at, first_low, buffers):
        self.at = at
        self.first, self.landing, *self.sems = buffers
        self.bit = half_order(at.dp, first_low)[1][0]

    @staticmethod
    def scratch(at, rows, columns, halves):
        return [
            pltpu.VMEM((at.dp, rows, columns), bf16),
            pltpu.VMEM((at.dp // 2 if halves else 1, rows if halves else 16, columns), bf16),
            pltpu.SemaphoreType.DMA((2,)),
            pltpu.SemaphoreType.DMA((2,)),
        ]

    def start_core(self, source):
        self.core = remote(source, self.first, self.sems, 0, "tp", other_core())
        self.core.start()

    def end_core(self, keep):
        self.core.wait()
        for s in range(self.at.dp):
            self.first[s] = self.first[s] + keep[s]

    def start_half(self):
        n = self.at.dp // 2
        partner = xor_static(lax.axis_index("dp"), 1 << self.bit, self.at.dp)
        self.half = remote(
            self.first.at[pl.ds(n, n)], self.landing, self.sems, 1, "dp", partner
        )
        self.half.start()

    def end_half(self, out):
        self.half.wait()
        for s in range(self.at.dp // 2):
            out[s] = self.first[s] + self.landing[s]


class FfnSum:
    def __init__(self, at, source, out, take):
        self.at, self.source, self.out = at, source, out
        self.total = DpSum(at)
        (self.work,) = take(1)
        self.landings = [take(3) for _ in range(1, bits_of(at.dp))]
        self.z_in, *self.z_sems, self.load_sems = take(4)
        self.z_sems = tuple(self.z_sems)
        self.z = lax.axis_index("tp") // 2
        self.copies = {}

    @staticmethod
    def scratch(at, half_shape):
        inner = half_shape[2:]
        scratch = [pltpu.VMEM((2, at.dp // 4, *inner), bf16)]
        for step in range(1, bits_of(at.dp)):
            count = at.dp >> (step + 1)
            scratch += [
                pltpu.VMEM((2, count, *inner), bf16),
                pltpu.SemaphoreType.DMA((2 * count,)),
                pltpu.SemaphoreType.DMA((2 * count,)),
            ]
        return scratch + [
            pltpu.VMEM((at.z_count - 1, *inner[1:]), bf16),
            pltpu.SemaphoreType.DMA((at.z_count - 1,)),
            pltpu.SemaphoreType.DMA((at.z_count - 1,)),
            pltpu.SemaphoreType.DMA((2 * (at.dp // 4),)),
        ]

    def start(self):
        total = self.total
        self.loads = []
        for half in range(2):
            for slot, s in enumerate(total.held(half, 2)):
                place = total.held(half, 1).index(s)
                self.loads.append(
                    pltpu.make_async_copy(
                        self.source.at[half, place],
                        self.work.at[half, slot],
                        self.load_sems.at[half * total.count(2) + slot],
                    )
                )
        entry = lambda half, s: self.source.at[half, total.held(half, 1).index(s)]
        self.send(1, entry)
        for copy in self.loads:
            copy.start()

    def send(self, step, entry):
        landing, *sems = self.landings[step - 1]
        self.dp_copies = self.total.copies(step, entry, landing, tuple(sems))
        for copy in self.dp_copies:
            copy.start()

    def to_z(self):
        total = self.total
        for copy in self.loads:
            copy.wait()
        for step in range(1, bits_of(self.at.dp)):
            for copy in self.dp_copies:
                copy.wait()
            landing = self.landings[step - 1][0]
            for half in range(2):
                for slot, s in enumerate(total.held(half, step + 1)):
                    place = total.held(half, 2).index(s)
                    for chunk in range(self.at.z_count // 2):
                        for m in range(3):
                            self.work[half, place, chunk, m] = (
                                self.work[half, place, chunk, m] + landing[half, slot, chunk, m]
                            )
            if step + 1 < bits_of(self.at.dp):
                self.send(
                    step + 1,
                    lambda half, s: self.work.at[half, total.held(half, 2).index(s)],
                )
        self.start_z(0)

    def chunk(self, r):
        z = xor_static(self.z, r, self.at.z_count)
        half_z = self.at.z_count // 2
        return self.work.at[z // half_z, 0, z % half_z]

    def start_z(self, bit):
        partner = tp_at(self.at, xor_static(self.z, 1 << bit, self.at.z_count))
        for r, slot in z_slots(self.at, bit):
            self.copies[slot] = remote(
                self.chunk(r), self.z_in.at[slot], self.z_sems, slot, "tp", partner
            )
            self.copies[slot].start()

    def end_z(self, bit):
        for r, slot in z_slots(self.at, bit):
            self.copies[slot].wait()
            kept = self.chunk(r ^ 1 << bit)
            for m in range(3):
                total = kept[m].astype(f32) + self.z_in[slot, m].astype(f32)
                if 2 << bit == self.at.z_count:
                    self.out[m] = total
                else:
                    kept[m] = total.astype(bf16)


def self_backward_kernel(at, *refs):
    refs = list(refs)
    take = lambda n: [refs.pop(0) for _ in range(n)]
    held, queries, seg_ref, logsum, grad_context, tiles, last_parts = take(7)
    kv_refs, feat_refs = take(at.share), take(at.share)
    gain, wq, wk, wv = take(4)
    late_sources = take(4)
    send_low, send_high = take(2)
    *ffn_ins, memory_in = take(3)
    flushed = take(5)
    gain_out, relative_out, *ffn_outs, memory_out = take(5)
    keep_low, keep_high, x_ref, grad_ref = late_targets = take(4)
    middle_outs, last_outs, (rows_out,) = buffers = take(2), take(2), take(1)
    late_sems, flush_sems = take(2)
    late_loads = [
        pltpu.make_async_copy(source, target, late_sems.at[number])
        for number, (source, target) in enumerate(zip(late_sources, late_targets))
    ]
    flushes = [
        pltpu.make_async_copy(source, target, flush_sems.at[number])
        for number, (source, target) in enumerate(zip(sum(buffers, []), flushed))
    ]
    middle = [CoreStep(at, half == 0, take(CoreStep.BUFFERS)) for half in range(2)]
    last = [CoreStep(at, half == 0, take(CoreStep.BUFFERS)) for half in range(2)]
    ffn_sums = [FfnSum(at, *pair, take) for pair in zip(ffn_ins, ffn_outs)]
    memory_return = RowReturn(at, memory_in, memory_out, take(RowReturn.BUFFERS))
    z_bits = range(bits_of(at.z_count))
    product_send, kv_in, dq, diagonals, dfar = take(5)
    own_kv, *other_kv = take(at.share)
    weight_sems, = take(1)
    kv_sems = take(2)
    d = lax.axis_index("dp")
    core = lax.axis_index("tp") % 2
    row, part = at.row(), at.part()
    features = held.shape[1]
    rows = features // at.dp
    kinds = near_kinds(at.share)
    keys = Keys(at.share, at.rows, True)
    lanes_at = lambda start, width: pl.ds(pl.multiple_of(start, BLOCK), width)

    def one_pair(scratch, pair, carry):
        four = lanes_at(pair * 2 * BLOCK, 2 * BLOCK)
        two = lanes_at(pair * BLOCK, BLOCK)
        values = lanes_at(GROUPS * HEAD_DIM + pair * BLOCK, BLOCK)
        both = pl.ds(pair * 2, 2)
        backward_body(
            keys,
            kinds,
            pair,
            queries.at[:, four],
            seg_ref,
            [ref.at[:, two] for ref in kv_refs],
            [ref.at[:, values] for ref in kv_refs],
            feat_refs,
            tiles.at[both],
            last_parts,
            logsum.at[both],
            grad_context.at[:, four],
            dq.at[:, four],
            [ref.at[:, :, two] for ref in (own_kv, *other_kv)],
            diagonals.at[both],
            dfar.at[both],
            scratch,
        )
        return carry

    def products(number, right, offset):
        width = right.shape[1] // 2
        order, _ = half_order(at.dp, number == 0)
        block = jnp.concatenate(
            [
                right[:, pl.ds(pl.multiple_of(half * width, width), width)]
                for half in (core, 1 - core)
            ],
            axis=1,
        )
        for place, s in enumerate(order):
            chosen = pl.ds(pl.multiple_of(xor_static(d, s, at.dp) * rows, rows), rows)
            both = tn(held[:, chosen], block).astype(bf16)
            last_outs[number][place, :, offset : offset + width] = both[:, :width]
            product_send[number, place, :, offset : offset + width] = both[:, width:]

    greet(at)
    for ffn_sum in ffn_sums:
        ffn_sum.start()
    middle[0].start_core(send_low)
    middle[1].start_core(send_high)
    memory_return.start()
    for copy in late_loads:
        copy.start()

    def attention(first, last):
        def pairs(*scratch):
            lax.fori_loop(first, last, functools.partial(one_pair, scratch), 0)

        pl.run_scoped(
            pairs,
            *backward_scratch(keys.count * BLOCK),
            pltpu.VMEM((len(kinds), BLOCK, 2 * BLOCK), f32),
        )

    attention(0, 2)
    ffn_sums[0].to_z()
    for copy in late_loads:
        copy.wait()
    for number, keep in enumerate((keep_low, keep_high)):
        middle[number].end_core(keep)
        middle[number].start_half()
    attention(2, PAIRS)
    ffn_sums[1].to_z()
    for bit in z_bits[1:]:
        ffn_sums[0].end_z(bit - 1)
        ffn_sums[0].start_z(bit)
    kv_copies = []
    for s in range(1, at.share):
        kv_copies.append(
            remote(
                other_kv[s - 1],
                kv_in.at[s - 1],
                kv_sems,
                s - 1,
                "tp",
                row * at.share + (part + s) % at.share,
            )
        )
    for copy in kv_copies:
        copy.start()
    products(0, dq, 0)
    last[0].start_core(product_send.at[0])
    for copy in kv_copies:
        copy.wait()
    for which in range(2):
        total = own_kv[which].astype(f32)
        for s in range(1, at.share):
            total = total + kv_in[s - 1, which].astype(f32)
        own_kv[which] = total.astype(bf16)
    for which in range(2):
        products(1, own_kv.at[which], which * (own_kv.shape[2] // 2))
    last[1].start_core(product_send.at[1])
    for bit in z_bits[1:]:
        ffn_sums[1].end_z(bit - 1)
        ffn_sums[1].start_z(bit)

    seq = rows_out.shape[1]

    def input_gradient(*weights):
        loads = [
            pltpu.make_async_copy(source, target, weight_sems.at[number])
            for number, (source, target) in enumerate(zip((wq, wk, wv), weights))
        ]
        for copy in loads:
            copy.start()
        for copy in loads:
            copy.wait()
        gain_sum = jnp.zeros((1, features), f32)
        gain_row = gain[...]
        for i in range(at.rows):
            here = pl.ds(i * seq, seq)
            dy = nt(dq[here, :], weights[0][...])
            dy = dy + nt(own_kv[0, here, :], weights[1][...])
            dy = dy + nt(own_kv[1, here, :], weights[2][...])
            grad, gain_part = norm_back(x_ref[here, :].astype(f32), gain_row, dy)
            gain_sum = gain_sum + gain_part
            rows_out[i] = (grad_ref[here, :] + grad).astype(bf16)
        gain_out[...] = gain_sum

    pl.run_scoped(input_gradient, *[pltpu.VMEM(w.shape, bf16) for w in (wq, wk, wv)])
    flushes[4].start()
    relative_out[...] = jnp.zeros(relative_out.shape, f32)
    for head, sums in enumerate(relative_sums(at, kinds, diagonals, dfar)):
        lane = head // 4 * BLOCK
        relative_out[head % 4 : head % 4 + 1, lane : lane + BLOCK] = sums
    for number in range(2):
        last[number].end_core(last_outs[number])
        for s in range(at.dp):
            last_outs[number][s] = last[number].first[s]
        flushes[2 + number].start()
    for number in range(2):
        middle[number].end_half(middle_outs[number])
        flushes[number].start()
    for ffn_sum in ffn_sums:
        ffn_sum.end_z(z_bits[-1])
    memory_return.end()
    for copy in flushes:
        copy.wait()


def self_backward(
    at,
    held,
    queries,
    kvs,
    features_of,
    seg_row,
    logsum,
    grad_context,
    tiles,
    last_parts,
    x_low,
    grad_one,
    gain,
    weights,
    middle,
    ffn_parts_now,
    memory_grad,
):
    keep_low, send_low, keep_high, send_high = middle
    tokens, features = held.shape
    _, rows, middle_columns = keep_low.shape
    key_width = kvs[0].shape[1] // 2
    last_columns = features // 2
    kinds = len(near_kinds(at.share))
    of = jax.ShapeDtypeStruct
    flushed = [of((at.dp // 2, rows, middle_columns), bf16)] * 2
    flushed += [of((at.dp, rows, last_columns), bf16)] * 2
    flushed += [of((at.rows, tokens // at.rows, features), bf16)]
    late = [keep_low, keep_high, x_low, grad_one]
    scratch = [pltpu.VMEM(array.shape, array.dtype) for array in late + flushed]
    scratch += [pltpu.SemaphoreType.DMA((len(late),)), pltpu.SemaphoreType.DMA((len(flushed),))]
    for columns, halves in ((middle_columns, True), (last_columns, False)):
        scratch += CoreStep.scratch(at, rows, columns, halves) * 2
    for part in ffn_parts_now:
        scratch += FfnSum.scratch(at, part.shape)
    scratch += RowReturn.scratch(at, memory_grad)
    scratch += [
        pltpu.VMEM((2, at.dp, rows, last_columns), bf16),
        pltpu.VMEM((at.share - 1, 2, tokens, key_width), bf16),
        pltpu.VMEM((tokens, features), bf16),
        pltpu.VMEM((GROUPS, 2 * kinds, 2 * BLOCK), f32),
        pltpu.VMEM((GROUPS, 8, 2 * BLOCK), f32),
        *[pltpu.VMEM((2, tokens, key_width), bf16)] * at.share,
        pltpu.SemaphoreType.DMA((3,)),
        pltpu.SemaphoreType.DMA((at.share - 1,)),
        pltpu.SemaphoreType.DMA((at.share - 1,)),
    ]
    return pl.pallas_call(
        functools.partial(self_backward_kernel, at),
        out_shape=flushed
        + [
            of((1, features), f32),
            of((4, features), f32),
            *[of(part.shape[3:], f32) for part in ffn_parts_now],
            of(memory_grad.shape, bf16),
        ],
        in_specs=[whole_vmem()] * 6
        + [whole_smem()]
        + [whole_vmem()] * (2 * at.share + 1)
        + [any_space()] * 12,
        out_specs=[any_space()] * len(flushed) + [whole_vmem()] * 5,
        scratch_shapes=scratch,
        compiler_params=params(62, collective_id=3, has_side_effects=True),
        cost_estimate=pl.CostEstimate(
            flops=20 * tokens * features * features,
            bytes_accessed=100 * MIB,
            transcendentals=0,
        ),
        name="self_backward",
    )(
        held,
        queries,
        seg_row,
        logsum,
        grad_context,
        tiles,
        last_parts,
        *kvs,
        *features_of,
        gain,
        *weights,
        *late,
        send_low,
        send_high,
        *ffn_parts_now,
        memory_grad,
    )


def tail_kernel(at, *refs):
    refs = list(refs)
    take = lambda n: [refs.pop(0) for _ in range(n)]
    middle_in, last_in = take(2), take(2)
    grad_rows, small_in = take(2)
    input_out, small_out, middle_out, last_out = take(4)
    middle = [
        Reduction(at, True, take(Reduction.BUFFERS)),
        Reduction(at, False, take(Reduction.BUFFERS)),
    ]
    last = [
        Reduction(at, True, take(Reduction.BUFFERS)),
        Reduction(at, False, take(Reduction.BUFFERS)),
    ]
    input_return = RowReturn(at, grad_rows, input_out, take(RowReturn.BUFFERS))
    small, small_ins = take(2)
    small_sems = take(2)
    (load_sems,) = take(1)
    d = lax.axis_index("dp")
    t = lax.axis_index("tp")
    z = t // 2
    bits = list(range(bits_of(at.dp)))
    z_bits = range(bits_of(at.z_count))

    loads = []
    for number, (source, reduction) in enumerate(zip(middle_in + last_in, middle + last)):
        reduction.base = source
        n = at.dp >> (2 if number < 2 else 1)
        loads.append(
            pltpu.make_async_copy(
                source.at[pl.ds(0, n)], reduction.first.at[pl.ds(0, n)], load_sems.at[number]
            )
        )
        loads[-1].start()
    greet(at)
    for reduction in middle:
        reduction.start_half(1)
    for reduction in last:
        reduction.start_half(0)
    input_return.start()
    for copy in loads:
        copy.wait()

    small[0:8, :] = small_in[...]
    steps = [("tp", other_core())]
    steps += [("dp", xor_static(d, 1 << bit, at.dp)) for bit in bits]
    small_copies = []

    def start_small(number):
        axis, index = steps[number]
        copy = remote(
            small.at[pl.ds(8 * number, 8)], small_ins.at[number], small_sems, number, axis, index
        )
        small_copies.append(copy)
        copy.start()

    def end_small(number):
        small_copies[number].wait()
        small[8 * number + 8 : 8 * number + 16, :] = (
            small[8 * number : 8 * number + 8, :] + small_ins[number]
        )

    start_small(0)
    end_small(0)
    start_small(1)
    for place in bits[1:]:
        for reduction in middle:
            reduction.end_half(place)
            if place + 1 < len(bits):
                reduction.start_half(place + 1)
            else:
                reduction.start_z(0)
        for reduction in last:
            reduction.end_half(place - 1)
            reduction.start_half(place)
        end_small(place)
        start_small(place + 1)
    for reduction in last:
        reduction.end_half(len(bits) - 1)
        reduction.start_z(0)
    final = len(steps)
    end_small(final - 1)
    z_copies = []
    for k in range(1, at.z_count):
        z_copies.append(
            remote(
                small.at[pl.ds(8 * final, 8)],
                small_ins.at[final + k - 1],
                small_sems,
                final + k - 1,
                "tp",
                tp_at(at, (z + k) % at.z_count),
            )
        )
    for copy in z_copies:
        copy.start()
    for bit in z_bits[1:]:
        for reduction in middle + last:
            reduction.end_z(bit - 1)
            reduction.start_z(bit)
    input_return.end()
    total = small[8 * final : 8 * final + 8, :]
    for k, copy in enumerate(z_copies):
        copy.wait()
        total = total + small_ins[final + k]
    small_out[...] = total
    for reduction in middle + last:
        reduction.end_z(z_bits[-1])
        reduction.start_last()
    for reductions, out in ((middle, middle_out), (last, last_out)):
        columns = out.shape[2] // 2
        for number, reduction in enumerate(reductions):
            reduction.end_last(out, slice(number * columns, (number + 1) * columns))


def tail(at, grad_rows, middle, last, small):
    _, rows, middle_columns = middle[0].shape
    last_columns = last[0].shape[2]
    share_rows = rows // at.z_count // 2
    steps = 1 + bits_of(at.dp)
    out_shape = [
        jax.ShapeDtypeStruct(grad_rows.shape, bf16),
        jax.ShapeDtypeStruct(small.shape, f32),
        jax.ShapeDtypeStruct((2, share_rows, 2 * middle_columns), f32),
        jax.ShapeDtypeStruct((2, share_rows, 2 * last_columns), f32),
    ]
    scratch = []
    for columns in (middle_columns, middle_columns, last_columns, last_columns):
        scratch += Reduction.scratch(at, rows, columns)
    scratch += RowReturn.scratch(at, grad_rows)
    dma = lambda n: [pltpu.SemaphoreType.DMA((n,))] * 2
    scratch += [
        pltpu.VMEM((8 * (steps + 1), small.shape[1]), f32),
        pltpu.VMEM((steps + at.z_count - 1, *small.shape), f32),
        *dma(steps + at.z_count - 1),
        pltpu.SemaphoreType.DMA((4,)),
    ]
    return pl.pallas_call(
        functools.partial(tail_kernel, at),
        out_shape=out_shape,
        in_specs=[any_space()] * 5 + [whole_vmem()],
        out_specs=[whole_vmem()] * 4,
        scratch_shapes=scratch,
        compiler_params=params(62, collective_id=1, has_side_effects=True),
        cost_estimate=pl.CostEstimate(
            flops=MIB, bytes_accessed=200 * MIB, transcendentals=0
        ),
        name="tail",
    )(*middle, *last, grad_rows, small)


def finish_kernel(widths, *refs):
    refs = list(refs)
    take = lambda n: [refs.pop(0) for _ in range(n)]
    input_in, memory_in = take(2)
    pairs = take(len(widths))
    parts = take(2)
    input_out, memory_out = take(2)
    outs = [take(len(group)) for group in widths]
    gate_out, up_out, down_out = take(3)
    core = lax.axis_index("tp") % 2
    for source, target in ((input_in, input_out), (memory_in, memory_out)):
        for r in range(source.shape[0]):
            target[r] = source[r].astype(f32)
    for pair, group, targets in zip(pairs, widths, outs):
        offset = 0
        for width, target in zip(group, targets):
            half = width // 2
            for place in range(2):
                columns = pl.ds(pl.multiple_of((core + place) % 2 * half, half), half)
                target[:, columns] = pair[place, :, offset : offset + half]
            offset += half
    first = parts[0].shape[1]
    for m, target in enumerate((gate_out, up_out, down_out)):
        target[:first, :] = parts[0][m]
        target[first:, :] = parts[1][m]


def finish(input_rows, memory_rows, pairs, widths, parts):
    of = jax.ShapeDtypeStruct
    rows, columns = parts[0].shape[1] + parts[1].shape[1], parts[0].shape[2]
    out_shape = [of(input_rows.shape, f32), of(memory_rows.shape, f32)]
    for pair, group in zip(pairs, widths):
        out_shape += [of((pair.shape[1], width), f32) for width in group]
    out_shape += [of((rows, columns), f32)] * 3
    return pl.pallas_call(
        functools.partial(finish_kernel, widths),
        out_shape=out_shape,
        in_specs=[whole_vmem()] * (4 + len(pairs)),
        out_specs=[whole_vmem()] * len(out_shape),
        compiler_params=params(62),
        name="finish",
    )(input_rows, memory_rows, *pairs, *parts)


def on_device(
    inputs,
    memory,
    segments,
    memory_segments,
    gain_self,
    gain_cross,
    gain_ffn,
    relative_bias,
    self_query,
    self_key,
    self_value,
    self_out,
    cross_query,
    cross_key,
    cross_value,
    cross_out,
    ffn_gate,
    ffn_up,
    ffn_down,
    cotangent,
):
    rows, seq, features = inputs.shape
    mem_seq = memory.shape[1]
    at = Places(rows)
    tokens = rows * seq
    mem_tokens = rows * mem_seq
    key_width = GROUPS * HEAD_DIM
    width = features // at.dp
    d = lax.axis_index("dp")

    own_columns = lambda w: lax.dynamic_slice_in_dim(w, d * width, width, 1)
    own_rows = lambda w: lax.dynamic_slice_in_dim(w, d * width, width, 0).T
    own_piece = [own_rows(ffn_gate), own_rows(ffn_up), own_columns(ffn_down)]
    segs = jnp.zeros((rows, 8, BLOCK), jnp.int32)
    segs = segs.at[:, 0, :].set(segments).at[:, 1, :mem_seq].set(memory_segments)

    table = relative_bias.reshape(-1)
    done = forward(
        at,
        inputs,
        memory,
        cotangent,
        segs,
        own_piece,
        [
            self_query,
            self_key,
            self_value,
            self_out,
            cross_query,
            cross_key,
            cross_value,
            cross_out,
        ],
        [gain.reshape(1, -1) for gain in (gain_self, gain_cross, gain_ffn)],
        table,
    )
    x_low, held_self, queries, kvs = done.x, done.held_self, done.queries, done.kvs
    self_context, self_log, stream_one = done.self_context, done.self_log, done.stream_one
    held_cross, cross_queries, mem = done.held_cross, done.cross_queries, done.mem
    mem_kvs, cross_context, cross_log = done.mem_kvs, done.cross_context, done.cross_log
    stream_two, held_ffn, cot = done.stream_two, done.held_ffn, done.cot
    self_features, mem_features = done.self_features, done.mem_features
    seg_row, tiles = done.seg_row, done.tiles

    ffn_operands = (held_ffn, done.held_other, cot, done.cot_other, done.gathered)
    first_span, second_span = ffn_parts(done.gathered.shape[3])
    *ffn_sums, ffn_grads_first = ffn(at, first_span, *ffn_operands)
    ffn_out, ffn_back, ffn_grads_second, ffn_first = ffn(
        at, second_span, *ffn_operands, ffn_sums, ffn_grads_first
    )
    grad_stream, gain_ffn_part = norm_back(stream_two, gain_ffn, ffn_back.astype(f32))
    grad_two = cot.astype(f32) + grad_stream
    output = (stream_two + ffn_out.astype(f32)).astype(bf16)
    output = output.reshape(rows, seq, features)

    cross_branch = grad_two.astype(bf16)
    grad_cross_context = nt(cross_branch, cross_out).astype(bf16)
    grad_cross_queries, *grad_mem_kvs, ffn_second, output = cross_backward(
        at,
        cross_queries,
        mem_kvs,
        mem_features,
        seg_row,
        cross_log,
        grad_cross_context,
        ffn_grads_second,
        output,
    )

    def gathered_grads(parts):
        total = parts[0].astype(f32)
        for s in range(1, at.share):
            total = total + lax.ppermute(
                parts[s], "tp", at.part_perm(at.share - s)
            ).astype(f32)
        return total[0].astype(bf16), total[1].astype(bf16)

    grad_mem_keys, grad_mem_values = gathered_grads(grad_mem_kvs)
    grad_stream, gain_cross_part = norm_back(
        stream_one, gain_cross, nt(grad_cross_queries, cross_query)
    )
    grad_one = grad_two + grad_stream
    self_branch = grad_one.astype(bf16)
    grad_self_context = nt(self_branch, self_out).astype(bf16)
    memory_grad = (nt(grad_mem_keys, cross_key) + nt(grad_mem_values, cross_value)).astype(bf16)
    memory_grad = memory_grad.reshape(rows, mem_seq, features)
    middle_products = weight_products(
        at,
        [
            (cross_context, cross_branch),
            (held_cross, grad_cross_queries),
            (self_context, self_branch),
            (mem, grad_mem_keys),
            (mem, grad_mem_values),
        ],
    )
    grad_self_context, middle_products = lax.optimization_barrier(
        (grad_self_context, middle_products)
    )
    (
        *products,
        grad_rows,
        gain_self_part,
        relative_part,
        ffn_first,
        ffn_second,
        memory_rows,
    ) = self_backward(
        at,
        held_self,
        queries,
        kvs,
        self_features,
        seg_row,
        self_log,
        grad_self_context,
        tiles,
        table,
        x_low,
        grad_one,
        gain_self.reshape(1, -1),
        (self_query, self_key, self_value),
        middle_products,
        (ffn_first, ffn_second),
        memory_grad,
    )
    small = jnp.concatenate(
        [gain_self_part, gain_cross_part, gain_ffn_part, jnp.zeros((1, features), f32), relative_part]
    )
    input_rows, small, middle_pair, last_pair = tail(
        at, grad_rows, products[:2], products[2:], small
    )
    wide, narrow = features, key_width
    (
        input_grad,
        memory_grad,
        cross_out_grad,
        cross_query_grad,
        self_out_grad,
        cross_key_grad,
        cross_value_grad,
        self_query_grad,
        self_key_grad,
        self_value_grad,
        ffn_gate_grad,
        ffn_up_grad,
        ffn_down_grad,
    ) = finish(
        input_rows,
        memory_rows,
        (middle_pair, last_pair),
        ((wide, wide, wide, narrow, narrow), (wide, narrow, narrow)),
        (ffn_first, ffn_second),
    )
    shards = at.dp * at.tp
    shard = lax.axis_index("dp") * at.tp + lax.axis_index("tp")
    share_of = lambda vector: lax.dynamic_slice_in_dim(
        vector, shard * (vector.size // shards), vector.size // shards
    )
    relative = small[4:8].reshape(4, -1, BLOCK)[:, : HEADS // 4, :BUCKETS]
    return (
        output,
        input_grad,
        memory_grad,
        share_of(small[0]),
        share_of(small[1]),
        share_of(small[2]),
        share_of(relative.transpose(2, 1, 0).reshape(-1)),
        self_query_grad,
        self_key_grad,
        self_value_grad,
        self_out_grad,
        cross_query_grad,
        cross_key_grad,
        cross_value_grad,
        cross_out_grad,
        ffn_gate_grad.T,
        ffn_up_grad.T,
        ffn_down_grad,
    )


def solution(mesh):
    placed = (
        P("dp", "tp", None),
        P("dp", "tp", None),
        P("dp", "tp"),
        P("dp", "tp"),
        P(),
        P(),
        P(),
        P(),
        P(),
        P(),
        P(),
        P(),
        P(),
        P(),
        P(),
        P(),
        P(None, "tp"),
        P(None, "tp"),
        P("tp", None),
        P("dp", "tp", None),
    )
    return jax.shard_map(
        on_device,
        mesh=mesh,
        in_specs=placed,
        out_specs=(
            P("dp", "tp", None),
            P("dp", "tp", None),
            P("dp", "tp", None),
            P(("dp", "tp")),
            P(("dp", "tp")),
            P(("dp", "tp")),
            P(("dp", "tp")),
            P(("dp", "tp"), None),
            P(("dp", "tp"), None),
            P(("dp", "tp"), None),
            P(("dp", "tp"), None),
            P(("dp", "tp"), None),
            P(("dp", "tp"), None),
            P(("dp", "tp"), None),
            P(("dp", "tp"), None),
            P("dp", "tp"),
            P("dp", "tp"),
            P("tp", "dp"),
        ),
        check_vma=False,
    )
```

```python
import functools
import math
import types
import typing

import jax
import jax.numpy as jnp
from jax import lax
from jax.experimental import pallas as pl
from jax.experimental.pallas import tpu as pltpu
from jax.sharding import PartitionSpec as P

HEADS = 16
HEAD_DIM = 64
GROUPS = 8
BUCKETS = 32
MAX_DIST = 128
BLOCK = 128
PAIRS = GROUPS // 2
FAR = -1e30
SCALE = HEAD_DIM ** (-0.5)
MIB = 1 << 20

norm_epsilon = 1e-06
f32 = jnp.float32
bf16 = jnp.bfloat16


def nn(left, right):
    return lax.dot_general(left, right, (((1,), (0,)), ((), ())), preferred_element_type=f32)


def nt(left, right):
    return lax.dot_general(left, right, (((1,), (1,)), ((), ())), preferred_element_type=f32)


def tn(left, right):
    return lax.dot_general(left, right, (((0,), (0,)), ((), ())), preferred_element_type=f32)


def bits_of(count):
    return count.bit_length() - 1


def xor_static(value, flips, count):
    result = value
    for bit in range(bits_of(count)):
        if flips >> bit & 1:
            result = result + (1 << bit) * (1 - 2 * ((value // (1 << bit)) % 2))
    return result


def half_order(count, first_low):
    nb = bits_of(count)
    bits = list(range(nb)) if first_low else list(range(nb))[::-1]
    order = []
    for index in range(count):
        s = 0
        for place, bit in enumerate(bits):
            if index >> (nb - 1 - place) & 1:
                s |= 1 << bit
        order.append(s)
    return order, bits


def norm_scale(v):
    return lax.rsqrt(jnp.mean(v * v, axis=-1, keepdims=True) + norm_epsilon)


def norm_back(v, gain, dy):
    s = norm_scale(v)
    gained = dy * gain
    grad = s * gained - v * (s * s * s * jnp.mean(gained * v, axis=-1, keepdims=True))
    return grad, jnp.sum(dy * v * s, axis=0, keepdims=True)


def bucket_of(distance):
    exact = BUCKETS // 2
    bucket_count = jnp.zeros_like(distance)
    for step_index in range(1, exact):
        threshold = math.ceil(exact * (MAX_DIST / exact) ** (step_index / exact))
        bucket_count = bucket_count + (distance >= threshold).astype(jnp.int32)
    return jnp.where(distance < exact, distance, exact + bucket_count)


def whole_vmem():
    return pl.BlockSpec(memory_space=pltpu.VMEM)


def whole_smem():
    return pl.BlockSpec(memory_space=pltpu.SMEM)


def any_space():
    return pl.BlockSpec(memory_space=pl.ANY)


def params(limit_mib, **more):
    return pltpu.CompilerParams(vmem_limit_bytes=limit_mib * MIB, **more)


class Places:
    def __init__(self, rows):
        self.tp = lax.axis_size("tp")
        self.dp = lax.axis_size("dp")
        self.rows = rows
        self.share = self.tp // rows
        self.z_count = self.tp // 2

    def row(self):
        return lax.axis_index("tp") // self.share

    def part(self):
        return lax.axis_index("tp") % self.share

    def row_perm(self, k):
        share = self.share
        return [(t, ((t // share) ^ k) * share + t % share) for t in range(self.tp)]

    def part_perm(self, shift):
        share = self.share
        return [
            (t // share * share + (t % share + shift) % share, t) for t in range(self.tp)
        ]

    def core_perm(self):
        return [(t, t ^ 1) for t in range(self.tp)]

    def z_perm(self, shift):
        z_count = self.z_count
        return [(t, (t // 2 + shift) % z_count * 2 + t % 2) for t in range(self.tp)]

    def dp_perm(self, flips):
        return [(d, d ^ flips) for d in range(self.dp)]


def near_kinds(share):
    kinds = [(s, 0) for s in range(share)]
    return kinds + [(s, 1) for s in range(share) if s > 0 or share == 1]


def kind_distance(at, kind):
    s, back = kind
    part = at.part()
    return part - (part + s) % at.share + at.share * back


def tile_distance(at, kind):
    key = lax.broadcasted_iota(jnp.int32, (BLOCK, BLOCK), 0)
    query = lax.broadcasted_iota(jnp.int32, (BLOCK, BLOCK), 1)
    return BLOCK * kind_distance(at, kind) + query - key


def fill_bias_tiles(at, table, tiles):
    kinds = near_kinds(at.share)

    def one_group(group, carry):
        for number, kind in enumerate(kinds):
            distance = tile_distance(at, kind)
            bucket = bucket_of(jnp.maximum(distance, 0))
            for j in range(2):
                head = group * 2 + j
                last = table[(BUCKETS - 1) * HEADS + head]
                value = jnp.zeros((BLOCK, BLOCK), f32)
                for b in range(BUCKETS - 1):
                    value = jnp.where(bucket == b, table[b * HEADS + head] - last, value)
                tiles[group, number, :, j * BLOCK : (j + 1) * BLOCK] = jnp.where(
                    distance < 0, FAR, value
                )
        return carry

    lax.fori_loop(0, GROUPS, one_group, 0)


def query_features(seg_block, table, group):
    shape = (HEAD_DIM, 2 * BLOCK)
    row = lax.broadcasted_iota(jnp.int32, shape, 0)
    seg = jnp.concatenate([seg_block, seg_block], axis=1)
    feature = jnp.where((row < 3) & (seg != row), FAR, 0.0)
    if table is not None:
        lane = lax.broadcasted_iota(jnp.int32, shape, 1)
        far = (BUCKETS - 1) * HEADS + group * 2
        rest = jnp.where(lane < BLOCK, table[far], table[far + 1])
        for part in range(3):
            rounded = rest.astype(bf16).astype(f32)
            feature = jnp.where(row == 3 + part, rounded, feature)
            rest = rest - rounded
    return feature.astype(bf16)


def turned(block):
    return block.astype(f32).T.astype(block.dtype)


def stacked_heads(pair):
    t = turned(pair)
    return jnp.concatenate([t[:HEAD_DIM], t[HEAD_DIM:]], axis=1)


def unstacked_heads(wide):
    return jnp.concatenate([wide[:, :BLOCK], wide[:, BLOCK:]], axis=0).T


def with_other(half, other, odd):
    return jnp.concatenate([other, half] if odd else [half, other], axis=0)


def fold_rows(tile):
    return tile.reshape(tile.shape[0] // 8, 8, tile.shape[1])


class Keys:
    def __init__(self, share, blocks, causal):
        self.share, self.blocks, self.causal = share, blocks, causal
        self.count = share * blocks

    def blocks_for(self, i):
        return (i + 1 if self.causal else self.blocks) * self.share

    def near(self, i, index, kinds):
        if not self.causal:
            return None
        j, s = divmod(index, self.share)
        kind = (s, i - j)
        return kinds.index(kind) if kind in kinds else None


def load_keys(keys, k_refs, feat_refs, odd, kaug):
    lane = lax.broadcasted_iota(jnp.int32, (BLOCK, 2 * HEAD_DIM), 1)
    own = (lane >= HEAD_DIM) if odd else (lane < HEAD_DIM)
    for index in range(keys.count):
        j, s = divmod(index, keys.share)
        rows = pl.ds(j * BLOCK, BLOCK)
        kaug[pl.ds(index * BLOCK, BLOCK), :] = jnp.where(
            own, k_refs[s][rows, :].astype(f32), feat_refs[s][rows, :].astype(f32)
        ).astype(bf16)


def turn_keys(keys, refs, target):
    for index in range(keys.count):
        j, s = divmod(index, keys.share)
        target[:, pl.ds(index * BLOCK, BLOCK)] = turned(refs[s][pl.ds(j * BLOCK, BLOCK), :])


def forward_pair(
    keys, kinds, pair, q_ref, seg_ref, kv_refs, feat_refs, tiles, last_parts, ctx_ref, log_ref, scratch
):
    kaug, vt, sbuf, pbuf = scratch
    lanes_at = lambda start, width: pl.ds(pl.multiple_of(start, BLOCK), width)
    k_refs = [ref.at[:, lanes_at(pair * BLOCK, BLOCK)] for ref in kv_refs]
    v_refs = [
        ref.at[:, lanes_at(GROUPS * HEAD_DIM + pair * BLOCK, BLOCK)] for ref in kv_refs
    ]
    turn_keys(keys, v_refs, vt)
    for gi in range(2):
        load_keys(keys, k_refs, feat_refs, gi, kaug)
        for i in range(q_ref.shape[0] // BLOCK):
            tokens = pl.ds(i * BLOCK, BLOCK)
            lanes = lanes_at((pair * 2 + gi) * BLOCK, BLOCK)
            features = query_features(seg_ref[:, tokens], last_parts, pair * 2 + gi)
            right = with_other(stacked_heads(q_ref[tokens, lanes]), features, gi)
            count = keys.blocks_for(i)
            top = jnp.full((8, 2 * BLOCK), -jnp.inf, f32)
            for index in range(count):
                rows = pl.ds(index * BLOCK, BLOCK)
                scores = nn(kaug[rows, :], right)
                near = keys.near(i, index, kinds)
                if near is not None:
                    scores = scores + tiles[pair * 2 + gi, near]
                sbuf[rows, :] = scores
                top = jnp.maximum(top, jnp.max(fold_rows(scores), axis=0))
            top = jnp.max(top, axis=0, keepdims=True)
            total = jnp.zeros((8, 2 * BLOCK), f32)
            for index in range(count):
                rows = pl.ds(index * BLOCK, BLOCK)
                exponent = jnp.exp(sbuf[rows, :] - top)
                total = total + jnp.sum(fold_rows(exponent), axis=0)
                pbuf[rows, :] = exponent.astype(bf16)
            total = jnp.sum(total, axis=0, keepdims=True)
            length = count * BLOCK
            context = nn(vt[pl.ds(gi * HEAD_DIM, HEAD_DIM), :length], pbuf[:length, :])
            ctx_ref[tokens, lanes] = unstacked_heads(context * (1.0 / total)).astype(bf16)
            log_ref[pair * 2 + gi, pl.ds(i, 1), :] = top + jnp.log(total)


def diagonal_sums(tile):
    row = lax.broadcasted_iota(jnp.int32, (BLOCK, BLOCK), 0)
    lane = lax.broadcasted_iota(jnp.int32, (BLOCK, BLOCK), 1)
    turn = (row + lane == BLOCK - 1).astype(f32).astype(bf16)
    high = tile.astype(bf16)
    rest = tile - high.astype(f32)
    mid = rest.astype(bf16)
    low = (rest - mid.astype(f32)).astype(bf16)
    turned_rows = nn(turn, high) + nn(turn, mid) + nn(turn, low)
    sums = []
    for j in range(2):
        part = turned_rows[:, j * BLOCK : (j + 1) * BLOCK]
        wide = jnp.concatenate([part, jnp.zeros_like(part)], axis=1)
        rolled = pltpu.roll(wide, 0, 1, stride=1, stride_axis=0)
        sums.append(jnp.sum(rolled, axis=0, keepdims=True))
    return jnp.concatenate(sums, axis=0)


def backward_body(
    keys,
    kinds,
    pair,
    q_ref,
    seg_ref,
    k_refs,
    v_refs,
    feat_refs,
    tiles,
    last_parts,
    log_ref,
    dctx_ref,
    dq_ref,
    dkv_refs,
    diagonals,
    dfar,
    scratch,
):
    kaug, kt, vn, sbuf, pbuf, gbuf, dk_acc, dv_acc, dtiles = scratch
    turn_keys(keys, k_refs, kt)
    for index in range(keys.count):
        j, s = divmod(index, keys.share)
        vn[pl.ds(index * BLOCK, BLOCK), :] = v_refs[s][pl.ds(j * BLOCK, BLOCK), :]
    for gi in range(2):
        load_keys(keys, k_refs, feat_refs, gi, kaug)
        group_rows = pl.ds(gi * HEAD_DIM, HEAD_DIM)
        seen = set()
        far = jnp.zeros((8, 2 * BLOCK), f32)
        n_blocks = q_ref.shape[0] // BLOCK
        for i in reversed(range(n_blocks)):
            tokens = pl.ds(i * BLOCK, BLOCK)
            lanes = pl.ds(gi * BLOCK, BLOCK)
            features = query_features(seg_ref[:, tokens], last_parts, pair * 2 + gi)
            queries = stacked_heads(q_ref[tokens, lanes])
            right = with_other(queries, features, gi)
            grads = stacked_heads(dctx_ref[tokens, lanes])
            grads_right = with_other(grads, jnp.zeros_like(grads), gi)
            logsum = log_ref[gi, pl.ds(i, 1), :]
            count = keys.blocks_for(i)
            middle = jnp.zeros((8, 2 * BLOCK), f32)
            for index in range(count):
                rows = pl.ds(index * BLOCK, BLOCK)
                scores = nn(kaug[rows, :], right)
                near = keys.near(i, index, kinds)
                if near is not None:
                    scores = scores + tiles[gi, near]
                probs = jnp.exp(scores - logsum)
                grad_probs = nn(vn[rows, :], grads_right)
                middle = middle + jnp.sum(fold_rows(probs * grad_probs), axis=0)
                sbuf[rows, :] = probs
                gbuf[rows, :] = grad_probs
                pbuf[rows, :] = probs.astype(bf16)
            middle = jnp.sum(middle, axis=0, keepdims=True)
            length = count * BLOCK
            grad_v = nt(grads, pbuf[:length, :])
            for index in range(count):
                rows = pl.ds(index * BLOCK, BLOCK)
                grad_scores = (sbuf[rows, :] * (gbuf[rows, :] - middle)).astype(bf16)
                pbuf[rows, :] = grad_scores
                if keys.causal:
                    wide = grad_scores.astype(f32)
                    near = keys.near(i, index, kinds)
                    if near is None:
                        far = far + jnp.sum(fold_rows(wide), axis=0)
                    elif near in seen:
                        dtiles[near] = dtiles[near] + wide
                    else:
                        dtiles[near] = wide
                        seen.add(near)
            grad_k = nt(queries, pbuf[:length, :])
            grad_q = nn(kt[group_rows, :length], pbuf[:length, :])
            dq_ref[tokens, lanes] = unstacked_heads(grad_q * SCALE).astype(bf16)
            if i == n_blocks - 1:
                dk_acc[group_rows, :length] = grad_k
                dv_acc[group_rows, :length] = grad_v
            else:
                dk_acc[group_rows, :length] += grad_k
                dv_acc[group_rows, :length] += grad_v
        if keys.causal:
            dfar[gi] = far
            for near in range(len(kinds)):
                diagonals[gi, 2 * near : 2 * near + 2, :] = diagonal_sums(dtiles[near])
    for index in range(keys.count):
        j, s = divmod(index, keys.share)
        columns = pl.ds(index * BLOCK, BLOCK)
        rows = pl.ds(j * BLOCK, BLOCK)
        dkv_refs[s][0, rows, :] = dk_acc[:, columns].T.astype(bf16)
        dkv_refs[s][1, rows, :] = dv_acc[:, columns].T.astype(bf16)


class DpSum:
    def __init__(self, at):
        self.at = at
        self.bits = [half_order(at.dp, half == 0)[1] for half in range(2)]
        self.d = lax.axis_index("dp")

    def held(self, half, step):
        gone = self.bits[half][:step]
        return [s for s in range(self.at.dp) if not any(s >> bit & 1 for bit in gone)]

    def sent(self, half, step):
        bit = self.bits[half][step]
        return [(s, s ^ 1 << bit) for s in self.held(half, step) if s >> bit & 1]

    def count(self, step):
        return len(self.held(0, step))

    def partner(self, half, step):
        return xor_static(self.d, 1 << self.bits[half][step], self.at.dp)

    def copies(self, step, source_of, landing, sems):
        made = []
        for half in range(2):
            for sent, joined in self.sent(half, step):
                slot = self.held(half, step + 1).index(joined)
                made.append(
                    remote(
                        source_of(half, sent),
                        landing.at[half, slot],
                        sems,
                        half * self.count(step + 1) + slot,
                        "dp",
                        self.partner(half, step),
                    )
                )
        return made


def first_step_scratch(at, half_shape):
    return [
        pltpu.VMEM(half_shape, bf16),
        pltpu.VMEM(half_shape, bf16),
        pltpu.SemaphoreType.DMA((at.dp,)),
        pltpu.SemaphoreType.DMA((at.dp,)),
        pltpu.SemaphoreType.DMA((at.dp,)),
    ]


def half_shape_of(at, grads):
    return (2, at.dp // 2, at.z_count // 2, *grads.shape[2:])


class FirstStep:
    BUFFERS = 5

    def __init__(self, at, source, out, buffers):
        self.at, self.source, self.out = at, source, out
        self.landing, self.own, *self.sems, self.own_sems = buffers

    def copies(self):
        total = DpSum(self.at)
        half_z = self.at.z_count // 2
        entry = lambda half, s: self.source.at[
            xor_static(total.d, s, self.at.dp), pl.ds(half * half_z, half_z)
        ]
        made = total.copies(0, entry, self.landing, self.sems)
        for half in range(2):
            for slot, s in enumerate(total.held(half, 1)):
                made.append(
                    pltpu.make_async_copy(
                        entry(half, s),
                        self.own.at[half, slot],
                        self.own_sems.at[half * total.count(1) + slot],
                    )
                )
        return made

    def start(self):
        for copy in self.copies():
            copy.start()

    def end(self):
        for copy in self.copies():
            copy.wait()
        for half in range(2):
            for slot in range(self.at.dp // 2):
                for chunk in range(self.at.z_count // 2):
                    for m in range(3):
                        self.out[half, slot, chunk, m] = (
                            self.own[half, slot, chunk, m] + self.landing[half, slot, chunk, m]
                        )


def cross_backward_kernel(at, keys, *refs):
    refs = list(refs)
    take = lambda n: [refs.pop(0) for _ in range(n)]
    q_ref, seg_ref = take(2)
    k_refs, v_refs, feat_refs = take(keys.share), take(keys.share), take(keys.share)
    log_ref, dctx_ref, ffn_in, output_in = take(4)
    (dq_ref,) = take(1)
    dkv_refs = take(keys.share)
    ffn_out, output_out = take(2)
    first = FirstStep(at, ffn_in, ffn_out, take(FirstStep.BUFFERS))
    return_buffers = take(RowReturn.BUFFERS)

    @pl.when(pl.program_id(0) == 0)
    def _():
        greet(at)
        first.start()
        RowReturn(at, output_in, output_out, return_buffers).start()

    backward_body(
        keys,
        None,
        pl.program_id(0),
        q_ref,
        seg_ref,
        k_refs,
        v_refs,
        feat_refs,
        None,
        None,
        log_ref,
        dctx_ref,
        dq_ref,
        dkv_refs,
        None,
        None,
        (*refs, None),
    )

    @pl.when(pl.program_id(0) == PAIRS - 1)
    def _():
        first.end()
        RowReturn(at, output_in, output_out, return_buffers).end()


def backward_scratch(length):
    return [
        pltpu.VMEM((length, 2 * HEAD_DIM), bf16),
        pltpu.VMEM((2 * HEAD_DIM, length), bf16),
        pltpu.VMEM((length, 2 * HEAD_DIM), bf16),
        pltpu.VMEM((length, 2 * BLOCK), f32),
        pltpu.VMEM((length, 2 * BLOCK), bf16),
        pltpu.VMEM((length, 2 * BLOCK), f32),
        pltpu.VMEM((2 * HEAD_DIM, length), f32),
        pltpu.VMEM((2 * HEAD_DIM, length), f32),
    ]


def cross_backward(
    at, queries, key_values, features, seg_row, logsum, grad_context, ffn_grads, output
):
    tokens = queries.shape[0]
    span = key_values[0].shape[0]
    blocks = tokens // BLOCK
    keys = Keys(at.share, span // BLOCK, False)
    length = keys.count * BLOCK
    work = blocks * length * 2 * BLOCK * GROUPS
    token_spec = pl.BlockSpec((tokens, 2 * BLOCK), lambda p: (0, p))
    specs = [token_spec, pl.BlockSpec(seg_row.shape, lambda p: (0, 0))]
    specs += [pl.BlockSpec((span, BLOCK), lambda p: (0, p))] * at.share
    specs += [pl.BlockSpec((span, BLOCK), lambda p: (0, PAIRS + p))] * at.share
    specs += [pl.BlockSpec((span, BLOCK), lambda p: (0, 0))] * at.share
    specs += [pl.BlockSpec((2, blocks, 2 * BLOCK), lambda p: (p, 0, 0)), token_spec]
    specs += [any_space()] * 2
    half_shape = half_shape_of(at, ffn_grads)
    return pl.pallas_call(
        functools.partial(cross_backward_kernel, at, keys),
        grid=(PAIRS,),
        out_shape=[jax.ShapeDtypeStruct((tokens, HEADS * HEAD_DIM), bf16)]
        + [jax.ShapeDtypeStruct((2, span, GROUPS * HEAD_DIM), bf16)] * at.share
        + [jax.ShapeDtypeStruct(half_shape, bf16), jax.ShapeDtypeStruct(output.shape, bf16)],
        in_specs=specs,
        out_specs=[token_spec]
        + [pl.BlockSpec((2, span, BLOCK), lambda p: (0, 0, p))] * at.share
        + [whole_vmem()] * 2,
        scratch_shapes=[
            *first_step_scratch(at, half_shape),
            *RowReturn.scratch(at, output),
            *backward_scratch(length),
        ],
        compiler_params=params(48, collective_id=4, has_side_effects=True),
        cost_estimate=pl.CostEstimate(
            flops=work * 1024, bytes_accessed=16 * MIB, transcendentals=work
        ),
        name="cross_backward",
    )(
        queries,
        seg_row,
        *key_values,
        *key_values,
        *features,
        logsum,
        grad_context,
        ffn_grads,
        output,
    )


def remote(source, target, sems, number, axis, index):
    send, receive = sems
    return pltpu.make_async_remote_copy(
        src_ref=source,
        dst_ref=target,
        send_sem=send.at[number],
        recv_sem=receive.at[number],
        device_id={axis: index},
        device_id_type=pl.DeviceIdType.MESH,
    )


def tp_at(at, z):
    return z * 2 + lax.axis_index("tp") % 2


def other_core():
    t = lax.axis_index("tp")
    return t + 1 - 2 * (t % 2)


def greet(at):
    barrier = pltpu.get_barrier_semaphore()
    t, d = lax.axis_index("tp"), lax.axis_index("dp")
    if at.share == 2:
        others = [other_core()]
        others += [tp_at(at, (t // 2 + k) % at.z_count) for k in range(1, at.z_count)]
    else:
        others = [(t + k) % at.tp for k in range(1, at.tp)]
    targets = [{"tp": other} for other in others]
    targets += [{"dp": xor_static(d, 1 << bit, at.dp)} for bit in range(bits_of(at.dp))]
    for target in targets:
        pl.semaphore_signal(
            barrier, inc=1, device_id=target, device_id_type=pl.DeviceIdType.MESH
        )
    pl.semaphore_wait(barrier, len(targets))


def key_feature_tile(seg_line):
    column = jnp.broadcast_to(seg_line.astype(f32), (BLOCK, BLOCK)).T
    lane = lax.broadcasted_iota(jnp.int32, (BLOCK, BLOCK), 1) % HEAD_DIM
    same = jnp.where(column == lane.astype(f32), 1.0, 0.0)
    ones = jnp.where(lane < 6, 1.0, 0.0)
    return jnp.where(lane < 3, same, ones).astype(bf16)


def forward_messages(at):
    names = [(kind, k) for k in range(1, at.rows) for kind in ("x", "seg", "mem", "cot")]
    names += [(kind, s) for s in range(1, at.share) for kind in ("seg_part", "kv", "mem_kv")]
    names += [("ring", k) for k in range(1, at.z_count)]
    names += [("w", k, s) for k in range(at.z_count) for s in range(1, at.dp)]
    names += [("cot_core",), ("held",)]
    return {name: number for number, name in enumerate(names)}


class Gather:
    def __init__(self, at, start, copies, flush, own, gathered, out):
        self.at, self.start, self.copies, self.flush = at, start, copies, flush
        self.own, self.gathered, self.out = own, gathered, out
        self.z, self.d = lax.axis_index("tp") // 2, lax.axis_index("dp")

    def order(self, k):
        return half_order(self.at.dp, k % 2 == 0)[1]

    def held(self, k, s):
        return self.own if (k, s) == (0, 0) else self.gathered.at[k, s]

    def pass_on(self, k, s):
        bits = self.order(k)
        seen = [place for place, bit in enumerate(bits) if s >> bit & 1]
        for bit in bits[max(seen) + 1 if seen else 0 :]:
            self.start(
                ("w", k, s | 1 << bit),
                self.held(k, s),
                self.gathered.at[k, s | 1 << bit],
                "dp",
                xor_static(self.d, 1 << bit, self.at.dp),
            )

    def ring(self, k):
        self.start(
            ("ring", k),
            self.held(k - 1, 0),
            self.gathered.at[k, 0],
            "tp",
            tp_at(self.at, (self.z + 1) % self.at.z_count),
        )

    def arrived(self, k, s):
        self.copies["w", k, s].wait()
        self.flush(self.gathered.at[k, s], self.out.at[k, s])

    def arrive_ring(self, k):
        self.copies["ring", k].wait()
        self.flush(self.gathered.at[k, 0], self.out.at[k, 0])
        if k + 1 < self.at.z_count:
            self.ring(k + 1)
        self.pass_on(k, 0)

    def relay(self, k):
        bits = self.order(k)
        held = [0]
        for bit in bits[:-1]:
            for s in list(held):
                self.arrived(k, s | 1 << bit)
                self.pass_on(k, s | 1 << bit)
                held.append(s | 1 << bit)

    def finish(self, k):
        last = self.order(k)[-1]
        for s in range(self.at.dp):
            if s >> last & 1:
                self.arrived(k, s)


class Kept(typing.NamedTuple):
    x: typing.Any
    held_self: typing.Any
    queries: typing.Any
    kv: typing.Any
    self_context: typing.Any
    self_log: typing.Any
    stream_one: typing.Any
    held_cross: typing.Any
    cross_queries: typing.Any
    mem: typing.Any
    mem_kv: typing.Any
    cross_context: typing.Any
    cross_log: typing.Any
    stream_two: typing.Any
    held_ffn: typing.Any
    tiles: typing.Any
    seg_row: typing.Any


def forward_kernel(at, shapes, *refs):
    refs = list(refs)
    take = lambda n: [refs.pop(0) for _ in range(n)]
    inputs, memory, cot_in, segs = take(4)
    piece_parts = take(3)
    weight_refs = take(8)
    *gains, table = take(4)
    outs = Kept(*take(len(Kept._fields)))
    feat_outs, mem_feat_outs = take(at.share), take(at.share)
    kv_outs, mem_kv_outs = take(at.share - 1), take(at.share - 1)
    cot_out, cot_other_out, held_other_out, gathered_out = take(4)
    bufs = Kept(*take(len(Kept._fields)))
    feats, mem_feats = take(at.share), take(at.share)
    kv_others, mem_kv_others = take(at.share - 1), take(at.share - 1)
    weights = take(8)
    cot, cot_other, held_other, piece, gathered = take(5)
    seg_buf, seg_others, kaug, vt, sbuf, pbuf = take(6)
    send_sems, recv_sems, load_sems, flush_sems = take(4)
    scratch = (kaug, vt, sbuf, pbuf)
    numbers = forward_messages(at)
    kinds = near_kinds(at.share)
    row, part = at.row(), at.part()
    z = lax.axis_index("tp") // 2
    seq, features = inputs.shape[1:]
    mem_seq = memory.shape[1]
    tokens, mem_tokens = at.rows * seq, at.rows * mem_seq
    key_width = GROUPS * HEAD_DIM
    copies, flushes = {}, []

    def start(name, source, target, axis, index):
        copies[name] = remote(source, target, (send_sems, recv_sems), numbers[name], axis, index)
        copies[name].start()

    def start_rows(kind, source, target, height):
        for k in range(1, at.rows):
            there = xor_static(row, k, at.rows)
            start(
                (kind, k),
                source.at[there],
                target.at[pl.ds(pl.multiple_of(row * height, height), height), :],
                "tp",
                there * at.share + part,
            )

    def start_parts(kind, source, targets):
        for s in range(1, at.share):
            start(
                (kind, s),
                source,
                targets[s - 1],
                "tp",
                row * at.share + (part + at.share - s) % at.share,
            )

    def wait(kind, count):
        for k in range(1, count):
            copies[kind, k].wait()

    def flush(source, target):
        copy = pltpu.make_async_copy(source, target, flush_sems.at[len(flushes)])
        flushes.append(copy)
        copy.start()
        return copy

    def local_rows(source, target, height, number):
        return pltpu.make_async_copy(
            source.at[row],
            target.at[pl.ds(pl.multiple_of(row * height, height), height), :],
            load_sems.at[number],
        )

    greet(at)
    start_rows("x", inputs, bufs.x, seq)
    for k in range(1, at.rows):
        there = xor_static(row, k, at.rows)
        start(
            ("seg", k), segs.at[there], seg_buf.at[row], "tp", there * at.share + part
        )
    for m in range(3):
        piece[m] = piece_parts[m][...]
    gather = Gather(at, start, copies, flush, piece, gathered, gathered_out)
    gather.pass_on(0, 0)
    loads = [local_rows(inputs, bufs.x, seq, 8), local_rows(memory, bufs.mem, mem_seq, 9)]
    loads += [
        local_rows(cot_in, cot, seq, 10),
        pltpu.make_async_copy(segs.at[row], seg_buf.at[row], load_sems.at[11]),
    ]
    weight_loads = [
        pltpu.make_async_copy(source, target, load_sems.at[number])
        for number, (source, target) in enumerate(zip(weight_refs, weights))
    ]
    for copy in loads + weight_loads:
        copy.start()
    for copy in loads:
        copy.wait()
    flush(piece, gathered_out.at[0, 0])
    fill_bias_tiles(at, table, bufs.tiles)
    flush(bufs.tiles, outs.tiles)
    wait("seg", at.rows)
    start_parts("seg_part", seg_buf, [seg_others.at[s] for s in range(at.share - 1)])
    wait("seg_part", at.share)
    for s in range(at.share):
        for i in range(at.rows):
            line = lambda j: seg_buf[i, j : j + 1, :] if s == 0 else seg_others[s - 1, i, j : j + 1, :]
            feats[s][i * seq : (i + 1) * seq, :] = key_feature_tile(line(0))
            mem_feats[s][i * mem_seq : (i + 1) * mem_seq, :] = key_feature_tile(line(1))[:mem_seq]
            if s == 0:
                bufs.seg_row[:, i * seq : (i + 1) * seq] = line(0)
        flush(feats[s], feat_outs[s])
        flush(mem_feats[s], mem_feat_outs[s])
    flush(bufs.seg_row, outs.seg_row)
    gather.relay(0)
    for copy in weight_loads:
        copy.wait()
    sq, sk, sv, so, cq, ck, cv, co = weights

    def blocks(height):
        step = min(256, height)
        return [pl.ds(first, step) for first in range(0, height, step)]

    def normed(value, number):
        return (value * norm_scale(value) * gains[number][...]).astype(bf16)

    wait("x", at.rows)
    gather.ring(1)
    flush(bufs.x, outs.x)
    for here in blocks(tokens):
        held = normed(bufs.x[here, :].astype(f32), 0)
        bufs.held_self[here, :] = held
        bufs.kv[here, :key_width] = nn(held, sk[...]).astype(bf16)
        bufs.kv[here, key_width:] = nn(held, sv[...]).astype(bf16)
    start_parts("kv", bufs.kv, kv_others)
    for here in blocks(tokens):
        bufs.queries[here, :] = (nn(bufs.held_self[here, :], sq[...]) * SCALE).astype(bf16)
    flush(bufs.held_self, outs.held_self)
    flush(bufs.kv, outs.kv)
    flush(bufs.queries, outs.queries)
    gather.arrive_ring(1)
    wait("kv", at.share)
    for s in range(at.share - 1):
        flush(kv_others[s], kv_outs[s])

    def self_pair(pair, carry):
        forward_pair(
            Keys(at.share, at.rows, True),
            kinds,
            pair,
            bufs.queries,
            bufs.seg_row,
            [bufs.kv, *kv_others],
            feats,
            bufs.tiles,
            table,
            bufs.self_context,
            bufs.self_log,
            scratch,
        )
        return carry

    start_rows("mem", memory, bufs.mem, mem_seq)
    lax.fori_loop(0, 2, self_pair, 0)
    if at.z_count > 2:
        gather.arrive_ring(2)
    gather.relay(1)
    lax.fori_loop(2, PAIRS, self_pair, 0)
    for k in range(3, at.z_count):
        gather.arrive_ring(k)
        gather.relay(k - 1)
    start_rows("cot", cot_in, cot, seq)
    wait("mem", at.rows)
    flush(bufs.mem, outs.mem)
    flush(bufs.self_context, outs.self_context)
    flush(bufs.self_log, outs.self_log)
    for here in blocks(mem_tokens):
        rows = bufs.mem[here, :]
        bufs.mem_kv[here, :key_width] = nn(rows, ck[...]).astype(bf16)
        bufs.mem_kv[here, key_width:] = nn(rows, cv[...]).astype(bf16)
    start_parts("mem_kv", bufs.mem_kv, mem_kv_others)
    flush(bufs.mem_kv, outs.mem_kv)
    for here in blocks(tokens):
        stream = bufs.x[here, :].astype(f32) + nn(bufs.self_context[here, :], so[...])
        bufs.stream_one[here, :] = stream
        held = normed(stream, 1)
        bufs.held_cross[here, :] = held
        bufs.cross_queries[here, :] = (nn(held, cq[...]) * SCALE).astype(bf16)
    flush(bufs.stream_one, outs.stream_one)
    flush(bufs.held_cross, outs.held_cross)
    flush(bufs.cross_queries, outs.cross_queries)

    wait("mem_kv", at.share)
    for s in range(at.share - 1):
        flush(mem_kv_others[s], mem_kv_outs[s])

    def cross_pair(pair, carry):
        forward_pair(
            Keys(at.share, mem_tokens // BLOCK, False),
            kinds,
            pair,
            bufs.cross_queries,
            bufs.seg_row,
            [bufs.mem_kv, *mem_kv_others],
            mem_feats,
            None,
            None,
            bufs.cross_context,
            bufs.cross_log,
            scratch,
        )
        return carry

    lax.fori_loop(0, 2, cross_pair, 0)
    gather.relay(at.z_count - 1)
    lax.fori_loop(2, PAIRS, cross_pair, 0)
    flush(bufs.cross_context, outs.cross_context)
    flush(bufs.cross_log, outs.cross_log)
    for here in blocks(tokens):
        stream = bufs.stream_one[here, :] + nn(bufs.cross_context[here, :], co[...])
        bufs.stream_two[here, :] = stream
        bufs.held_ffn[here, :] = normed(stream, 2)
    start(("held",), bufs.held_ffn, held_other, "tp", other_core())
    flush(bufs.stream_two, outs.stream_two)
    flush(bufs.held_ffn, outs.held_ffn)
    for k in range(at.z_count):
        gather.finish(k)
    wait("cot", at.rows)
    start(("cot_core",), cot, cot_other, "tp", other_core())
    flush(cot, cot_out)
    copies[("held",)].wait()
    flush(held_other, held_other_out)
    copies[("cot_core",)].wait()
    flush(cot_other, cot_other_out)
    for copy in flushes:
        copy.wait()


def forward(at, inputs, memory, cotangent, segs, piece_parts, weights, gains, table):
    seq, features = inputs.shape[1:]
    mem_seq = memory.shape[1]
    tokens, mem_tokens = at.rows * seq, at.rows * mem_seq
    key_width = GROUPS * HEAD_DIM
    of = jax.ShapeDtypeStruct
    wide = of((tokens, features), bf16)
    log = of((GROUPS, at.rows, 2 * BLOCK), f32)
    kv, mem_kv = of((tokens, 2 * key_width), bf16), of((mem_tokens, 2 * key_width), bf16)
    shapes = Kept(
        x=wide,
        held_self=wide,
        queries=wide,
        kv=kv,
        self_context=wide,
        self_log=log,
        stream_one=of((tokens, features), f32),
        held_cross=wide,
        cross_queries=wide,
        mem=of((mem_tokens, features), bf16),
        mem_kv=mem_kv,
        cross_context=wide,
        cross_log=log,
        stream_two=of((tokens, features), f32),
        held_ffn=wide,
        tiles=of((GROUPS, len(near_kinds(at.share)), BLOCK, 2 * BLOCK), f32),
        seg_row=of((1, tokens), jnp.int32),
    )
    buffered = list(shapes)
    buffered += [of((tokens, 2 * HEAD_DIM), bf16)] * at.share
    buffered += [of((mem_tokens, 2 * HEAD_DIM), bf16)] * at.share
    buffered += [kv] * (at.share - 1) + [mem_kv] * (at.share - 1)
    piece_shape = (3, *piece_parts[0].shape)
    gathered = of((at.z_count, at.dp, *piece_shape), bf16)
    length = max(tokens, mem_tokens) * at.share
    messages = len(forward_messages(at))
    results = pl.pallas_call(
        functools.partial(forward_kernel, at, shapes),
        out_shape=buffered + [wide, wide, wide, gathered],
        in_specs=[any_space()] * 4
        + [whole_vmem()] * 3
        + [any_space()] * 8
        + [whole_vmem()] * 3
        + [whole_smem()],
        out_specs=[any_space()] * (len(buffered) + 4),
        scratch_shapes=[pltpu.VMEM(shape.shape, shape.dtype) for shape in buffered]
        + [pltpu.VMEM(weight.shape, bf16) for weight in weights]
        + [pltpu.VMEM((tokens, features), bf16)] * 3
        + [
            pltpu.VMEM(piece_shape, bf16),
            pltpu.VMEM(gathered.shape, bf16),
            pltpu.VMEM((at.rows, 8, BLOCK), jnp.int32),
            pltpu.VMEM((at.share - 1, at.rows, 8, BLOCK), jnp.int32),
            pltpu.VMEM((length, 2 * HEAD_DIM), bf16),
            pltpu.VMEM((2 * HEAD_DIM, length), bf16),
            pltpu.VMEM((length, 2 * BLOCK), f32),
            pltpu.VMEM((length, 2 * BLOCK), bf16),
            pltpu.SemaphoreType.DMA((messages,)),
            pltpu.SemaphoreType.DMA((messages,)),
            pltpu.SemaphoreType.DMA((12,)),
            pltpu.SemaphoreType.DMA((len(buffered) + 3 + at.z_count * at.dp,)),
        ],
        compiler_params=params(60, collective_id=2, has_side_effects=True),
        cost_estimate=pl.CostEstimate(
            flops=40 * tokens * features * features,
            bytes_accessed=60 * MIB,
            transcendentals=0,
        ),
        name="forward",
    )(inputs, memory, cotangent, segs, *piece_parts, *weights, *gains, table)
    results = list(results)
    take = lambda n: [results.pop(0) for _ in range(n)]
    kept = Kept(*take(len(Kept._fields)))
    self_features, mem_features = take(at.share), take(at.share)
    kvs = [kept.kv, *take(at.share - 1)]
    mem_kvs = [kept.mem_kv, *take(at.share - 1)]
    cot, cot_other, held_other, gathered = results
    return types.SimpleNamespace(
        **kept._asdict(),
        self_features=self_features,
        mem_features=mem_features,
        kvs=kvs,
        mem_kvs=mem_kvs,
        cot=cot,
        cot_other=cot_other,
        held_other=held_other,
        gathered=gathered,
    )


def gelu_parts(v):
    slope = math.sqrt(2 / math.pi)
    square = v * v
    t = jnp.tanh(slope * v * (1.0 + 0.044715 * square))
    half = 0.5 * (1.0 + t)
    derivative = half + 0.5 * v * (1.0 - t * t) * slope * (1.0 + 3 * 0.044715 * square)
    return v * half, derivative


def ffn_parts(rows):
    first = (rows // 2 + 15) // 16 * 16
    return (0, first), (first, rows - first)


def ffn_kernel(at, span, later, *refs):
    held_refs, cot_refs = refs[0:2], refs[2:4]
    gathered = refs[4]
    sums, earlier, refs = (refs[5:9], refs[9], refs[10:]) if later else (None, None, refs[5:])
    if later:
        beside = FirstStep(at, earlier, refs[3], refs[-FirstStep.BUFFERS :])
        landings, *swap_sems = refs[-FirstStep.BUFFERS - 3 : -FirstStep.BUFFERS]
        refs = (*refs[:2], None, None, refs[2], *refs[4 : -FirstStep.BUFFERS - 3])
    out_refs = refs[0:4]
    grad_ref = refs[4]
    weights, acts, held, cot, out_stage, back_stage = refs[5:11]
    in_sems, w_sems, out_sems = refs[11:]
    d = lax.axis_index("dp")
    z = lax.axis_index("tp") // 2
    tokens = held_refs[0].shape[0]
    first_row, rows = span
    width = gathered.shape[4]

    def columns(s):
        return pl.ds(pl.multiple_of(xor_static(d, s, at.dp) * width, width), width)

    loads = [], []
    for which, (sources, target) in enumerate(((held_refs, held), (cot_refs, cot))):
        for half in range(2):
            for s in range(at.dp):
                loads[half].append(
                    pltpu.make_async_copy(
                        sources[half].at[:, columns(s)],
                        target.at[pl.ds(half * tokens, tokens), pl.ds(s * width, width)],
                        in_sems.at[(which * 2 + half) * at.dp + s],
                    )
                )
    stages = (out_stage, back_stage)
    if later:
        for which, target in enumerate(stages):
            for half in range(2):
                for s in range(at.dp):
                    loads[half].append(
                        pltpu.make_async_copy(
                            sums[which * 2 + half].at[:, columns(s)],
                            target.at[pl.ds(half * tokens, tokens), pl.ds(s * width, width)],
                            out_sems.at[(which * 2 + half) * at.dp + s],
                        )
                    )
    for k in range(at.z_count):
        for s in range(at.dp):
            number = k * at.dp + s
            loads[0].append(
                pltpu.make_async_copy(
                    gathered.at[k, s, :, pl.ds(first_row, rows), :],
                    weights.at[
                        :,
                        pl.ds(pl.multiple_of((z + at.z_count - k) % at.z_count * rows, rows), rows),
                        pl.ds(s * width, width),
                    ],
                    w_sems.at[number],
                )
            )
    for copy in loads[0] + loads[1]:
        copy.start()
    if later:
        greet(at)
        beside.start()

    tile = 256

    def keep(stage, here, value):
        if later:
            value = value + stage[here, :].astype(f32)
        stage[here, :] = value.astype(bf16)

    def step(index, carry):
        here = pl.ds(pl.multiple_of(index * tile, tile), tile)
        held_tile, cot_tile = held[here, :], cot[here, :]
        gate = nt(held_tile, weights[0])
        up = nt(held_tile, weights[1])
        grad_hidden = nt(cot_tile, weights[2])
        active, slope = gelu_parts(gate)
        hidden = (active * up).astype(bf16)
        acts[2, here, :] = hidden
        keep(out_stage, here, nn(hidden, weights[2]))
        grad_gate = (grad_hidden * up * slope).astype(bf16)
        grad_up = (grad_hidden * active).astype(bf16)
        acts[0, here, :] = grad_gate
        acts[1, here, :] = grad_up
        keep(back_stage, here, nn(grad_gate, weights[0]) + nn(grad_up, weights[1]))
        return carry

    tiles = tokens // tile
    for half in range(2):
        for copy in loads[half]:
            copy.wait()
        lax.fori_loop(half * tiles, (half + 1) * tiles, step, 0)

    swaps = []
    if later:
        for which, stage in enumerate(stages):
            swaps.append(
                remote(
                    stage.at[pl.ds(tokens, tokens), :],
                    landings.at[which],
                    swap_sems,
                    which,
                    "tp",
                    other_core(),
                )
            )
            swaps[which].start()

    stores = []
    for which, stage in enumerate(stages):
        for half in range(1 if later else 2):
            for s in range(at.dp):
                stores.append(
                    pltpu.make_async_copy(
                        stage.at[pl.ds(half * tokens, tokens), pl.ds(s * width, width)],
                        out_refs[which if later else which * 2 + half].at[:, columns(s)],
                        out_sems.at[(which * 2 + half) * at.dp + s],
                    )
                )
    if not later:
        for copy in stores:
            copy.start()

    hidden_rows = rows * at.z_count
    for start in range(0, hidden_rows, BLOCK):
        size = min(BLOCK, hidden_rows - start)
        for m in range(3):
            right = cot if m == 2 else held
            grad = tn(acts[m, :, start : start + size], right[...]).astype(bf16)
            first = start
            while first < start + size:
                chunk, inside = divmod(first, rows)
                last = min(start + size, (chunk + 1) * rows)
                for s in range(at.dp):
                    grad_ref[
                        xor_static(d, s, at.dp), chunk, m, inside : inside + last - first, :
                    ] = grad[first - start : last - start, s * width : (s + 1) * width]
                first = last
    if later:
        for which, stage in enumerate(stages):
            swaps[which].wait()
            for first in range(0, tokens, tile):
                here = pl.ds(first, tile)
                stage[here, :] = (
                    stage[here, :].astype(f32) + landings[which, here, :].astype(f32)
                ).astype(bf16)
        for copy in stores:
            copy.start()
    for copy in stores:
        copy.wait()
    if later:
        beside.end()


def ffn(at, span, held_own, held_other, cot_own, cot_other, gathered, sums=(), earlier=None):
    tokens, features = held_own.shape
    rows, width = span[1], gathered.shape[4]
    hidden = rows * at.z_count
    grad_shape = jax.ShapeDtypeStruct((at.dp, at.z_count, 3, rows, width), bf16)
    token_shape = jax.ShapeDtypeStruct((tokens, features), bf16)
    extra, extra_shape, extra_scratch, extra_params, results = [], [], [], {}, 4
    if sums:
        results = 2
        half_shape = half_shape_of(at, earlier)
        extra = [*sums, earlier]
        extra_shape = [jax.ShapeDtypeStruct(half_shape, bf16)]
        extra_scratch = [
            pltpu.VMEM((2, tokens, features), bf16),
            pltpu.SemaphoreType.DMA((2,)),
            pltpu.SemaphoreType.DMA((2,)),
            *first_step_scratch(at, half_shape),
        ]
        extra_params = dict(collective_id=5, has_side_effects=True)
    return pl.pallas_call(
        functools.partial(ffn_kernel, at, span, bool(sums)),
        out_shape=[token_shape] * results + [grad_shape] + extra_shape,
        in_specs=[any_space()] * (5 + len(extra)),
        out_specs=[any_space()] * results + [whole_vmem()] * (1 + len(extra_shape)),
        scratch_shapes=[
            pltpu.VMEM((3, hidden, features), bf16),
            pltpu.VMEM((3, 2 * tokens, hidden), bf16),
            pltpu.VMEM((2 * tokens, features), bf16),
            pltpu.VMEM((2 * tokens, features), bf16),
            pltpu.VMEM((2 * tokens, features), bf16),
            pltpu.VMEM((2 * tokens, features), bf16),
            pltpu.SemaphoreType.DMA((4 * at.dp,)),
            pltpu.SemaphoreType.DMA((at.z_count * at.dp,)),
            pltpu.SemaphoreType.DMA((4 * at.dp,)),
            *extra_scratch,
        ],
        compiler_params=params(58, **extra_params),
        cost_estimate=pl.CostEstimate(
            flops=18 * 2 * tokens * features * hidden,
            bytes_accessed=40 * MIB,
            transcendentals=2 * tokens * hidden,
        ),
        name="ffn",
    )(held_own, held_other, cot_own, cot_other, gathered, *extra)


def weight_grad_kernel(at, widths, *refs):
    n = len(widths)
    lefts, rights, outs = refs[:n], refs[n : 2 * n], refs[2 * n :]
    d = lax.axis_index("dp")
    core = lax.axis_index("tp") % 2
    rows = lefts[0].shape[1] // at.dp
    quarter = sum(widths) // 4
    offset = 0
    for left, right, total in zip(lefts, rights, widths):
        width = total // 2
        block = jnp.concatenate(
            [
                right[:, pl.ds(pl.multiple_of(half * width, width), width)]
                for half in (core, 1 - core)
            ],
            axis=1,
        )
        for s in range(at.dp):
            chosen = pl.ds(pl.multiple_of(xor_static(d, s, at.dp) * rows, rows), rows)
            grad = tn(left[:, chosen], block).astype(bf16)
            done = 0
            while done < width:
                part, inside = divmod(offset + done, quarter)
                taken = min(width - done, quarter - inside)
                place = half_order(at.dp, part == 0)[0].index(s)
                for sent in range(2):
                    first = sent * width + done
                    outs[part * 2 + sent][place, :, inside : inside + taken] = grad[
                        :, first : first + taken
                    ]
                done += taken
        offset += width


def weight_products(at, pairs):
    lefts = [left for left, _ in pairs]
    rights = [right for _, right in pairs]
    widths = [right.shape[1] for right in rights]
    features = lefts[0].shape[1]
    quarter = sum(widths) // 4
    shape = jax.ShapeDtypeStruct((at.dp, features // at.dp, quarter), bf16)
    return pl.pallas_call(
        functools.partial(weight_grad_kernel, at, widths),
        out_shape=[shape] * 4,
        in_specs=[whole_vmem()] * (2 * len(pairs)),
        out_specs=[whole_vmem()] * 4,
        compiler_params=params(48),
        cost_estimate=pl.CostEstimate(
            flops=2 * lefts[0].shape[0] * features * sum(widths),
            bytes_accessed=16 * MIB,
            transcendentals=0,
        ),
        name="weight_grads",
    )(*lefts, *rights)


def z_slots(at, bit):
    sent = [r for r in range(at.z_count) if r >> bit & 1 and r % (1 << bit) == 0]
    base = at.z_count - (at.z_count >> bit)
    return [(r, base + number) for number, r in enumerate(sent)]


class RowReturn:
    BUFFERS = 4

    def __init__(self, at, source, target, buffers):
        self.at, self.source, self.target = at, source, target
        self.landing, *sems, self.own_sem = buffers
        self.sems = tuple(sems)
        self.row, self.part = at.row(), at.part()

    @staticmethod
    def scratch(at, array):
        return [
            pltpu.VMEM(array.shape, array.dtype),
            pltpu.SemaphoreType.DMA((at.rows - 1,)),
            pltpu.SemaphoreType.DMA((at.rows - 1,)),
            pltpu.SemaphoreType.DMA((1,)),
        ]

    def copies(self):
        own = pltpu.make_async_copy(
            self.source.at[self.row], self.landing.at[self.row], self.own_sem.at[0]
        )
        made = [own]
        for k in range(1, self.at.rows):
            there = xor_static(self.row, k, self.at.rows)
            made.append(
                remote(
                    self.source.at[there],
                    self.landing.at[self.row],
                    self.sems,
                    k - 1,
                    "tp",
                    there * self.at.share + self.part,
                )
            )
        return made

    def start(self):
        for copy in self.copies():
            copy.start()

    def end(self):
        for copy in self.copies():
            copy.wait()
        for r in range(self.at.rows):
            self.target[r] = self.landing[r]


class Reduction:
    def __init__(self, at, first_low, buffers):
        self.at = at
        self.first, self.halves, self.z_in, self.done, self.last_in, *self.sems = buffers
        self.base = self.first
        _, self.bits = half_order(at.dp, first_low)
        self.z = lax.axis_index("tp") // 2
        self.core = lax.axis_index("tp") % 2
        self.rows = self.first.shape[1] // at.z_count
        self.copies = {}

    @staticmethod
    def scratch(at, rows, columns):
        n = at.dp // 2
        messages = 1 + bits_of(at.dp) + at.z_count
        return [
            pltpu.VMEM((at.dp, rows, columns), bf16),
            pltpu.VMEM((max(2 * n - 1, 1), rows, columns), bf16),
            pltpu.VMEM((at.z_count - 1, rows // at.z_count, columns), bf16),
            pltpu.VMEM((rows // at.z_count, columns), f32),
            pltpu.VMEM((rows // at.z_count // 2, columns), f32),
            pltpu.SemaphoreType.DMA((messages,)),
            pltpu.SemaphoreType.DMA((messages,)),
        ]

    BUFFERS = 7

    def start(self, key, copy):
        self.copies[key] = copy
        copy.start()

    def start_core(self, source):
        self.start("core", remote(source, self.first, self.sems, 0, "tp", other_core()))

    def end_core(self, keep):
        self.copies["core"].wait()
        for s in range(self.at.dp):
            self.first[s] = self.first[s] + keep[s]

    def half_at(self, place):
        n = self.at.dp >> (place + 1)
        return n, self.at.dp - 2 * n

    def start_half(self, place):
        n, offset = self.half_at(place)
        d = lax.axis_index("dp")
        self.start(
            ("half", place),
            remote(
                self.base.at[pl.ds(n, n)],
                self.halves.at[pl.ds(offset, n)],
                self.sems,
                1 + place,
                "dp",
                xor_static(d, 1 << self.bits[place], self.at.dp),
            ),
        )

    def end_half(self, place):
        self.copies["half", place].wait()
        n, offset = self.half_at(place)
        for s in range(n):
            self.first[s] = self.first[s] + self.halves[offset + s]
        self.base = self.first

    def z_rows(self, r):
        z = xor_static(self.z, r, self.at.z_count)
        return pl.ds(pl.multiple_of(z * self.rows, self.rows), self.rows)

    def start_z(self, bit):
        base = 1 + len(self.bits)
        partner = tp_at(self.at, xor_static(self.z, 1 << bit, self.at.z_count))
        for r, slot in z_slots(self.at, bit):
            self.start(
                ("z", slot),
                remote(
                    self.first.at[0, self.z_rows(r), :],
                    self.z_in.at[slot],
                    self.sems,
                    base + slot,
                    "tp",
                    partner,
                ),
            )

    def end_z(self, bit):
        for r, slot in z_slots(self.at, bit):
            self.copies["z", slot].wait()
            rows = self.z_rows(r ^ 1 << bit)
            total = self.first[0, rows, :].astype(f32) + self.z_in[slot].astype(f32)
            if 2 << bit == self.at.z_count:
                self.done[...] = total
            else:
                self.first[0, rows, :] = total.astype(bf16)

    def part(self, core):
        rows = self.rows // 2
        return pl.ds(pl.multiple_of(core * rows, rows), rows)

    def start_last(self):
        number = len(self.bits) + self.at.z_count
        self.start(
            "last",
            remote(
                self.done.at[self.part(1 - self.core), :],
                self.last_in,
                self.sems,
                number,
                "tp",
                other_core(),
            ),
        )

    def end_last(self, out, columns):
        out[0, :, columns] = self.done[self.part(self.core), :]
        self.copies["last"].wait()
        out[1, :, columns] = self.last_in[...]


def relative_sums(at, kinds, diagonals, dfar):
    lane = lax.broadcasted_iota(jnp.int32, (1, BLOCK), 1)
    onehots = []
    for kind in kinds:
        offset = lax.broadcasted_iota(jnp.int32, (2 * BLOCK, BLOCK), 0) - (BLOCK - 1)
        distance = BLOCK * kind_distance(at, kind) + offset
        bucket = bucket_of(jnp.maximum(distance, 0))
        column = lax.broadcasted_iota(jnp.int32, (2 * BLOCK, BLOCK), 1)
        onehots.append(jnp.where(bucket == column, 1.0, 0.0).astype(bf16))
    results = []
    for group in range(GROUPS):
        sums = jnp.zeros((2, BLOCK), f32)
        for number, onehot in enumerate(onehots):
            rest = diagonals[group, 2 * number : 2 * number + 2, :]
            for _ in range(3):
                part = rest.astype(bf16)
                sums = sums + nn(part, onehot)
                rest = rest - part.astype(f32)
        for j in range(2):
            far = jnp.sum(dfar[group, :, j * BLOCK : (j + 1) * BLOCK], axis=0, keepdims=True)
            far = jnp.sum(far, axis=1, keepdims=True)
            results.append(sums[j : j + 1] + jnp.where(lane == BUCKETS - 1, far, 0.0))
    return results


class CoreStep:
    BUFFERS = 4

    def __init__(self, at, first_low, buffers):
        self.at = at
        self.first, self.landing, *self.sems = buffers
        self.bit = half_order(at.dp, first_low)[1][0]

    @staticmethod
    def scratch(at, rows, columns, halves):
        return [
            pltpu.VMEM((at.dp, rows, columns), bf16),
            pltpu.VMEM((at.dp // 2 if halves else 1, rows if halves else 16, columns), bf16),
            pltpu.SemaphoreType.DMA((2,)),
            pltpu.SemaphoreType.DMA((2,)),
        ]

    def start_core(self, source):
        self.core = remote(source, self.first, self.sems, 0, "tp", other_core())
        self.core.start()

    def end_core(self, keep):
        self.core.wait()
        for s in range(self.at.dp):
            self.first[s] = self.first[s] + keep[s]

    def start_half(self):
        n = self.at.dp // 2
        partner = xor_static(lax.axis_index("dp"), 1 << self.bit, self.at.dp)
        self.half = remote(
            self.first.at[pl.ds(n, n)], self.landing, self.sems, 1, "dp", partner
        )
        self.half.start()

    def end_half(self, out):
        self.half.wait()
        for s in range(self.at.dp // 2):
            out[s] = self.first[s] + self.landing[s]


class FfnSum:
    def __init__(self, at, source, out, take):
        self.at, self.source, self.out = at, source, out
        self.total = DpSum(at)
        (self.work,) = take(1)
        self.landings = [take(3) for _ in range(1, bits_of(at.dp))]
        self.z_in, *self.z_sems, self.load_sems = take(4)
        self.z_sems = tuple(self.z_sems)
        self.z = lax.axis_index("tp") // 2
        self.copies = {}

    @staticmethod
    def scratch(at, half_shape):
        inner = half_shape[2:]
        scratch = [pltpu.VMEM((2, at.dp // 4, *inner), bf16)]
        for step in range(1, bits_of(at.dp)):
            count = at.dp >> (step + 1)
            scratch += [
                pltpu.VMEM((2, count, *inner), bf16),
                pltpu.SemaphoreType.DMA((2 * count,)),
                pltpu.SemaphoreType.DMA((2 * count,)),
            ]
        return scratch + [
            pltpu.VMEM((at.z_count - 1, *inner[1:]), bf16),
            pltpu.SemaphoreType.DMA((at.z_count - 1,)),
            pltpu.SemaphoreType.DMA((at.z_count - 1,)),
            pltpu.SemaphoreType.DMA((2 * (at.dp // 4),)),
        ]

    def start(self):
        total = self.total
        self.loads = []
        for half in range(2):
            for slot, s in enumerate(total.held(half, 2)):
                place = total.held(half, 1).index(s)
                self.loads.append(
                    pltpu.make_async_copy(
                        self.source.at[half, place],
                        self.work.at[half, slot],
                        self.load_sems.at[half * total.count(2) + slot],
                    )
                )
        entry = lambda half, s: self.source.at[half, total.held(half, 1).index(s)]
        self.send(1, entry)
        for copy in self.loads:
            copy.start()

    def send(self, step, entry):
        landing, *sems = self.landings[step - 1]
        self.dp_copies = self.total.copies(step, entry, landing, tuple(sems))
        for copy in self.dp_copies:
            copy.start()

    def to_z(self):
        total = self.total
        for copy in self.loads:
            copy.wait()
        for step in range(1, bits_of(self.at.dp)):
            for copy in self.dp_copies:
                copy.wait()
            landing = self.landings[step - 1][0]
            for half in range(2):
                for slot, s in enumerate(total.held(half, step + 1)):
                    place = total.held(half, 2).index(s)
                    for chunk in range(self.at.z_count // 2):
                        for m in range(3):
                            self.work[half, place, chunk, m] = (
                                self.work[half, place, chunk, m] + landing[half, slot, chunk, m]
                            )
            if step + 1 < bits_of(self.at.dp):
                self.send(
                    step + 1,
                    lambda half, s: self.work.at[half, total.held(half, 2).index(s)],
                )
        self.start_z(0)

    def chunk(self, r):
        z = xor_static(self.z, r, self.at.z_count)
        half_z = self.at.z_count // 2
        return self.work.at[z // half_z, 0, z % half_z]

    def start_z(self, bit):
        partner = tp_at(self.at, xor_static(self.z, 1 << bit, self.at.z_count))
        for r, slot in z_slots(self.at, bit):
            self.copies[slot] = remote(
                self.chunk(r), self.z_in.at[slot], self.z_sems, slot, "tp", partner
            )
            self.copies[slot].start()

    def end_z(self, bit):
        for r, slot in z_slots(self.at, bit):
            self.copies[slot].wait()
            kept = self.chunk(r ^ 1 << bit)
            for m in range(3):
                total = kept[m].astype(f32) + self.z_in[slot, m].astype(f32)
                if 2 << bit == self.at.z_count:
                    self.out[m] = total
                else:
                    kept[m] = total.astype(bf16)


def self_backward_kernel(at, *refs):
    refs = list(refs)
    take = lambda n: [refs.pop(0) for _ in range(n)]
    held, queries, seg_ref, logsum, grad_context, tiles, last_parts = take(7)
    kv_refs, feat_refs = take(at.share), take(at.share)
    gain, wq, wk, wv = take(4)
    late_sources = take(4)
    send_low, send_high = take(2)
    *ffn_ins, memory_in = take(3)
    flushed = take(5)
    gain_out, relative_out, *ffn_outs, memory_out = take(5)
    keep_low, keep_high, x_ref, grad_ref = late_targets = take(4)
    middle_outs, last_outs, (rows_out,) = buffers = take(2), take(2), take(1)
    late_sems, flush_sems = take(2)
    late_loads = [
        pltpu.make_async_copy(source, target, late_sems.at[number])
        for number, (source, target) in enumerate(zip(late_sources, late_targets))
    ]
    flushes = [
        pltpu.make_async_copy(source, target, flush_sems.at[number])
        for number, (source, target) in enumerate(zip(sum(buffers, []), flushed))
    ]
    middle = [CoreStep(at, half == 0, take(CoreStep.BUFFERS)) for half in range(2)]
    last = [CoreStep(at, half == 0, take(CoreStep.BUFFERS)) for half in range(2)]
    ffn_sums = [FfnSum(at, *pair, take) for pair in zip(ffn_ins, ffn_outs)]
    memory_return = RowReturn(at, memory_in, memory_out, take(RowReturn.BUFFERS))
    z_bits = range(bits_of(at.z_count))
    product_send, kv_in, dq, diagonals, dfar = take(5)
    own_kv, *other_kv = take(at.share)
    weight_sems, = take(1)
    kv_sems = take(2)
    d = lax.axis_index("dp")
    core = lax.axis_index("tp") % 2
    row, part = at.row(), at.part()
    features = held.shape[1]
    rows = features // at.dp
    kinds = near_kinds(at.share)
    keys = Keys(at.share, at.rows, True)
    lanes_at = lambda start, width: pl.ds(pl.multiple_of(start, BLOCK), width)

    def one_pair(scratch, pair, carry):
        four = lanes_at(pair * 2 * BLOCK, 2 * BLOCK)
        two = lanes_at(pair * BLOCK, BLOCK)
        values = lanes_at(GROUPS * HEAD_DIM + pair * BLOCK, BLOCK)
        both = pl.ds(pair * 2, 2)
        backward_body(
            keys,
            kinds,
            pair,
            queries.at[:, four],
            seg_ref,
            [ref.at[:, two] for ref in kv_refs],
            [ref.at[:, values] for ref in kv_refs],
            feat_refs,
            tiles.at[both],
            last_parts,
            logsum.at[both],
            grad_context.at[:, four],
            dq.at[:, four],
            [ref.at[:, :, two] for ref in (own_kv, *other_kv)],
            diagonals.at[both],
            dfar.at[both],
            scratch,
        )
        return carry

    def products(number, right, offset):
        width = right.shape[1] // 2
        order, _ = half_order(at.dp, number == 0)
        block = jnp.concatenate(
            [
                right[:, pl.ds(pl.multiple_of(half * width, width), width)]
                for half in (core, 1 - core)
            ],
            axis=1,
        )
        for place, s in enumerate(order):
            chosen = pl.ds(pl.multiple_of(xor_static(d, s, at.dp) * rows, rows), rows)
            both = tn(held[:, chosen], block).astype(bf16)
            last_outs[number][place, :, offset : offset + width] = both[:, :width]
            product_send[number, place, :, offset : offset + width] = both[:, width:]

    greet(at)
    for ffn_sum in ffn_sums:
        ffn_sum.start()
    middle[0].start_core(send_low)
    middle[1].start_core(send_high)
    memory_return.start()
    for copy in late_loads:
        copy.start()

    def attention(first, last):
        def pairs(*scratch):
            lax.fori_loop(first, last, functools.partial(one_pair, scratch), 0)

        pl.run_scoped(
            pairs,
            *backward_scratch(keys.count * BLOCK),
            pltpu.VMEM((len(kinds), BLOCK, 2 * BLOCK), f32),
        )

    attention(0, 2)
    ffn_sums[0].to_z()
    for copy in late_loads:
        copy.wait()
    for number, keep in enumerate((keep_low, keep_high)):
        middle[number].end_core(keep)
        middle[number].start_half()
    attention(2, PAIRS)
    ffn_sums[1].to_z()
    for bit in z_bits[1:]:
        ffn_sums[0].end_z(bit - 1)
        ffn_sums[0].start_z(bit)
    kv_copies = []
    for s in range(1, at.share):
        kv_copies.append(
            remote(
                other_kv[s - 1],
                kv_in.at[s - 1],
                kv_sems,
                s - 1,
                "tp",
                row * at.share + (part + s) % at.share,
            )
        )
    for copy in kv_copies:
        copy.start()
    products(0, dq, 0)
    last[0].start_core(product_send.at[0])
    for copy in kv_copies:
        copy.wait()
    for which in range(2):
        total = own_kv[which].astype(f32)
        for s in range(1, at.share):
            total = total + kv_in[s - 1, which].astype(f32)
        own_kv[which] = total.astype(bf16)
    for which in range(2):
        products(1, own_kv.at[which], which * (own_kv.shape[2] // 2))
    last[1].start_core(product_send.at[1])
    for bit in z_bits[1:]:
        ffn_sums[1].end_z(bit - 1)
        ffn_sums[1].start_z(bit)

    seq = rows_out.shape[1]

    def input_gradient(*weights):
        loads = [
            pltpu.make_async_copy(source, target, weight_sems.at[number])
            for number, (source, target) in enumerate(zip((wq, wk, wv), weights))
        ]
        for copy in loads:
            copy.start()
        for copy in loads:
            copy.wait()
        gain_sum = jnp.zeros((1, features), f32)
        gain_row = gain[...]
        for i in range(at.rows):
            here = pl.ds(i * seq, seq)
            dy = nt(dq[here, :], weights[0][...])
            dy = dy + nt(own_kv[0, here, :], weights[1][...])
            dy = dy + nt(own_kv[1, here, :], weights[2][...])
            grad, gain_part = norm_back(x_ref[here, :].astype(f32), gain_row, dy)
            gain_sum = gain_sum + gain_part
            rows_out[i] = (grad_ref[here, :] + grad).astype(bf16)
        gain_out[...] = gain_sum

    pl.run_scoped(input_gradient, *[pltpu.VMEM(w.shape, bf16) for w in (wq, wk, wv)])
    flushes[4].start()
    relative_out[...] = jnp.zeros(relative_out.shape, f32)
    for head, sums in enumerate(relative_sums(at, kinds, diagonals, dfar)):
        lane = head // 4 * BLOCK
        relative_out[head % 4 : head % 4 + 1, lane : lane + BLOCK] = sums
    for number in range(2):
        last[number].end_core(last_outs[number])
        for s in range(at.dp):
            last_outs[number][s] = last[number].first[s]
        flushes[2 + number].start()
    for number in range(2):
        middle[number].end_half(middle_outs[number])
        flushes[number].start()
    for ffn_sum in ffn_sums:
        ffn_sum.end_z(z_bits[-1])
    memory_return.end()
    for copy in flushes:
        copy.wait()


def self_backward(
    at,
    held,
    queries,
    kvs,
    features_of,
    seg_row,
    logsum,
    grad_context,
    tiles,
    last_parts,
    x_low,
    grad_one,
    gain,
    weights,
    middle,
    ffn_parts_now,
    memory_grad,
):
    keep_low, send_low, keep_high, send_high = middle
    tokens, features = held.shape
    _, rows, middle_columns = keep_low.shape
    key_width = kvs[0].shape[1] // 2
    last_columns = features // 2
    kinds = len(near_kinds(at.share))
    of = jax.ShapeDtypeStruct
    flushed = [of((at.dp // 2, rows, middle_columns), bf16)] * 2
    flushed += [of((at.dp, rows, last_columns), bf16)] * 2
    flushed += [of((at.rows, tokens // at.rows, features), bf16)]
    late = [keep_low, keep_high, x_low, grad_one]
    scratch = [pltpu.VMEM(array.shape, array.dtype) for array in late + flushed]
    scratch += [pltpu.SemaphoreType.DMA((len(late),)), pltpu.SemaphoreType.DMA((len(flushed),))]
    for columns, halves in ((middle_columns, True), (last_columns, False)):
        scratch += CoreStep.scratch(at, rows, columns, halves) * 2
    for part in ffn_parts_now:
        scratch += FfnSum.scratch(at, part.shape)
    scratch += RowReturn.scratch(at, memory_grad)
    scratch += [
        pltpu.VMEM((2, at.dp, rows, last_columns), bf16),
        pltpu.VMEM((at.share - 1, 2, tokens, key_width), bf16),
        pltpu.VMEM((tokens, features), bf16),
        pltpu.VMEM((GROUPS, 2 * kinds, 2 * BLOCK), f32),
        pltpu.VMEM((GROUPS, 8, 2 * BLOCK), f32),
        *[pltpu.VMEM((2, tokens, key_width), bf16)] * at.share,
        pltpu.SemaphoreType.DMA((3,)),
        pltpu.SemaphoreType.DMA((at.share - 1,)),
        pltpu.SemaphoreType.DMA((at.share - 1,)),
    ]
    return pl.pallas_call(
        functools.partial(self_backward_kernel, at),
        out_shape=flushed
        + [
            of((1, features), f32),
            of((4, features), f32),
            *[of(part.shape[3:], f32) for part in ffn_parts_now],
            of(memory_grad.shape, bf16),
        ],
        in_specs=[whole_vmem()] * 6
        + [whole_smem()]
        + [whole_vmem()] * (2 * at.share + 1)
        + [any_space()] * 12,
        out_specs=[any_space()] * len(flushed) + [whole_vmem()] * 5,
        scratch_shapes=scratch,
        compiler_params=params(62, collective_id=3, has_side_effects=True),
        cost_estimate=pl.CostEstimate(
            flops=20 * tokens * features * features,
            bytes_accessed=100 * MIB,
            transcendentals=0,
        ),
        name="self_backward",
    )(
        held,
        queries,
        seg_row,
        logsum,
        grad_context,
        tiles,
        last_parts,
        *kvs,
        *features_of,
        gain,
        *weights,
        *late,
        send_low,
        send_high,
        *ffn_parts_now,
        memory_grad,
    )


def tail_kernel(at, *refs):
    refs = list(refs)
    take = lambda n: [refs.pop(0) for _ in range(n)]
    middle_in, last_in = take(2), take(2)
    grad_rows, small_in = take(2)
    input_out, small_out, middle_out, last_out = take(4)
    middle = [
        Reduction(at, True, take(Reduction.BUFFERS)),
        Reduction(at, False, take(Reduction.BUFFERS)),
    ]
    last = [
        Reduction(at, True, take(Reduction.BUFFERS)),
        Reduction(at, False, take(Reduction.BUFFERS)),
    ]
    input_return = RowReturn(at, grad_rows, input_out, take(RowReturn.BUFFERS))
    small, small_ins = take(2)
    small_sems = take(2)
    (load_sems,) = take(1)
    d = lax.axis_index("dp")
    t = lax.axis_index("tp")
    z = t // 2
    bits = list(range(bits_of(at.dp)))
    z_bits = range(bits_of(at.z_count))

    loads = []
    for number, (source, reduction) in enumerate(zip(middle_in + last_in, middle + last)):
        reduction.base = source
        n = at.dp >> (2 if number < 2 else 1)
        loads.append(
            pltpu.make_async_copy(
                source.at[pl.ds(0, n)], reduction.first.at[pl.ds(0, n)], load_sems.at[number]
            )
        )
        loads[-1].start()
    greet(at)
    for reduction in middle:
        reduction.start_half(1)
    for reduction in last:
        reduction.start_half(0)
    input_return.start()
    for copy in loads:
        copy.wait()

    small[0:8, :] = small_in[...]
    steps = [("tp", other_core())]
    steps += [("dp", xor_static(d, 1 << bit, at.dp)) for bit in bits]
    small_copies = []

    def start_small(number):
        axis, index = steps[number]
        copy = remote(
            small.at[pl.ds(8 * number, 8)], small_ins.at[number], small_sems, number, axis, index
        )
        small_copies.append(copy)
        copy.start()

    def end_small(number):
        small_copies[number].wait()
        small[8 * number + 8 : 8 * number + 16, :] = (
            small[8 * number : 8 * number + 8, :] + small_ins[number]
        )

    start_small(0)
    end_small(0)
    start_small(1)
    for place in bits[1:]:
        for reduction in middle:
            reduction.end_half(place)
            if place + 1 < len(bits):
                reduction.start_half(place + 1)
            else:
                reduction.start_z(0)
        for reduction in last:
            reduction.end_half(place - 1)
            reduction.start_half(place)
        end_small(place)
        start_small(place + 1)
    for reduction in last:
        reduction.end_half(len(bits) - 1)
        reduction.start_z(0)
    final = len(steps)
    end_small(final - 1)
    z_copies = []
    for k in range(1, at.z_count):
        z_copies.append(
            remote(
                small.at[pl.ds(8 * final, 8)],
                small_ins.at[final + k - 1],
                small_sems,
                final + k - 1,
                "tp",
                tp_at(at, (z + k) % at.z_count),
            )
        )
    for copy in z_copies:
        copy.start()
    for bit in z_bits[1:]:
        for reduction in middle + last:
            reduction.end_z(bit - 1)
            reduction.start_z(bit)
    input_return.end()
    total = small[8 * final : 8 * final + 8, :]
    for k, copy in enumerate(z_copies):
        copy.wait()
        total = total + small_ins[final + k]
    small_out[...] = total
    for reduction in middle + last:
        reduction.end_z(z_bits[-1])
        reduction.start_last()
    for reductions, out in ((middle, middle_out), (last, last_out)):
        columns = out.shape[2] // 2
        for number, reduction in enumerate(reductions):
            reduction.end_last(out, slice(number * columns, (number + 1) * columns))


def tail(at, grad_rows, middle, last, small):
    _, rows, middle_columns = middle[0].shape
    last_columns = last[0].shape[2]
    share_rows = rows // at.z_count // 2
    steps = 1 + bits_of(at.dp)
    out_shape = [
        jax.ShapeDtypeStruct(grad_rows.shape, bf16),
        jax.ShapeDtypeStruct(small.shape, f32),
        jax.ShapeDtypeStruct((2, share_rows, 2 * middle_columns), f32),
        jax.ShapeDtypeStruct((2, share_rows, 2 * last_columns), f32),
    ]
    scratch = []
    for columns in (middle_columns, middle_columns, last_columns, last_columns):
        scratch += Reduction.scratch(at, rows, columns)
    scratch += RowReturn.scratch(at, grad_rows)
    dma = lambda n: [pltpu.SemaphoreType.DMA((n,))] * 2
    scratch += [
        pltpu.VMEM((8 * (steps + 1), small.shape[1]), f32),
        pltpu.VMEM((steps + at.z_count - 1, *small.shape), f32),
        *dma(steps + at.z_count - 1),
        pltpu.SemaphoreType.DMA((4,)),
    ]
    return pl.pallas_call(
        functools.partial(tail_kernel, at),
        out_shape=out_shape,
        in_specs=[any_space()] * 5 + [whole_vmem()],
        out_specs=[whole_vmem()] * 4,
        scratch_shapes=scratch,
        compiler_params=params(62, collective_id=1, has_side_effects=True),
        cost_estimate=pl.CostEstimate(
            flops=MIB, bytes_accessed=200 * MIB, transcendentals=0
        ),
        name="tail",
    )(*middle, *last, grad_rows, small)


def finish_kernel(widths, *refs):
    refs = list(refs)
    take = lambda n: [refs.pop(0) for _ in range(n)]
    input_in, memory_in = take(2)
    pairs = take(len(widths))
    parts = take(2)
    input_out, memory_out = take(2)
    outs = [take(len(group)) for group in widths]
    gate_out, up_out, down_out = take(3)
    core = lax.axis_index("tp") % 2
    for source, target in ((input_in, input_out), (memory_in, memory_out)):
        for r in range(source.shape[0]):
            target[r] = source[r].astype(f32)
    for pair, group, targets in zip(pairs, widths, outs):
        offset = 0
        for width, target in zip(group, targets):
            half = width // 2
            for place in range(2):
                columns = pl.ds(pl.multiple_of((core + place) % 2 * half, half), half)
                target[:, columns] = pair[place, :, offset : offset + half]
            offset += half
    first = parts[0].shape[1]
    for m, target in enumerate((gate_out, up_out, down_out)):
        target[:first, :] = parts[0][m]
        target[first:, :] = parts[1][m]


def finish(input_rows, memory_rows, pairs, widths, parts):
    of = jax.ShapeDtypeStruct
    rows, columns = parts[0].shape[1] + parts[1].shape[1], parts[0].shape[2]
    out_shape = [of(input_rows.shape, f32), of(memory_rows.shape, f32)]
    for pair, group in zip(pairs, widths):
        out_shape += [of((pair.shape[1], width), f32) for width in group]
    out_shape += [of((rows, columns), f32)] * 3
    return pl.pallas_call(
        functools.partial(finish_kernel, widths),
        out_shape=out_shape,
        in_specs=[whole_vmem()] * (4 + len(pairs)),
        out_specs=[whole_vmem()] * len(out_shape),
        compiler_params=params(62),
        name="finish",
    )(input_rows, memory_rows, *pairs, *parts)


def on_device(
    inputs,
    memory,
    segments,
    memory_segments,
    gain_self,
    gain_cross,
    gain_ffn,
    relative_bias,
    self_query,
    self_key,
    self_value,
    self_out,
    cross_query,
    cross_key,
    cross_value,
    cross_out,
    ffn_gate,
    ffn_up,
    ffn_down,
    cotangent,
):
    rows, seq, features = inputs.shape
    mem_seq = memory.shape[1]
    at = Places(rows)
    tokens = rows * seq
    mem_tokens = rows * mem_seq
    key_width = GROUPS * HEAD_DIM
    width = features // at.dp
    d = lax.axis_index("dp")

    own_columns = lambda w: lax.dynamic_slice_in_dim(w, d * width, width, 1)
    own_rows = lambda w: lax.dynamic_slice_in_dim(w, d * width, width, 0).T
    own_piece = [own_rows(ffn_gate), own_rows(ffn_up), own_columns(ffn_down)]
    segs = jnp.zeros((rows, 8, BLOCK), jnp.int32)
    segs = segs.at[:, 0, :].set(segments).at[:, 1, :mem_seq].set(memory_segments)

    table = relative_bias.reshape(-1)
    done = forward(
        at,
        inputs,
        memory,
        cotangent,
        segs,
        own_piece,
        [
            self_query,
            self_key,
            self_value,
            self_out,
            cross_query,
            cross_key,
            cross_value,
            cross_out,
        ],
        [gain.reshape(1, -1) for gain in (gain_self, gain_cross, gain_ffn)],
        table,
    )
    x_low, held_self, queries, kvs = done.x, done.held_self, done.queries, done.kvs
    self_context, self_log, stream_one = done.self_context, done.self_log, done.stream_one
    held_cross, cross_queries, mem = done.held_cross, done.cross_queries, done.mem
    mem_kvs, cross_context, cross_log = done.mem_kvs, done.cross_context, done.cross_log
    stream_two, held_ffn, cot = done.stream_two, done.held_ffn, done.cot
    self_features, mem_features = done.self_features, done.mem_features
    seg_row, tiles = done.seg_row, done.tiles

    ffn_operands = (held_ffn, done.held_other, cot, done.cot_other, done.gathered)
    first_span, second_span = ffn_parts(done.gathered.shape[3])
    *ffn_sums, ffn_grads_first = ffn(at, first_span, *ffn_operands)
    ffn_out, ffn_back, ffn_grads_second, ffn_first = ffn(
        at, second_span, *ffn_operands, ffn_sums, ffn_grads_first
    )
    grad_stream, gain_ffn_part = norm_back(stream_two, gain_ffn, ffn_back.astype(f32))
    grad_two = cot.astype(f32) + grad_stream
    output = (stream_two + ffn_out.astype(f32)).astype(bf16)
    output = output.reshape(rows, seq, features)

    cross_branch = grad_two.astype(bf16)
    grad_cross_context = nt(cross_branch, cross_out).astype(bf16)
    grad_cross_queries, *grad_mem_kvs, ffn_second, output = cross_backward(
        at,
        cross_queries,
        mem_kvs,
        mem_features,
        seg_row,
        cross_log,
        grad_cross_context,
        ffn_grads_second,
        output,
    )

    def gathered_grads(parts):
        total = parts[0].astype(f32)
        for s in range(1, at.share):
            total = total + lax.ppermute(
                parts[s], "tp", at.part_perm(at.share - s)
            ).astype(f32)
        return total[0].astype(bf16), total[1].astype(bf16)

    grad_mem_keys, grad_mem_values = gathered_grads(grad_mem_kvs)
    grad_stream, gain_cross_part = norm_back(
        stream_one, gain_cross, nt(grad_cross_queries, cross_query)
    )
    grad_one = grad_two + grad_stream
    self_branch = grad_one.astype(bf16)
    grad_self_context = nt(self_branch, self_out).astype(bf16)
    memory_grad = (nt(grad_mem_keys, cross_key) + nt(grad_mem_values, cross_value)).astype(bf16)
    memory_grad = memory_grad.reshape(rows, mem_seq, features)
    middle_products = weight_products(
        at,
        [
            (cross_context, cross_branch),
            (held_cross, grad_cross_queries),
            (self_context, self_branch),
            (mem, grad_mem_keys),
            (mem, grad_mem_values),
        ],
    )
    grad_self_context, middle_products = lax.optimization_barrier(
        (grad_self_context, middle_products)
    )
    (
        *products,
        grad_rows,
        gain_self_part,
        relative_part,
        ffn_first,
        ffn_second,
        memory_rows,
    ) = self_backward(
        at,
        held_self,
        queries,
        kvs,
        self_features,
        seg_row,
        self_log,
        grad_self_context,
        tiles,
        table,
        x_low,
        grad_one,
        gain_self.reshape(1, -1),
        (self_query, self_key, self_value),
        middle_products,
        (ffn_first, ffn_second),
        memory_grad,
    )
    small = jnp.concatenate(
        [gain_self_part, gain_cross_part, gain_ffn_part, jnp.zeros((1, features), f32), relative_part]
    )
    input_rows, small, middle_pair, last_pair = tail(
        at, grad_rows, products[:2], products[2:], small
    )
    wide, narrow = features, key_width
    (
        input_grad,
        memory_grad,
        cross_out_grad,
        cross_query_grad,
        self_out_grad,
        cross_key_grad,
        cross_value_grad,
        self_query_grad,
        self_key_grad,
        self_value_grad,
        ffn_gate_grad,
        ffn_up_grad,
        ffn_down_grad,
    ) = finish(
        input_rows,
        memory_rows,
        (middle_pair, last_pair),
        ((wide, wide, wide, narrow, narrow), (wide, narrow, narrow)),
        (ffn_first, ffn_second),
    )
    shards = at.dp * at.tp
    shard = lax.axis_index("dp") * at.tp + lax.axis_index("tp")
    share_of = lambda vector: lax.dynamic_slice_in_dim(
        vector, shard * (vector.size // shards), vector.size // shards
    )
    relative = small[4:8].reshape(4, -1, BLOCK)[:, : HEADS // 4, :BUCKETS]
    return (
        output,
        input_grad,
        memory_grad,
        share_of(small[0]),
        share_of(small[1]),
        share_of(small[2]),
        share_of(relative.transpose(2, 1, 0).reshape(-1)),
        self_query_grad,
        self_key_grad,
        self_value_grad,
        self_out_grad,
        cross_query_grad,
        cross_key_grad,
        cross_value_grad,
        cross_out_grad,
        ffn_gate_grad.T,
        ffn_up_grad.T,
        ffn_down_grad,
    )


def solution(mesh):
    placed = (
        P("dp", "tp", None),
        P("dp", "tp", None),
        P("dp", "tp"),
        P("dp", "tp"),
        P(),
        P(),
        P(),
        P(),
        P(),
        P(),
        P(),
        P(),
        P(),
        P(),
        P(),
        P(),
        P(None, "tp"),
        P(None, "tp"),
        P("tp", None),
        P("dp", "tp", None),
    )
    return jax.shard_map(
        on_device,
        mesh=mesh,
        in_specs=placed,
        out_specs=(
            P("dp", "tp", None),
            P("dp", "tp", None),
            P("dp", "tp", None),
            P(("dp", "tp")),
            P(("dp", "tp")),
            P(("dp", "tp")),
            P(("dp", "tp")),
            P(("dp", "tp"), None),
            P(("dp", "tp"), None),
            P(("dp", "tp"), None),
            P(("dp", "tp"), None),
            P(("dp", "tp"), None),
            P(("dp", "tp"), None),
            P(("dp", "tp"), None),
            P(("dp", "tp"), None),
            P("dp", "tp"),
            P("dp", "tp"),
            P("tp", "dp"),
        ),
        check_vma=False,
    )
```
